32 devices in a mesh: seq: 16 (over z, y, core), ch: 2 (over x).
Axes of the slice: x: 2, y: 2, z: 4, core: 2. Of those that a mesh axis runs over, the one named last changes fastest.
Arguments:
- tokens: bfloat16 [16, 1280, 4096], P(None, None, 'seq'), may hold values from -6 to 6
- pad_mask: int32 [16, 4096], P(None, 'seq'), may hold values from 0 to 1, as said below
- cotangent: bfloat16 [16, 1280, 4096], P(None, 'ch', 'seq'), may hold values from -6 to 6
- ln1_gain: float32 [1280], replicated, may hold values from 0.25 to 1.75
- first_norm_bias: float32 [1280], replicated, may hold values from -3 to 3
- w_in: bfloat16 [640, 1280], P('ch'), may hold values from -0.15625 to 0.15625
- b_in: float32 [640], P('ch'), may hold values from -3 to 3
- ln2_gain: float32 [640], P('ch'), may hold values from 0.25 to 1.75
- ln2_bias: float32 [640], P('ch'), may hold values from -3 to 3
- conv_w: bfloat16 [5, 640, 640], P(None, 'ch'), may hold values from -0.109375 to 0.109375
- conv_b: float32 [640], P('ch'), may hold values from -3 to 3
- ln3_gain: float32 [640], P('ch'), may hold values from 0.25 to 1.75
- ln3_bias: float32 [640], P('ch'), may hold values from -3 to 3
- w_out: bfloat16 [640, 1280], P('ch'), may hold values from -0.25 to 0.25
- b_out: float32 [1280], P('ch'), may hold values from -3 to 3
Outputs:
- mixed: bfloat16 [16, 1280, 4096], P(None, 'ch', 'seq')
- grad_tokens: float32 [16, 1280, 4096], P(None, 'ch', 'seq')
- grad_ln1_gain: float32 [1280], P('ch')
- grad_ln1_bias: float32 [1280], P('ch')
- grad_w_in: float32 [640, 1280], P('ch')
- grad_b_in: float32 [640], P('ch')
- grad_ln2_gain: float32 [640], P('ch')
- grad_ln2_bias: float32 [640], P('ch')
- grad_conv_w: float32 [5, 640, 640], P(None, 'ch')
- grad_conv_b: float32 [640], P('ch')
- grad_ln3_gain: float32 [640], P('ch')
- grad_ln3_bias: float32 [640], P('ch')
- grad_w_out: float32 [640, 1280], P('ch')
- grad_b_out: float32 [1280], P('ch')
The draws below stay inside these ranges and needn't reach their ends.
Inputs may be any that keep to these rules, and one draw needn't show every extreme that they name: `pad_mask`: in each sequence the ones form a prefix of 1024 to 4096 positions; the first sequence is all ones.
All inputs are finite; a program needn't handle non-finite values.
Results may differ from the reference program's by a relative error of at most 0.0066.
Values may be sent and summed in bfloat16 or wider, within the bound.
A program may use at most 256 MiB of HBM per device.

```python
import jax
import jax.numpy as jnp
from jax import lax

D = 1280
INNER = 640
KERNEL = 5
DILATION = 16
SEQS = 16
LEN = 4096


def draw_pad_mask(key, part):
    lengths = jax.random.randint(key, (SEQS,), LEN // 4, LEN + 1)
    lengths = lengths.at[0].set(LEN)
    slots = jnp.arange(LEN, dtype=jnp.int32)[None, :]
    return (slots < lengths[:, None]).astype(jnp.int32)


def shard_levels(key, shape, pieces, low, largest):
    level = 1.0
    for axis_at, blocks in pieces:
        heights = jax.random.uniform(jax.random.fold_in(jax.random.fold_in(key, 6), axis_at), (blocks,), jnp.float32, low / len(pieces), largest / len(pieces))
        level = level * jnp.repeat(jnp.exp(heights), shape[axis_at] // blocks).reshape((-1,) + (1,) * (len(shape) - 1 - axis_at))
    return level


def centred(rng, extent, scale, most, split=(), kind=jnp.bfloat16):
    entries = jax.random.normal(rng, extent, jnp.float32) * scale
    if len(split) > 0:
        entries = shard_levels(rng, extent, split, -0.22, 0.18) * entries
    return jnp.clip(entries, min=-most, max=most).astype(kind)


def setup_inputs(seed: int = 0) -> dict:
    keys = jax.random.split(jax.random.key(seed), 16)
    return {
        "tokens": centred(keys[0], (SEQS, D, LEN), 1.0, 6.0, ((2, 16),)),
        "pad_mask": draw_pad_mask(jax.random.fold_in(keys[15], 71), 0),
        "cotangent": centred(keys[2], (SEQS, D, LEN), 1.0, 6.0, ((1, 2), (2, 16))),
        "ln1_gain": jnp.clip(1.0 + 0.15 * jax.random.normal(keys[3], (D,), jnp.float32), 0.25, 1.75),
        "first_norm_bias": centred(keys[4], (D,), 0.5, 3.0, (), jnp.float32),
        "w_in": centred(keys[5], (INNER, D), D ** -0.5, 0.15625, ((0, 2),)),
        "b_in": centred(keys[6], (INNER,), 0.5, 3.0, ((0, 2),), jnp.float32),
        "ln2_gain": jnp.clip(1.0 + 0.15 * jax.random.normal(keys[7], (INNER,), jnp.float32), 0.25, 1.75),
        "ln2_bias": centred(keys[8], (INNER,), 0.5, 3.0, ((0, 2),), jnp.float32),
        "conv_w": centred(keys[9], (KERNEL, INNER, INNER), (KERNEL * INNER) ** -0.5, 0.109375, ((1, 2),)),
        "conv_b": centred(keys[10], (INNER,), 0.5, 3.0, ((0, 2),), jnp.float32),
        "ln3_gain": jnp.clip(1.0 + 0.15 * jax.random.normal(keys[11], (INNER,), jnp.float32), 0.25, 1.75),
        "ln3_bias": centred(keys[12], (INNER,), 0.5, 3.0, ((0, 2),), jnp.float32),
        "w_out": centred(keys[13], (INNER, D), INNER ** -0.5, 0.25, ((0, 2),)),
        "b_out": centred(keys[14], (D,), 0.5, 3.0, ((0, 2),), jnp.float32),
    }


EPS = 1e-05

@jax.custom_vjp
def low(v):
    return lax.optimization_barrier(v.astype(jnp.bfloat16)).astype(jnp.float32)

@jax.custom_vjp
def low_back(v):
    return v

def low_keep(v):
    return (low(v), None)

def low_pass(kept, grad):
    return (grad,)

def back_keep(v):
    return (v, None)

def back_low(kept, grad):
    return (low(grad),)
low.defvjp(low_keep, low_pass)
low_back.defvjp(back_keep, back_low)

def layer_norm(value, gain, bias):
    center = value - lax.optimization_barrier(jnp.mean(value, axis=-1, keepdims=True))
    scaled = center * lax.rsqrt(lax.optimization_barrier(jnp.mean(center * center, axis=-1, keepdims=True)) + EPS)
    return scaled * gain + bias

def gelu_exact(value):
    return jax.nn.gelu(value, approximate=False)

def project(left_edge, right_edge):
    return jnp.einsum('tzb,bj->tzj', left_edge, right_edge, precision=lax.Precision.HIGHEST)

def block(params, tokens, live_mask):
    ln1_gain, first_norm_bias, w_in, b_in, ln2_gain, ln2_bias, conv_w, conv_b, ln3_gain, ln3_bias, w_out, b_out = params
    first = low(gelu_exact(layer_norm(tokens, ln1_gain, first_norm_bias)))
    narrow = low_back(project(first, w_in.T) + b_in)
    middle = low(gelu_exact(layer_norm(narrow, ln2_gain, ln2_bias)) * live_mask[:, :, None])
    reach = KERNEL // 2 * DILATION
    padded = jnp.pad(middle, ((0, 0), (reach, reach), (0, 0)))
    length_total = tokens.shape[1]
    convolved = conv_b + jnp.zeros_like(middle)
    for kernel_tap in range(KERNEL):
        window = padded[:, kernel_tap * DILATION:kernel_tap * DILATION + length_total]
        convolved = convolved + project(window, conv_w[kernel_tap].T)
    convolved = low_back(convolved)
    last = low(gelu_exact(layer_norm(convolved, ln3_gain, ln3_bias)))
    return tokens + project(last, w_out) + b_out

def reference(tokens, pad_mask, cotangent, ln1_gain, first_norm_bias, w_in, b_in, ln2_gain, ln2_bias, conv_w, conv_b, ln3_gain, ln3_bias, w_out, b_out):
    params = tuple((p.astype(jnp.float32) for p in (ln1_gain, first_norm_bias, w_in, b_in, ln2_gain, ln2_bias, conv_w, conv_b, ln3_gain, ln3_bias, w_out, b_out)))
    groups = SEQS // 2
    inputs = jnp.transpose(tokens.astype(jnp.float32), (0, 2, 1)).reshape(groups, 2, LEN, D)
    masks = pad_mask.astype(jnp.float32).reshape(groups, 2, LEN)
    grads_out = jnp.transpose(cotangent.astype(jnp.float32), (0, 2, 1)).reshape(groups, 2, LEN, D)

    def group_step(totals, item):
        group_in, group_mask, group_grad = item
        result, pull = jax.vjp(lambda p, v: block(p, v, group_mask), params, group_in)
        param_grads, input_grad = pull(group_grad)
        new_totals = tuple((a + b for a, b in zip(totals, param_grads)))
        return (new_totals, (result.astype(jnp.bfloat16), input_grad))
    zeros = tuple((jnp.zeros_like(p) for p in params))
    totals, (results, input_grads) = lax.scan(group_step, zeros, (inputs, masks, grads_out))
    mixed = jnp.transpose(results.reshape(SEQS, LEN, D), (0, 2, 1))
    grad_tokens = jnp.transpose(input_grads.reshape(SEQS, LEN, D), (0, 2, 1))
    return (mixed, grad_tokens, totals[0], totals[1], totals[2], totals[3], totals[4], totals[5], totals[6], totals[7], totals[8], totals[9], totals[10], totals[11])
```

```python
import functools
import math

import jax
import jax.numpy as jnp
from jax import lax
from jax.experimental import pallas as pl
from jax.experimental.pallas import tpu as pltpu
from jax.sharding import PartitionSpec as P

D = 1280
INNER = 640
KERNEL = 5
DILATION = 16
REACH = KERNEL // 2 * DILATION
EPS = 1e-05
HALF_ROOT = math.sqrt(0.5)
DENSITY = 1.0 / math.sqrt(2.0 * math.pi)
F32 = jnp.float32
BF16 = jnp.bfloat16
LANES = 128
VMEM_BYTES = 60 * 1024 * 1024


def rows_of(width):
    return next(r for r in (64, 32, 16) if width % r == 0)


def fold_rows(v):
    return v.reshape(v.shape[0] // 8, 8, v.shape[1]).sum(0)


def fold_lanes(v):
    out = v[:, :LANES]
    for j in range(1, v.shape[1] // LANES):
        out = out + v[:, j * LANES : (j + 1) * LANES]
    return out


def spread(p, length):
    return jnp.concatenate([p] * (length // LANES), axis=1)


def loop(width, body, init):
    rows = rows_of(width)

    def step(i, carry):
        return body(pl.ds(pl.multiple_of(i * rows, rows), rows), carry)

    return lax.fori_loop(0, width // rows, step, init)


def norm_stats(load, width, length):
    zero = jnp.zeros((8, length), F32)
    total = loop(width, lambda sl, a: a + fold_rows(load(sl)), zero)
    mean = total.sum(0, keepdims=True) / width

    def square(sl, a):
        c = load(sl) - mean
        return a + fold_rows(c * c)

    total = loop(width, square, zero)
    return mean, lax.rsqrt(total.sum(0, keepdims=True) / width + EPS)


def cdf(p):
    return 0.5 + 0.5 * lax.erf(p * HALF_ROOT)


def slope(p, phi):
    return phi + p * (DENSITY * jnp.exp(p * p * -0.5))


def call(kernel, grid, in_specs, out_specs, out_shape, scratch=(), prefetch=1, aliases=None, cost=None):
    return pl.pallas_call(
        kernel,
        grid_spec=pltpu.PrefetchScalarGridSpec(
            num_scalar_prefetch=prefetch,
            grid=grid,
            in_specs=in_specs,
            out_specs=out_specs,
            scratch_shapes=list(scratch),
        ),
        out_shape=out_shape,
        input_output_aliases=aliases or {},
        cost_estimate=cost,
        compiler_params=pltpu.CompilerParams(vmem_limit_bytes=VMEM_BYTES),
    )


def cost_of(macs, bytes_accessed):
    return pl.CostEstimate(flops=int(2 * macs), bytes_accessed=int(bytes_accessed), transcendentals=0)


def whole(shape):
    return pl.BlockSpec(shape, lambda i, pre: (0,) * len(shape), pipeline_mode=pl.Buffered(1))


def sds(shape, dtype):
    return jax.ShapeDtypeStruct(shape, dtype)


def first_kernel(pre, x_ref, p_ref, first_ref, stat_ref):
    length = x_ref.shape[2]
    mean, scale = norm_stats(lambda sl: x_ref[0, sl, :].astype(F32), D, length)
    stat_ref[0, 0:1, :] = mean
    stat_ref[0, 1:2, :] = scale

    def body(sl, carry):
        hat = (x_ref[0, sl, :].astype(F32) - mean) * scale
        point = hat * spread(p_ref[0, sl, :], length) + spread(p_ref[1, sl, :], length)
        first_ref[0, sl, :] = (point * cdf(point)).astype(BF16)
        return carry

    loop(D, body, 0)


def first_call(pre, tokens, p1, count, offset):
    seqs, _, length = tokens.shape
    return call(
        first_kernel,
        (count,),
        [
            pl.BlockSpec((1, D, length), lambda i, pre: ((pre[0] + offset + i) % seqs, 0, 0)),
            whole((2, D, LANES)),
        ],
        (
            pl.BlockSpec((1, D, length), lambda i, pre: (i, 0, 0)),
            pl.BlockSpec((1, 2, length), lambda i, pre: (i, 0, 0)),
        ),
        (sds((count, D, length), BF16), sds((count, 2, length), F32)),
        cost=cost_of(count * D * length * 40, count * D * length * 4),
    )(pre, tokens, p1)


def middle_kernel(group, keep, pre, first_ref, mask_ref, w_ref, p_ref, mid_ref, lead_ref, trail_ref, *rest):
    nar_ref = rest[-1]
    length = first_ref.shape[2]
    nar_ref[...] = jnp.dot(w_ref[...], first_ref[0], preferred_element_type=F32)
    mean, scale = norm_stats(lambda sl: nar_ref[sl, :] + spread(p_ref[0, sl, :], length), INNER, length)
    mask = mask_ref[0].astype(F32)

    def body(sl, carry):
        hat = (nar_ref[sl, :] + spread(p_ref[0, sl, :], length) - mean) * scale
        point = hat * spread(p_ref[1, sl, :], length) + spread(p_ref[2, sl, :], length)
        phi = cdf(point)
        mid_ref[0, sl, :] = (point * phi * mask).astype(BF16)
        if keep:
            rest[0][0, sl, :] = hat.astype(BF16)
            rest[1][0, sl, :] = (slope(point, phi) * mask).astype(BF16)
        return carry

    loop(INNER, body, 0)
    if keep:
        rest[2][0] = scale
    place = pl.program_id(0) % group
    for k in range(group):

        @pl.when(place == k)
        def _():
            lead_ref[0, :, k * REACH : (k + 1) * REACH] = mid_ref[0, :, :REACH]
            trail_ref[0, :, k * REACH : (k + 1) * REACH] = mid_ref[0, :, length - REACH :]


def middle_call(pre, first, mask, w_in, p2, count, offset, group, keep):
    _, _, length = first.shape
    seqs = mask.shape[0]
    edge = pl.BlockSpec((1, INNER, group * REACH), lambda i, pre: (i // group, 0, 0))
    edge_shape = sds((count // group, INNER, group * REACH), BF16)
    own = pl.BlockSpec((1, INNER, length), lambda i, pre: (i, 0, 0))
    outs = [own, edge, edge]
    shapes = [sds((count, INNER, length), BF16), edge_shape, edge_shape]
    if keep:
        outs += [own, own, pl.BlockSpec((1, 1, length), lambda i, pre: (i, 0, 0))]
        shapes += [sds((count, INNER, length), BF16)] * 2 + [sds((count, 1, length), F32)]
    return call(
        functools.partial(middle_kernel, group, keep),
        (count,),
        [
            pl.BlockSpec((1, D, length), lambda i, pre: (i, 0, 0)),
            pl.BlockSpec((1, 1, length), lambda i, pre: ((pre[0] + offset + i) % seqs, 0, 0)),
            whole((INNER, D)),
            whole((3, INNER, LANES)),
        ],
        tuple(outs),
        tuple(shapes),
        scratch=[pltpu.VMEM((INNER, length), F32)],
        cost=cost_of(count * INNER * D * length * 1.5, count * (D + INNER * 3) * length * 2),
    )(pre, first, mask.reshape(seqs, 1, length), w_in, p2)


def gather_windows(group, place, body_ref, before_ref, after_ref, pad_ref, cat_ref, order):
    width, length = body_ref.shape[1], body_ref.shape[2]
    pad_ref[:, LANES : LANES + length] = body_ref[0]
    for k in range(group):

        @pl.when(place == k)
        def _():
            pad_ref[:, LANES - REACH : LANES] = before_ref[0, :, k * REACH : (k + 1) * REACH]
            pad_ref[:, LANES + length : LANES + length + REACH] = after_ref[0, :, k * REACH : (k + 1) * REACH]

    for tap in range(KERNEL):
        start = LANES + order * (tap - KERNEL // 2) * DILATION
        cat_ref[tap * width : (tap + 1) * width, :] = pad_ref[:, start : start + length]


def last_kernel(
    group, keep, pre, mid_ref, before_ref, after_ref, x_ref, dy_ref, wc_ref, wo_ref, p_ref, b_ref, *rest
):
    if keep:
        mixed_ref, gw_ref, gb_ref, hat_ref, gp_ref, scale_ref = rest[:6]
    else:
        mixed_ref, gw_ref, gb_ref = rest[1:4]
    pad_ref, cat_ref, conv_ref, last_ref = rest[-4:]
    length = mid_ref.shape[2]
    step = pl.program_id(0)
    gather_windows(group, step % group, mid_ref, before_ref, after_ref, pad_ref, cat_ref, 1)
    conv_ref[...] = jnp.dot(wc_ref[...], cat_ref[...], preferred_element_type=F32)
    mean, scale = norm_stats(lambda sl: conv_ref[sl, :] + spread(p_ref[0, sl, :], length), INNER, length)

    def body(sl, carry):
        hat = (conv_ref[sl, :] + spread(p_ref[0, sl, :], length) - mean) * scale
        point = hat * spread(p_ref[1, sl, :], length) + spread(p_ref[2, sl, :], length)
        phi = cdf(point)
        last_ref[sl, :] = (point * phi).astype(BF16)
        if keep:
            hat_ref[0, sl, :] = hat.astype(BF16)
            gp_ref[0, sl, :] = slope(point, phi).astype(BF16)
        return carry

    loop(INNER, body, 0)
    if keep:
        scale_ref[0] = scale
    branch = jnp.dot(wo_ref[...], last_ref[...], preferred_element_type=F32)
    mixed_ref[0] = (x_ref[0].astype(F32) + branch + spread(b_ref[...], length)).astype(BF16)

    @pl.when(step == 0)
    def _():
        gw_ref[...] = jnp.zeros_like(gw_ref)
        gb_ref[...] = jnp.zeros_like(gb_ref)

    gw_ref[...] += lax.dot_general(
        last_ref[...], dy_ref[0], (((1,), (1,)), ((), ())), preferred_element_type=F32
    )
    gb_ref[...] += fold_lanes(dy_ref[0].astype(F32))


def last_call(pre, mid, before, after, tokens, cot, wc, wo_t, p2, b_out, count, offset, group, keep, mixed):
    _, _, length = mid.shape
    seqs, share, _ = cot.shape
    edge = pl.BlockSpec((1, INNER, group * REACH), lambda i, pre: (i // group, 0, 0))
    own = pl.BlockSpec((1, INNER, length), lambda i, pre: (i, 0, 0))

    def seq_at(i, pre):
        return (pre[0] + offset + i) % seqs

    outs = [
        pl.BlockSpec((1, share, length), lambda i, pre: (seq_at(i, pre), 0, 0)),
        pl.BlockSpec((INNER, share), lambda i, pre: (0, 0)),
        pl.BlockSpec((share, LANES), lambda i, pre: (0, 0)),
    ]
    shapes = [sds((seqs, share, length), BF16), sds((INNER, share), F32), sds((share, LANES), F32)]
    in_specs = [
        own,
        edge,
        edge,
        pl.BlockSpec((1, share, length), lambda i, pre: (seq_at(i, pre), pre[1], 0)),
        pl.BlockSpec((1, share, length), lambda i, pre: (seq_at(i, pre), 0, 0)),
        whole((INNER, KERNEL * INNER)),
        whole((share, INNER)),
        whole((3, INNER, LANES)),
        whole((share, LANES)),
    ]
    args = [pre, mid, before, after, tokens, cot, wc, wo_t, p2, b_out]
    aliases = None
    if keep:
        outs += [own, own, pl.BlockSpec((1, 1, length), lambda i, pre: (i, 0, 0))]
        shapes += [sds((count, INNER, length), BF16)] * 2 + [sds((count, 1, length), F32)]
    else:
        in_specs.append(pl.BlockSpec(memory_space=pl.ANY))
        args.append(mixed)
        aliases = {len(args) - 1: 0}
    return call(
        functools.partial(last_kernel, group, keep),
        (count,),
        in_specs,
        tuple(outs),
        tuple(shapes),
        scratch=[
            pltpu.VMEM((INNER, length + 2 * LANES), BF16),
            pltpu.VMEM((KERNEL * INNER, length), BF16),
            pltpu.VMEM((INNER, length), F32),
            pltpu.VMEM((INNER, length), BF16),
        ],
        aliases=aliases,
        cost=cost_of(count * INNER * (KERNEL * INNER + 2 * share) * length * 1.3, count * share * 6 * length * 2),
    )(*args)


def rear_kernel(group, chs, pre, *refs):
    dy_refs = refs[:chs]
    w_ref, hat_ref, gp_ref, scale_ref, p_ref = refs[chs : chs + 5]
    dconv_ref, lead_ref, trail_ref, gg_ref, gb_ref, gc_ref = refs[chs + 5 : chs + 11]
    dy_ref, d_ref = refs[chs + 11 :]
    share, length = dy_refs[0].shape[1], dy_refs[0].shape[2]
    step = pl.program_id(0)

    @pl.when(step == 0)
    def _():
        gg_ref[...] = jnp.zeros_like(gg_ref)
        gb_ref[...] = jnp.zeros_like(gb_ref)
        gc_ref[...] = jnp.zeros_like(gc_ref)

    for r in range(chs):
        at = pl.multiple_of(((pre[1] + chs - r) % chs) * share, share)
        dy_ref[pl.ds(at, share), :] = dy_refs[r][0]
    d_ref[...] = jnp.dot(w_ref[...], dy_ref[...], preferred_element_type=F32)
    scale = scale_ref[0]
    zero = jnp.zeros((8, length), F32)

    def body(sl, carry):
        d_pre = d_ref[sl, :] * gp_ref[0, sl, :].astype(F32)
        hat = hat_ref[0, sl, :].astype(F32)
        gg_ref[sl, :] += fold_lanes(d_pre * hat)
        gb_ref[sl, :] += fold_lanes(d_pre)
        e = d_pre * spread(p_ref[0, sl, :], length)
        d_ref[sl, :] = e
        return carry[0] + fold_rows(e), carry[1] + fold_rows(e * hat)

    total, dot = loop(INNER, body, (zero, zero))
    total = total.sum(0, keepdims=True) * (scale / INNER)
    dot = dot.sum(0, keepdims=True) * (scale / INNER)

    def finish(sl, carry):
        v = (d_ref[sl, :] * scale - total - hat_ref[0, sl, :].astype(F32) * dot).astype(BF16)
        dconv_ref[0, sl, :] = v
        gc_ref[sl, :] += fold_lanes(v.astype(F32))
        return carry

    loop(INNER, finish, 0)
    place = step % group
    for k in range(group):

        @pl.when(place == k)
        def _():
            lead_ref[0, :, k * REACH : (k + 1) * REACH] = dconv_ref[0, :, :REACH]
            trail_ref[0, :, k * REACH : (k + 1) * REACH] = dconv_ref[0, :, length - REACH :]


def rear_call(pre, cot, others, w_out, hat, gp, scale, p2, begin, count, group):
    seqs, share, length = cot.shape
    chs = 1 + len(others)
    edge = pl.BlockSpec((1, INNER, group * REACH), lambda i, pre: (i // group, 0, 0))
    edge_shape = sds((count // group, INNER, group * REACH), BF16)
    own = pl.BlockSpec((1, INNER, length), lambda i, pre: (i, 0, 0))
    kept = pl.BlockSpec((1, INNER, length), lambda i, pre: (begin + i, 0, 0))
    part = pl.BlockSpec((INNER, LANES), lambda i, pre: (0, 0))
    part_shape = sds((INNER, LANES), F32)
    return call(
        functools.partial(rear_kernel, group, chs),
        (count,),
        [pl.BlockSpec((1, share, length), lambda i, pre: (pre[0] + begin + i, 0, 0))]
        + [pl.BlockSpec((1, share, length), lambda i, pre: (i, 0, 0))] * (chs - 1)
        + [
            whole((INNER, D)),
            kept,
            kept,
            pl.BlockSpec((1, 1, length), lambda i, pre: (begin + i, 0, 0)),
            whole((1, INNER, LANES)),
        ],
        (own, edge, edge, part, part, part),
        (sds((count, INNER, length), BF16), edge_shape, edge_shape, part_shape, part_shape, part_shape),
        scratch=[pltpu.VMEM((D, length), BF16), pltpu.VMEM((INNER, length), F32)],
        cost=cost_of(count * INNER * D * length * 1.5, count * INNER * 5 * length * 2),
    )(pre, cot, *others, w_out, hat, gp, scale, p2)


def front_kernel(group, chs, pre, *refs):
    (
        dconv_ref,
        before_ref,
        after_ref,
        mid_ref,
        hat_ref,
        gp_ref,
        scale_ref,
        x_ref,
        stat_ref,
        dy_ref,
        wc_ref,
        wi_ref,
        p2_ref,
        p1_ref,
    ) = refs[:14]
    refs = refs[14:]
    gt_ref = refs[0]
    send_refs = refs[1:chs]
    gcw_ref, gwi_ref, gg2_ref, gb2_ref, gbi_ref, gg1_ref, gb1_ref = refs[chs : chs + 7]
    pad_ref, cat_ref, d_ref, dn_ref, df_ref, first_ref = refs[chs + 7 :]
    share, length = dy_ref.shape[1], dy_ref.shape[2]
    step = pl.program_id(0)

    @pl.when(step == 0)
    def _():
        for ref in (gcw_ref, gwi_ref, gg2_ref, gb2_ref, gbi_ref, gg1_ref, gb1_ref):
            ref[...] = jnp.zeros_like(ref)

    gather_windows(group, step % group, dconv_ref, before_ref, after_ref, pad_ref, cat_ref, -1)
    d_ref[...] = jnp.dot(wc_ref[...], cat_ref[...], preferred_element_type=F32)
    gcw_ref[...] += lax.dot_general(
        cat_ref[...], mid_ref[0], (((1,), (1,)), ((), ())), preferred_element_type=F32
    )
    scale = scale_ref[0]
    zero = jnp.zeros((8, length), F32)

    def body(sl, carry):
        d_pre = d_ref[sl, :] * gp_ref[0, sl, :].astype(F32)
        hat = hat_ref[0, sl, :].astype(F32)
        gg2_ref[sl, :] += fold_lanes(d_pre * hat)
        gb2_ref[sl, :] += fold_lanes(d_pre)
        e = d_pre * spread(p2_ref[0, sl, :], length)
        d_ref[sl, :] = e
        return carry[0] + fold_rows(e), carry[1] + fold_rows(e * hat)

    total, dot = loop(INNER, body, (zero, zero))
    total = total.sum(0, keepdims=True) * (scale / INNER)
    dot = dot.sum(0, keepdims=True) * (scale / INNER)

    def finish(sl, carry):
        v = (d_ref[sl, :] * scale - total - hat_ref[0, sl, :].astype(F32) * dot).astype(BF16)
        dn_ref[sl, :] = v
        gbi_ref[sl, :] += fold_lanes(v.astype(F32))
        return carry

    loop(INNER, finish, 0)
    df_ref[...] = jnp.dot(wi_ref[...], dn_ref[...], preferred_element_type=F32)
    mean_in, scale_in = stat_ref[0, 0:1, :], stat_ref[0, 1:2, :]

    def inner(sl, carry):
        hat = (x_ref[0, sl, :].astype(F32) - mean_in) * scale_in
        gain = spread(p1_ref[0, sl, :], length)
        point = hat * gain + spread(p1_ref[1, sl, :], length)
        phi = cdf(point)
        first_ref[sl, :] = (point * phi).astype(BF16)
        d_pre = df_ref[sl, :] * slope(point, phi)
        gg1_ref[sl, :] += fold_lanes(d_pre * hat)
        gb1_ref[sl, :] += fold_lanes(d_pre)
        e = d_pre * gain
        df_ref[sl, :] = e
        return carry[0] + fold_rows(e), carry[1] + fold_rows(e * hat)

    total, dot = loop(D, inner, (zero, zero))
    total = total.sum(0, keepdims=True) * (scale_in / D)
    dot = dot.sum(0, keepdims=True) * (scale_in / D)
    gwi_ref[...] += lax.dot_general(
        dn_ref[...], first_ref[...], (((1,), (1,)), ((), ())), preferred_element_type=F32
    )
    rows = rows_of(share)
    for r in range(chs):
        base = ((pre[1] + r) % chs) * share

        def out(i, carry):
            to = pl.ds(pl.multiple_of(i * rows, rows), rows)
            sl = pl.ds(pl.multiple_of(base + i * rows, rows), rows)
            hat = (x_ref[0, sl, :].astype(F32) - mean_in) * scale_in
            v = df_ref[sl, :] * scale_in - total - hat * dot
            if r == 0:
                gt_ref[0, to, :] = v + dy_ref[0, to, :].astype(F32)
            else:
                send_refs[r - 1][0, to, :] = v.astype(BF16)
            return carry

        lax.fori_loop(0, share // rows, out, 0)


def front_call(
    pre, dconv, before, after, mid, hat, gp, scale, tokens, stat, cot, wc_t, wi_t, p2, p1, chs, begin, count, group, gt
):
    seqs, share, length = cot.shape
    edge = pl.BlockSpec((1, INNER, group * REACH), lambda i, pre: (i // group, 0, 0))
    own = pl.BlockSpec((1, INNER, length), lambda i, pre: (i, 0, 0))
    kept = pl.BlockSpec((1, INNER, length), lambda i, pre: (begin + i, 0, 0))

    def seq_block(rows):
        return pl.BlockSpec((1, rows, length), lambda i, pre: (pre[0] + begin + i, 0, 0))

    def const(shape):
        return pl.BlockSpec(shape, lambda i, pre: (0,) * len(shape))

    in_specs = [
        own,
        edge,
        edge,
        kept,
        kept,
        kept,
        pl.BlockSpec((1, 1, length), lambda i, pre: (begin + i, 0, 0)),
        seq_block(D),
        pl.BlockSpec((1, 2, length), lambda i, pre: (begin + i, 0, 0)),
        seq_block(share),
        whole((INNER, KERNEL * INNER)),
        whole((D, INNER)),
        whole((1, INNER, LANES)),
        whole((2, D, LANES)),
    ]
    args = [pre, dconv, before, after, mid, hat, gp, scale, tokens, stat, cot, wc_t, wi_t, p2, p1]
    aliases = None
    kernel = functools.partial(front_kernel, group, chs)
    if gt is not None:
        in_specs.append(pl.BlockSpec(memory_space=pl.ANY))
        args.append(gt)
        aliases = {len(args) - 1: 0}

        def kernel(pre, *refs):
            front_kernel(group, chs, pre, *refs[:14], *refs[15:])

    inner_part, outer_part = (INNER, LANES), (D, LANES)
    consts = [(KERNEL * INNER, INNER), (INNER, D), inner_part, inner_part, inner_part, outer_part, outer_part]
    return call(
        kernel,
        (count,),
        in_specs,
        tuple(
            [seq_block(share)]
            + [pl.BlockSpec((1, share, length), lambda i, pre: (i, 0, 0))] * (chs - 1)
            + [const(s) for s in consts]
        ),
        tuple(
            [sds((seqs, share, length), F32)]
            + [sds((count, share, length), BF16)] * (chs - 1)
            + [sds(s, F32) for s in consts]
        ),
        scratch=[
            pltpu.VMEM((INNER, length + 2 * LANES), BF16),
            pltpu.VMEM((KERNEL * INNER, length), BF16),
            pltpu.VMEM((INNER, length), F32),
            pltpu.VMEM((INNER, length), BF16),
            pltpu.VMEM((D, length), F32),
            pltpu.VMEM((D, length), BF16),
        ],
        aliases=aliases,
        cost=cost_of(count * INNER * (2 * KERNEL * INNER + 2 * D) * length * 1.3, count * D * 8 * length * 2),
    )(*args)


def add_kernel(pre, part_ref, dy_ref, _, gt_ref):
    gt_ref[...] = part_ref[...].astype(F32) + dy_ref[...].astype(F32)


def add_call(pre, part, cot, gt, start):
    seqs, share, length = cot.shape
    count = part.shape[0]
    at = lambda i, pre: (pre[start] + i, 0, 0)
    return call(
        add_kernel,
        (count,),
        [
            pl.BlockSpec((1, share, length), lambda i, pre: (i, 0, 0)),
            pl.BlockSpec((1, share, length), at),
            pl.BlockSpec(memory_space=pl.ANY),
        ],
        pl.BlockSpec((1, share, length), at),
        sds((seqs, share, length), F32),
        aliases={3: 0},
        cost=cost_of(count * share * length, count * share * length * 8),
    )(pre, part, cot, gt)


def rotate(value, axis, count, by):
    return lax.ppermute(value, axis, [(i, (i + by) % count) for i in range(count)])


def shift(value, by):
    count = lax.axis_size("seq")
    pairs = [(i, i + by) for i in range(count) if 0 <= i + by < count]
    return lax.ppermute(value, "seq", pairs)


def rims(lead, trail):
    return shift(trail, 1), shift(lead, -1)


def full_weight(own, axis, ch, chs):
    seq = lax.axis_size("seq")
    rows = own.shape[axis]
    if rows % (seq * 4) == 0 and chs == 2:
        piece_rows = rows // seq
        piece = lax.dynamic_slice_in_dim(own, lax.axis_index("seq") * piece_rows, piece_rows, axis)
        piece = rotate(piece, "ch", 2, 1)
        other = lax.all_gather(piece, "seq", axis=axis, tiled=True)
        first = jnp.where(ch == 0, own, other)
        second = jnp.where(ch == 0, other, own)
        return jnp.concatenate([first, second], axis=axis)
    return lax.all_gather(own, "ch", axis=axis, tiled=True)


def lane_copies(vectors):
    return jnp.broadcast_to(vectors[..., None], vectors.shape + (LANES,))


def body(
    tokens,
    pad_mask,
    cotangent,
    ln1_gain,
    first_norm_bias,
    w_in,
    b_in,
    ln2_gain,
    ln2_bias,
    conv_w,
    conv_b,
    ln3_gain,
    ln3_bias,
    w_out,
    b_out,
):
    chs = lax.axis_size("ch")
    ch = lax.axis_index("ch")
    seqs, _, length = tokens.shape
    share = b_out.shape[0]
    part = b_in.shape[0]
    n = seqs // chs
    group = min(4, n // 2)
    pieces = 2
    size = n // pieces
    starts = [((ch + chs - r) % chs) * n for r in range(1, chs)]
    pre = jnp.stack(
        [ch * n, ch] + [s + q * size for s in starts for q in range(pieces)]
    ).astype(jnp.int32)

    others = []
    for q in range(pieces):
        got = []
        for r in range(1, chs):
            to = (ch + r) % chs
            block = lax.dynamic_slice_in_dim(cotangent, to * n + q * size, size, 0)
            got.append(rotate(block, "ch", chs, r))
        others.append(got)

    inner = jnp.stack([b_in, ln2_gain, ln2_bias, conv_b, ln3_gain, ln3_bias])
    inner = lax.all_gather(inner, "ch", axis=1, tiled=True)
    p1 = lane_copies(jnp.stack([ln1_gain, first_norm_bias]))
    p2 = lane_copies(inner)
    bo = lane_copies(b_out)
    w_in_full = full_weight(w_in, 0, ch, chs)
    conv_full = full_weight(conv_w, 1, ch, chs)
    w_out_full = full_weight(w_out, 0, ch, chs)
    wc = conv_full.transpose(1, 0, 2).reshape(INNER, KERNEL * INNER)
    wc_t = conv_full.transpose(2, 0, 1).reshape(INNER, KERNEL * INNER)
    wi_t = w_in_full.T
    wo_t = lax.dynamic_slice_in_dim(w_out_full, ch * share, share, 1).T

    first_own, stat_own = first_call(pre, tokens, p1, n, 0)
    first_oth, _ = first_call(pre, tokens, p1, seqs - n, n)
    mid_own, lead, trail, hat_mid, gp_mid, scale_mid = middle_call(
        pre, first_own, pad_mask, w_in_full, p2[0:3], n, 0, group, True
    )
    before, after = rims(lead, trail)
    mid_oth, lead, trail = middle_call(pre, first_oth, pad_mask, w_in_full, p2[0:3], seqs - n, n, group, False)
    before_oth, after_oth = rims(lead, trail)
    mixed, gwo_own, gbo_own, hat_out, gp_out, scale_out = last_call(
        pre, mid_own, before, after, tokens, cotangent, wc, wo_t, p2[3:6], bo, n, 0, group, True, None
    )
    rear = []
    for q in range(pieces):
        dconv, lead, trail, *sums = rear_call(
            pre, cotangent, others[q], w_out_full, hat_out, gp_out, scale_out, p2[4:5], q * size, size, group
        )
        rear.append((dconv, rims(lead, trail), sums))
    gt = None
    back = []
    sends = []
    for q in range(pieces):
        dconv, (lead, trail), _ = rear[q]
        gt, *rest = front_call(
            pre, dconv, lead, trail, mid_own, hat_mid, gp_mid, scale_mid, tokens, stat_own, cotangent,
            wc_t, wi_t, p2[1:2], p1, chs, q * size, size, group, gt,
        )
        sends.append([rotate(v, "ch", chs, r + 1) for r, v in enumerate(rest[: chs - 1])])
        back.append(rest[chs - 1 :])
    mixed, gwo_oth, gbo_oth = last_call(
        pre, mid_oth, before_oth, after_oth, tokens, cotangent, wc, wo_t, p2[3:6], bo, seqs - n, n, group, False, mixed
    )
    for q in range(pieces):
        for r in range(chs - 1):
            gt = add_call(pre, sends[q][r], cotangent, gt, 2 + r * pieces + q)

    gcw, gwi, gg2, gb2, gbi, gg1, gb1 = (sum(v[1:], v[0]) for v in zip(*back))
    gg3, gb3, gcb = (sum(v[1:], v[0]) for v in zip(*(r[2] for r in rear)))
    gwo = gwo_own + gwo_oth
    gbo = gbo_own + gbo_oth

    gwo_sum = lax.psum(gwo, "seq")
    gwo_all = lax.all_to_all(gwo_sum.astype(BF16), "ch", 0, 1, tiled=True).astype(F32)
    gcw = lax.psum_scatter(gcw.reshape(KERNEL, INNER, INNER), "ch", scatter_dimension=1, tiled=True)
    gcw = lax.psum(gcw, "seq")
    gwi = lax.psum_scatter(gwi, "ch", scatter_dimension=0, tiled=True)
    gwi = lax.psum(gwi, "seq")
    small = jnp.stack([v.sum(1) for v in (gbi, gg2, gb2, gcb, gg3, gb3)]).reshape(-1)
    outer = jnp.stack([gg1.sum(1), gb1.sum(1)]).reshape(-1)
    bo_slot = lax.dynamic_update_slice(jnp.zeros((D,), F32), gbo.sum(1), (ch * share,))
    total = lax.psum(jnp.concatenate([small, outer, bo_slot]), ("seq", "ch"))
    inner_sums = lax.dynamic_slice_in_dim(total[: 6 * INNER].reshape(6, INNER), ch * part, part, 1)
    outer_sums = lax.dynamic_slice_in_dim(total[6 * INNER :].reshape(3, D), ch * share, share, 1)
    return (
        mixed,
        gt,
        outer_sums[0],
        outer_sums[1],
        gwi,
        inner_sums[0],
        inner_sums[1],
        inner_sums[2],
        gcw,
        inner_sums[3],
        inner_sums[4],
        inner_sums[5],
        gwo_all,
        outer_sums[2],
    )


def solution(mesh):
    in_specs = (
        P(None, None, "seq"),
        P(None, "seq"),
        P(None, "ch", "seq"),
        P(),
        P(),
        P("ch", None),
        P("ch"),
        P("ch"),
        P("ch"),
        P(None, "ch", None),
        P("ch"),
        P("ch"),
        P("ch"),
        P("ch", None),
        P("ch"),
    )
    out_specs = (
        P(None, "ch", "seq"),
        P(None, "ch", "seq"),
        P("ch"),
        P("ch"),
        P("ch", None),
        P("ch"),
        P("ch"),
        P("ch"),
        P(None, "ch", None),
        P("ch"),
        P("ch"),
        P("ch"),
        P("ch", None),
        P("ch"),
    )
    return jax.shard_map(body, mesh=mesh, in_specs=in_specs, out_specs=out_specs, check_vma=False)
```

```python
import functools
import math

import jax
import jax.numpy as jnp
from jax import lax
from jax.experimental import pallas as pl
from jax.experimental.pallas import tpu as pltpu
from jax.sharding import PartitionSpec as P

D = 1280
INNER = 640
KERNEL = 5
DILATION = 16
REACH = KERNEL // 2 * DILATION
EPS = 1e-05
HALF_ROOT = math.sqrt(0.5)
DENSITY = 1.0 / math.sqrt(2.0 * math.pi)
F32 = jnp.float32
BF16 = jnp.bfloat16
LANES = 128
VMEM_BYTES = 60 * 1024 * 1024


def rows_of(width):
    return next(r for r in (64, 32, 16) if width % r == 0)


def fold_rows(v):
    return v.reshape(v.shape[0] // 8, 8, v.shape[1]).sum(0)


def fold_lanes(v):
    out = v[:, :LANES]
    for j in range(1, v.shape[1] // LANES):
        out = out + v[:, j * LANES : (j + 1) * LANES]
    return out


def spread(p, length):
    return jnp.concatenate([p] * (length // LANES), axis=1)


def loop(width, body, init):
    rows = rows_of(width)

    def step(i, carry):
        return body(pl.ds(pl.multiple_of(i * rows, rows), rows), carry)

    return lax.fori_loop(0, width // rows, step, init)


def norm_stats(load, width, length):
    zero = jnp.zeros((8, length), F32)
    total = loop(width, lambda sl, a: a + fold_rows(load(sl)), zero)
    mean = total.sum(0, keepdims=True) / width

    def square(sl, a):
        c = load(sl) - mean
        return a + fold_rows(c * c)

    total = loop(width, square, zero)
    return mean, lax.rsqrt(total.sum(0, keepdims=True) / width + EPS)


def cdf(p):
    return 0.5 + 0.5 * lax.erf(p * HALF_ROOT)


def slope(p, phi):
    return phi + p * (DENSITY * jnp.exp(p * p * -0.5))


def call(kernel, grid, in_specs, out_specs, out_shape, scratch=(), prefetch=1, aliases=None, cost=None):
    return pl.pallas_call(
        kernel,
        grid_spec=pltpu.PrefetchScalarGridSpec(
            num_scalar_prefetch=prefetch,
            grid=grid,
            in_specs=in_specs,
            out_specs=out_specs,
            scratch_shapes=list(scratch),
        ),
        out_shape=out_shape,
        input_output_aliases=aliases or {},
        cost_estimate=cost,
        compiler_params=pltpu.CompilerParams(vmem_limit_bytes=VMEM_BYTES),
    )


def cost_of(macs, bytes_accessed):
    return pl.CostEstimate(flops=int(2 * macs), bytes_accessed=int(bytes_accessed), transcendentals=0)


def whole(shape):
    return pl.BlockSpec(shape, lambda i, pre: (0,) * len(shape), pipeline_mode=pl.Buffered(1))


def sds(shape, dtype):
    return jax.ShapeDtypeStruct(shape, dtype)


def weight_copies(own_refs, full_refs, sems):
    seq, ch = lax.axis_index("seq"), lax.axis_index("ch")
    core, row = seq % 2, (seq // 2) % 2
    send_sem, recv_sem = sems
    across, along, beside = {"ch": 1 - ch}, {"seq": seq + 2 - 4 * row}, {"seq": seq + 1 - 2 * core}

    def part(ref, at, size):
        at = pl.multiple_of(at, 16)
        return ref.at[:, pl.ds(at, size), :] if len(ref.shape) == 3 else ref.at[pl.ds(at, size), :]

    (w_in, conv, w_out), (w_in_full, conv_full, w_out_full) = own_refs, full_refs
    items = [
        (w_in, w_in_full),
        (conv.at[pl.ds(0, 2)], conv_full.at[pl.ds(0, 2)]),
        (conv.at[pl.ds(2, 3)], conv_full.at[pl.ds(2, 3)]),
        (w_out, w_out_full),
    ]
    local, first_hop, second_hop, third_hop = [], [], [], []
    for k, (own, full) in enumerate(items):
        half = own.shape[-2]
        size = half // 4

        def remote(src, dst, slot, device):
            return pltpu.make_async_remote_copy(
                src_ref=src,
                dst_ref=dst,
                send_sem=send_sem.at[k, slot],
                recv_sem=recv_sem.at[k, slot],
                device_id=device,
                device_id_type=pl.DeviceIdType.MESH,
            )

        quarter = (row * 2 + core) * size
        local.append(remote(own, part(full, ch * half, half), 4, beside))
        first_hop.append(remote(part(own, quarter, size), part(full, ch * half + quarter, size), 0, across))
        landed = (1 - ch) * half
        mine = part(full, landed + quarter, size)
        second_hop.append(remote(mine, mine, 1, along))
        both = []
        for j, r in enumerate((row, 1 - row)):
            piece = part(full, landed + (r * 2 + core) * size, size)
            both.append(remote(piece, piece, 2 + j, beside))
        third_hop.append(both)
    return local, first_hop, second_hop, third_hop


def first_kernel(comm, pre, x_ref, p_ref, *rest):
    if comm:
        own_refs, own_vec, first_ref, stat_ref = rest[:3], rest[3], rest[4], rest[5]
        full_refs, full_vec = rest[6:9], rest[9]
        exchange(own_refs, own_vec, full_refs, full_vec, rest[10:12], rest[12:])
    else:
        first_ref, stat_ref = rest
    length = x_ref.shape[2]
    mean, scale = norm_stats(lambda sl: x_ref[0, sl, :].astype(F32), D, length)
    stat_ref[0, 0:1, :] = mean
    stat_ref[0, 1:2, :] = scale

    def body(sl, carry):
        hat = (x_ref[0, sl, :].astype(F32) - mean) * scale
        point = hat * spread(p_ref[0, sl, :], length) + spread(p_ref[1, sl, :], length)
        first_ref[0, sl, :] = (point * cdf(point)).astype(BF16)
        return carry

    loop(D, body, 0)


def exchange(own_refs, own_vec, full_refs, full_vec, sems, vec_sems):
    step, steps = pl.program_id(0), pl.num_programs(0)
    seq, ch = lax.axis_index("seq"), lax.axis_index("ch")
    core, row = seq % 2, (seq // 2) % 2
    local, first_hop, second_hop, third_hop = weight_copies(own_refs, full_refs, sems)
    vec_local = pltpu.make_async_copy(own_vec, full_vec.at[ch], vec_sems[0])
    vec_remote = pltpu.make_async_remote_copy(
        src_ref=own_vec,
        dst_ref=full_vec.at[ch],
        send_sem=vec_sems[1],
        recv_sem=vec_sems[2],
        device_id={"ch": 1 - ch},
        device_id_type=pl.DeviceIdType.MESH,
    )

    @pl.when(step == 0)
    def _():
        barrier = pltpu.get_barrier_semaphore()
        for device in ({"ch": 1 - ch}, {"seq": seq + 2 - 4 * row}, {"seq": seq + 1 - 2 * core}):
            pl.semaphore_signal(barrier, inc=1, device_id=device, device_id_type=pl.DeviceIdType.MESH)
        pl.semaphore_wait(barrier, 3)
        vec_remote.start()
        first_hop[0].start()
        vec_local.start()
        for copy in local:
            copy.start()

    for k in range(4):

        if k > 0:

            @pl.when(step == (0, 1, 4, 7)[k])
            def _():
                first_hop[k].start()

        @pl.when(step == (4, 7, 10, 12)[k])
        def _():
            first_hop[k].wait()
            second_hop[k].start()
            third_hop[k][0].start()

        @pl.when(step == (7, 10, 14, 15)[k])
        def _():
            second_hop[k].wait()
            third_hop[k][1].start()

    @pl.when(step == steps - 1)
    def _():
        vec_remote.wait()
        vec_local.wait()
        for k in range(4):
            local[k].wait()
            third_hop[k][0].wait()
            third_hop[k][1].wait()


def first_call(pre, tokens, p1, weights, vec):
    seqs, _, length = tokens.shape
    comm = weights is not None
    any_spec = pl.BlockSpec(memory_space=pl.ANY)
    in_specs = [pl.BlockSpec((1, D, length), lambda i, pre: ((pre[0] + i) % seqs, 0, 0)), whole((2, D, LANES))]
    out_specs = [
        pl.BlockSpec((1, D, length), lambda i, pre: (i, 0, 0)),
        pl.BlockSpec((1, 2, length), lambda i, pre: (i, 0, 0)),
    ]
    shapes = [sds((seqs, D, length), BF16), sds((seqs, 2, length), F32)]
    args, scratch = [pre, tokens, p1], []
    if comm:
        in_specs += [any_spec] * 4
        out_specs += [any_spec] * 4
        shapes += [sds(w.shape[:-2] + (2 * w.shape[-2], w.shape[-1]), BF16) for w in weights]
        shapes.append(sds((2,) + vec.shape, F32))
        args += list(weights) + [vec]
        dma = pltpu.SemaphoreType.DMA
        scratch = [dma((4, 5)), dma((4, 5)), dma, dma, dma]

    def kernel(*refs):
        first_kernel(comm, *refs)

    if comm:

        def at(i):
            return ((lax.axis_index("ch") * (seqs // 2) + i) % seqs, 0, 0)

        return pl.pallas_call(
            lambda *refs: first_kernel(True, None, *refs),
            grid=(seqs,),
            in_specs=[
                pl.BlockSpec((1, D, length), at),
                pl.BlockSpec((2, D, LANES), lambda i: (0, 0, 0), pipeline_mode=pl.Buffered(1)),
            ]
            + [any_spec] * 4,
            out_specs=tuple(
                [pl.BlockSpec((1, D, length), lambda i: (i, 0, 0)), pl.BlockSpec((1, 2, length), lambda i: (i, 0, 0))]
                + [any_spec] * 4
            ),
            out_shape=tuple(shapes),
            scratch_shapes=scratch,
            cost_estimate=cost_of(seqs * D * length * 40, seqs * D * length * 4),
            compiler_params=pltpu.CompilerParams(
                vmem_limit_bytes=VMEM_BYTES, collective_id=1, has_side_effects=True
            ),
        )(*args[1:])
    return call(kernel, (seqs,), in_specs, tuple(out_specs), tuple(shapes))(*args)


def middle_kernel(group, keep, pre, first_ref, mask_ref, w_ref, p_ref, mid_ref, lead_ref, trail_ref, *rest):
    nar_ref = rest[-1]
    length = first_ref.shape[2]
    nar_ref[...] = jnp.dot(w_ref[...], first_ref[0], preferred_element_type=F32)
    mean, scale = norm_stats(lambda sl: nar_ref[sl, :] + spread(p_ref[0, sl, :], length), INNER, length)
    mask = mask_ref[0].astype(F32)

    def body(sl, carry):
        hat = (nar_ref[sl, :] + spread(p_ref[0, sl, :], length) - mean) * scale
        point = hat * spread(p_ref[1, sl, :], length) + spread(p_ref[2, sl, :], length)
        phi = cdf(point)
        mid_ref[0, sl, :] = (point * phi * mask).astype(BF16)
        if keep:
            rest[0][0, sl, :] = hat.astype(BF16)
            rest[1][0, sl, :] = (slope(point, phi) * mask).astype(BF16)
        return carry

    loop(INNER, body, 0)
    if keep:
        rest[2][0] = scale
    place = pl.program_id(0) % group
    for k in range(group):

        @pl.when(place == k)
        def _():
            lead_ref[0, :, k * REACH : (k + 1) * REACH] = mid_ref[0, :, :REACH]
            trail_ref[0, :, k * REACH : (k + 1) * REACH] = mid_ref[0, :, length - REACH :]


def middle_call(pre, first, mask, w_in, p2, count, offset, group, keep):
    _, _, length = first.shape
    seqs = mask.shape[0]
    edge = pl.BlockSpec((1, INNER, group * REACH), lambda i, pre: (i // group, 0, 0))
    edge_shape = sds((count // group, INNER, group * REACH), BF16)
    own = pl.BlockSpec((1, INNER, length), lambda i, pre: (i, 0, 0))
    outs = [own, edge, edge]
    shapes = [sds((count, INNER, length), BF16), edge_shape, edge_shape]
    if keep:
        outs += [own, own, pl.BlockSpec((1, 1, length), lambda i, pre: (i, 0, 0))]
        shapes += [sds((count, INNER, length), BF16)] * 2 + [sds((count, 1, length), F32)]
    return call(
        functools.partial(middle_kernel, group, keep),
        (count,),
        [
            pl.BlockSpec((1, D, length), lambda i, pre: (offset + i, 0, 0)),
            pl.BlockSpec((1, 1, length), lambda i, pre: ((pre[0] + offset + i) % seqs, 0, 0)),
            whole((INNER, D)),
            whole((3, INNER, LANES)),
        ],
        tuple(outs),
        tuple(shapes),
        scratch=[pltpu.VMEM((INNER, length), F32)],
        cost=cost_of(count * INNER * D * length * 1.5, count * (D + INNER * 3) * length * 2),
    )(pre, first, mask.reshape(seqs, 1, length), w_in, p2)


def gather_windows(group, place, body_ref, before_ref, after_ref, pad_ref, cat_ref, order):
    width, length = body_ref.shape[1], body_ref.shape[2]
    pad_ref[:, LANES : LANES + length] = body_ref[0]
    for k in range(group):

        @pl.when(place == k)
        def _():
            pad_ref[:, LANES - REACH : LANES] = before_ref[0, :, k * REACH : (k + 1) * REACH]
            pad_ref[:, LANES + length : LANES + length + REACH] = after_ref[0, :, k * REACH : (k + 1) * REACH]

    for tap in range(KERNEL):
        start = LANES + order * (tap - KERNEL // 2) * DILATION
        cat_ref[tap * width : (tap + 1) * width, :] = pad_ref[:, start : start + length]


def last_kernel(
    group, keep, pre, mid_ref, before_ref, after_ref, x_ref, wc_ref, wo_ref, p_ref, b_ref, *rest
):
    if keep:
        mixed_ref, hat_ref, gp_ref, scale_ref, last_ref = rest[:5]
        last_ref = last_ref.at[0]
        pad_ref, cat_ref, conv_ref = rest[-3:]
    else:
        mixed_ref = rest[1]
        pad_ref, cat_ref, conv_ref, last_ref = rest[-4:]
    length = mid_ref.shape[2]
    step = pl.program_id(0)
    gather_windows(group, step % group, mid_ref, before_ref, after_ref, pad_ref, cat_ref, 1)
    conv_ref[...] = jnp.dot(wc_ref[...], cat_ref[...], preferred_element_type=F32)
    mean, scale = norm_stats(lambda sl: conv_ref[sl, :] + spread(p_ref[0, sl, :], length), INNER, length)

    def body(sl, carry):
        hat = (conv_ref[sl, :] + spread(p_ref[0, sl, :], length) - mean) * scale
        point = hat * spread(p_ref[1, sl, :], length) + spread(p_ref[2, sl, :], length)
        phi = cdf(point)
        last_ref[sl, :] = (point * phi).astype(BF16)
        if keep:
            hat_ref[0, sl, :] = hat.astype(BF16)
            gp_ref[0, sl, :] = slope(point, phi).astype(BF16)
        return carry

    loop(INNER, body, 0)
    if keep:
        scale_ref[0] = scale
    branch = jnp.dot(wo_ref[...], last_ref[...], preferred_element_type=F32)
    mixed_ref[0] = (x_ref[0].astype(F32) + branch + spread(b_ref[...], length)).astype(BF16)


def last_call(pre, mid, before, after, tokens, wc, wo_t, p2, b_out, count, offset, group, keep, mixed):
    _, _, length = mid.shape
    seqs, share = tokens.shape[0], wo_t.shape[0]
    edge = pl.BlockSpec((1, INNER, group * REACH), lambda i, pre: (i // group, 0, 0))
    own = pl.BlockSpec((1, INNER, length), lambda i, pre: (i, 0, 0))

    def seq_at(i, pre):
        return (pre[0] + offset + i) % seqs

    outs = [pl.BlockSpec((1, share, length), lambda i, pre: (seq_at(i, pre), 0, 0))]
    shapes = [sds((seqs, share, length), BF16)]
    in_specs = [
        own,
        edge,
        edge,
        pl.BlockSpec((1, share, length), lambda i, pre: (seq_at(i, pre), pre[1], 0)),
        whole((INNER, KERNEL * INNER)),
        whole((share, INNER)),
        whole((3, INNER, LANES)),
        whole((share, LANES)),
    ]
    args = [pre, mid, before, after, tokens, wc, wo_t, p2, b_out]
    aliases = None
    scratch = [
        pltpu.VMEM((INNER, length + 2 * LANES), BF16),
        pltpu.VMEM((KERNEL * INNER, length), BF16),
        pltpu.VMEM((INNER, length), F32),
    ]
    if keep:
        outs += [own, own, pl.BlockSpec((1, 1, length), lambda i, pre: (i, 0, 0)), own]
        saved = sds((count, INNER, length), BF16)
        shapes += [saved, saved, sds((count, 1, length), F32), saved]
    else:
        scratch.append(pltpu.VMEM((INNER, length), BF16))
        in_specs.append(pl.BlockSpec(memory_space=pl.ANY))
        args.append(mixed)
        aliases = {len(args) - 1: 0}
    return call(
        functools.partial(last_kernel, group, keep),
        (count,),
        in_specs,
        tuple(outs),
        tuple(shapes),
        scratch=scratch,
        aliases=aliases,
        cost=cost_of(count * INNER * (KERNEL * INNER + share) * length * 1.3, count * share * 6 * length * 2),
    )(*args)


def rear_kernel(group, chs, pre, *refs):
    dy_refs = refs[:chs]
    w_ref, hat_ref, gp_ref, last_ref, scale_ref, p_ref = refs[chs : chs + 6]
    dconv_ref, lead_ref, trail_ref, gg_ref, gb_ref, gc_ref, gw_ref, go_ref = refs[chs + 6 : chs + 14]
    dy_ref, d_ref = refs[chs + 14 :]
    share, length = dy_refs[0].shape[1], dy_refs[0].shape[2]
    step = pl.program_id(0)

    @pl.when(step == 0)
    def _():
        gg_ref[...] = jnp.zeros_like(gg_ref)
        gb_ref[...] = jnp.zeros_like(gb_ref)
        gc_ref[...] = jnp.zeros_like(gc_ref)
        gw_ref[...] = jnp.zeros_like(gw_ref)
        go_ref[...] = jnp.zeros_like(go_ref)

    for r in range(chs):
        at = pl.multiple_of(((pre[1] + chs - r) % chs) * share, share)
        dy_ref[pl.ds(at, share), :] = dy_refs[r][0]
    d_ref[...] = jnp.dot(w_ref[...], dy_ref[...], preferred_element_type=F32)
    gw_ref[...] += lax.dot_general(
        last_ref[0], dy_ref[...], (((1,), (1,)), ((), ())), preferred_element_type=F32
    )
    go_ref[...] += fold_lanes(dy_ref[...].astype(F32))
    scale = scale_ref[0]
    zero = jnp.zeros((8, length), F32)

    def body(sl, carry):
        d_pre = d_ref[sl, :] * gp_ref[0, sl, :].astype(F32)
        hat = hat_ref[0, sl, :].astype(F32)
        gg_ref[sl, :] += fold_lanes(d_pre * hat)
        gb_ref[sl, :] += fold_lanes(d_pre)
        e = d_pre * spread(p_ref[0, sl, :], length)
        d_ref[sl, :] = e
        return carry[0] + fold_rows(e), carry[1] + fold_rows(e * hat)

    total, dot = loop(INNER, body, (zero, zero))
    total = total.sum(0, keepdims=True) * (scale / INNER)
    dot = dot.sum(0, keepdims=True) * (scale / INNER)

    def finish(sl, carry):
        v = (d_ref[sl, :] * scale - total - hat_ref[0, sl, :].astype(F32) * dot).astype(BF16)
        dconv_ref[0, sl, :] = v
        gc_ref[sl, :] += fold_lanes(v.astype(F32))
        return carry

    loop(INNER, finish, 0)
    place = step % group
    for k in range(group):

        @pl.when(place == k)
        def _():
            lead_ref[0, :, k * REACH : (k + 1) * REACH] = dconv_ref[0, :, :REACH]
            trail_ref[0, :, k * REACH : (k + 1) * REACH] = dconv_ref[0, :, length - REACH :]


def rear_call(pre, cot, others, w_out, hat, gp, last, scale, p2, begin, count, group):
    seqs, share, length = cot.shape
    chs = 1 + len(others)
    edge = pl.BlockSpec((1, INNER, group * REACH), lambda i, pre: (i // group, 0, 0))
    edge_shape = sds((count // group, INNER, group * REACH), BF16)
    own = pl.BlockSpec((1, INNER, length), lambda i, pre: (i, 0, 0))
    kept = pl.BlockSpec((1, INNER, length), lambda i, pre: (begin + i, 0, 0))
    part = pl.BlockSpec((INNER, LANES), lambda i, pre: (0, 0))
    part_shape = sds((INNER, LANES), F32)
    return call(
        functools.partial(rear_kernel, group, chs),
        (count,),
        [pl.BlockSpec((1, share, length), lambda i, pre: (pre[0] + begin + i, 0, 0))]
        + [pl.BlockSpec((1, share, length), lambda i, pre: (i, 0, 0))] * (chs - 1)
        + [
            whole((INNER, D)),
            kept,
            kept,
            kept,
            pl.BlockSpec((1, 1, length), lambda i, pre: (begin + i, 0, 0)),
            whole((1, INNER, LANES)),
        ],
        (
            own,
            edge,
            edge,
            part,
            part,
            part,
            pl.BlockSpec((INNER, D), lambda i, pre: (0, 0)),
            pl.BlockSpec((D, LANES), lambda i, pre: (0, 0)),
        ),
        (
            sds((count, INNER, length), BF16),
            edge_shape,
            edge_shape,
            part_shape,
            part_shape,
            part_shape,
            sds((INNER, D), F32),
            sds((D, LANES), F32),
        ),
        scratch=[pltpu.VMEM((D, length), BF16), pltpu.VMEM((INNER, length), F32)],
        cost=cost_of(count * INNER * D * length * 1.5, count * INNER * 5 * length * 2),
    )(pre, cot, *others, w_out, hat, gp, last, scale, p2)


def front_kernel(group, chs, pre, *refs):
    (
        dconv_ref,
        before_ref,
        after_ref,
        mid_ref,
        hat_ref,
        gp_ref,
        scale_ref,
        x_ref,
        stat_ref,
        dy_ref,
        wc_ref,
        wi_ref,
        p2_ref,
        p1_ref,
    ) = refs[:14]
    refs = refs[14:]
    gt_ref = refs[0]
    send_refs = refs[1:chs]
    gcw_ref, gwi_ref, gg2_ref, gb2_ref, gbi_ref, gg1_ref, gb1_ref = refs[chs : chs + 7]
    pad_ref, cat_ref, d_ref, dn_ref, df_ref, first_ref = refs[chs + 7 :]
    share, length = dy_ref.shape[1], dy_ref.shape[2]
    step = pl.program_id(0)

    @pl.when(step == 0)
    def _():
        for ref in (gcw_ref, gwi_ref, gg2_ref, gb2_ref, gbi_ref, gg1_ref, gb1_ref):
            ref[...] = jnp.zeros_like(ref)

    gather_windows(group, step % group, dconv_ref, before_ref, after_ref, pad_ref, cat_ref, -1)
    d_ref[...] = jnp.dot(wc_ref[...], cat_ref[...], preferred_element_type=F32)
    gcw_ref[...] += lax.dot_general(
        cat_ref[...], mid_ref[0], (((1,), (1,)), ((), ())), preferred_element_type=F32
    )
    scale = scale_ref[0]
    zero = jnp.zeros((8, length), F32)

    def body(sl, carry):
        d_pre = d_ref[sl, :] * gp_ref[0, sl, :].astype(F32)
        hat = hat_ref[0, sl, :].astype(F32)
        gg2_ref[sl, :] += fold_lanes(d_pre * hat)
        gb2_ref[sl, :] += fold_lanes(d_pre)
        e = d_pre * spread(p2_ref[0, sl, :], length)
        d_ref[sl, :] = e
        return carry[0] + fold_rows(e), carry[1] + fold_rows(e * hat)

    total, dot = loop(INNER, body, (zero, zero))
    total = total.sum(0, keepdims=True) * (scale / INNER)
    dot = dot.sum(0, keepdims=True) * (scale / INNER)

    def finish(sl, carry):
        v = (d_ref[sl, :] * scale - total - hat_ref[0, sl, :].astype(F32) * dot).astype(BF16)
        dn_ref[sl, :] = v
        gbi_ref[sl, :] += fold_lanes(v.astype(F32))
        return carry

    loop(INNER, finish, 0)
    df_ref[...] = jnp.dot(wi_ref[...], dn_ref[...], preferred_element_type=F32)
    mean_in, scale_in = stat_ref[0, 0:1, :], stat_ref[0, 1:2, :]

    def inner(sl, carry):
        hat = (x_ref[0, sl, :].astype(F32) - mean_in) * scale_in
        gain = spread(p1_ref[0, sl, :], length)
        point = hat * gain + spread(p1_ref[1, sl, :], length)
        phi = cdf(point)
        first_ref[sl, :] = (point * phi).astype(BF16)
        d_pre = df_ref[sl, :] * slope(point, phi)
        gg1_ref[sl, :] += fold_lanes(d_pre * hat)
        gb1_ref[sl, :] += fold_lanes(d_pre)
        e = d_pre * gain
        df_ref[sl, :] = e
        return carry[0] + fold_rows(e), carry[1] + fold_rows(e * hat)

    total, dot = loop(D, inner, (zero, zero))
    total = total.sum(0, keepdims=True) * (scale_in / D)
    dot = dot.sum(0, keepdims=True) * (scale_in / D)
    gwi_ref[...] += lax.dot_general(
        dn_ref[...], first_ref[...], (((1,), (1,)), ((), ())), preferred_element_type=F32
    )
    rows = rows_of(share)
    for r in range(chs):
        base = ((pre[1] + r) % chs) * share

        def out(i, carry):
            to = pl.ds(pl.multiple_of(i * rows, rows), rows)
            sl = pl.ds(pl.multiple_of(base + i * rows, rows), rows)
            hat = (x_ref[0, sl, :].astype(F32) - mean_in) * scale_in
            v = df_ref[sl, :] * scale_in - total - hat * dot
            if r == 0:
                gt_ref[0, to, :] = v + dy_ref[0, to, :].astype(F32)
            else:
                send_refs[r - 1][0, to, :] = v.astype(BF16)
            return carry

        lax.fori_loop(0, share // rows, out, 0)


def front_call(
    pre, dconv, before, after, mid, hat, gp, scale, tokens, stat, cot, wc_t, wi_t, p2, p1, chs, begin, count, group, gt
):
    seqs, share, length = cot.shape
    edge = pl.BlockSpec((1, INNER, group * REACH), lambda i, pre: (i // group, 0, 0))
    own = pl.BlockSpec((1, INNER, length), lambda i, pre: (i, 0, 0))
    kept = pl.BlockSpec((1, INNER, length), lambda i, pre: (begin + i, 0, 0))

    def seq_block(rows):
        return pl.BlockSpec((1, rows, length), lambda i, pre: (pre[0] + begin + i, 0, 0))

    def const(shape):
        return pl.BlockSpec(shape, lambda i, pre: (0,) * len(shape))

    in_specs = [
        own,
        edge,
        edge,
        kept,
        kept,
        kept,
        pl.BlockSpec((1, 1, length), lambda i, pre: (begin + i, 0, 0)),
        seq_block(D),
        pl.BlockSpec((1, 2, length), lambda i, pre: (begin + i, 0, 0)),
        seq_block(share),
        whole((INNER, KERNEL * INNER)),
        whole((D, INNER)),
        whole((1, INNER, LANES)),
        whole((2, D, LANES)),
    ]
    args = [pre, dconv, before, after, mid, hat, gp, scale, tokens, stat, cot, wc_t, wi_t, p2, p1]
    aliases = None
    kernel = functools.partial(front_kernel, group, chs)
    if gt is not None:
        in_specs.append(pl.BlockSpec(memory_space=pl.ANY))
        args.append(gt)
        aliases = {len(args) - 1: 0}

        def kernel(pre, *refs):
            front_kernel(group, chs, pre, *refs[:14], *refs[15:])

    inner_part, outer_part = (INNER, LANES), (D, LANES)
    consts = [(KERNEL * INNER, INNER), (INNER, D), inner_part, inner_part, inner_part, outer_part, outer_part]
    return call(
        kernel,
        (count,),
        in_specs,
        tuple(
            [seq_block(share)]
            + [pl.BlockSpec((1, share, length), lambda i, pre: (i, 0, 0))] * (chs - 1)
            + [const(s) for s in consts]
        ),
        tuple(
            [sds((seqs, share, length), F32)]
            + [sds((count, share, length), BF16)] * (chs - 1)
            + [sds(s, F32) for s in consts]
        ),
        scratch=[
            pltpu.VMEM((INNER, length + 2 * LANES), BF16),
            pltpu.VMEM((KERNEL * INNER, length), BF16),
            pltpu.VMEM((INNER, length), F32),
            pltpu.VMEM((INNER, length), BF16),
            pltpu.VMEM((D, length), F32),
            pltpu.VMEM((D, length), BF16),
        ],
        aliases=aliases,
        cost=cost_of(count * INNER * (2 * KERNEL * INNER + 2 * D) * length * 1.3, count * D * 8 * length * 2),
    )(*args)


def add_kernel(pre, part_ref, dy_ref, _, gt_ref):
    gt_ref[...] = part_ref[...].astype(F32) + dy_ref[...].astype(F32)


def add_call(pre, part, cot, gt, start):
    seqs, share, length = cot.shape
    count = part.shape[0]
    at = lambda i, pre: (pre[start] + i, 0, 0)
    return call(
        add_kernel,
        (count,),
        [
            pl.BlockSpec((1, share, length), lambda i, pre: (i, 0, 0)),
            pl.BlockSpec((1, share, length), at),
            pl.BlockSpec(memory_space=pl.ANY),
        ],
        pl.BlockSpec((1, share, length), at),
        sds((seqs, share, length), F32),
        aliases={3: 0},
        cost=cost_of(count * share * length, count * share * length * 8),
    )(pre, part, cot, gt)


def turn_kernel(pre, w_ref, flat_ref, turned_ref):
    unit = (
        lax.broadcasted_iota(jnp.int32, (INNER, INNER), 0) == lax.broadcasted_iota(jnp.int32, (INNER, INNER), 1)
    ).astype(F32).astype(BF16)
    flat_ref[...] = w_ref[0]
    turned_ref[...] = lax.dot_general(
        unit, w_ref[0], (((1,), (1,)), ((), ())), preferred_element_type=F32
    ).astype(BF16)


def turn_call(pre, conv):
    block = pl.BlockSpec((INNER, INNER), lambda k, pre: (0, k))
    shape = sds((INNER, KERNEL * INNER), BF16)
    return call(
        turn_kernel,
        (KERNEL,),
        [pl.BlockSpec((1, INNER, INNER), lambda k, pre: (k, 0, 0))],
        (block, block),
        (shape, shape),
        cost=cost_of(KERNEL * INNER**3, KERNEL * INNER * INNER * 6),
    )(pre, conv)


def reduce_kernel(stages, half_rows, *refs):
    gcw_ref, gwi_ref, gwo_ref, small_ref, out_ref = refs[:5]
    acc, send, recv, swap, res, load_sem, send_sem, recv_sem = refs[5:]
    seq, ch = lax.axis_index("seq"), lax.axis_index("ch")
    streams = len(stages)
    rows = acc.shape[1] // streams
    bits = sorted(stages[0])

    def partner(b):
        return {"seq": seq + (1 - 2 * ((seq // (1 << b)) % 2)) * (1 << b)}

    loads = []
    for h in range(2):
        mine = pl.ds(h * half_rows, half_rows)
        pieces = [gcw_ref.at[k, mine, :] for k in range(KERNEL)]
        for ref in (gwi_ref, gwo_ref):
            pieces += [ref.at[mine, pl.ds(j * INNER, INNER)] for j in range(D // INNER)]
        for j, piece in enumerate(pieces):
            loads.append((piece, acc.at[h, pl.ds(j * half_rows, half_rows), :]))
        used = len(pieces) * half_rows
        loads.append((small_ref.at[h], acc.at[h, pl.ds(used, small_ref.shape[1]), :]))
        used += small_ref.shape[1]
        acc[h, used:, :] = jnp.zeros((acc.shape[1] - used, INNER), F32)
    loads = [pltpu.make_async_copy(a, b, load_sem.at[j]) for j, (a, b) in enumerate(loads)]
    for copy in loads:
        copy.start()

    barrier = pltpu.get_barrier_semaphore()
    for device in [partner(b) for b in bits] + [{"ch": 1 - ch}]:
        pl.semaphore_signal(barrier, inc=1, device_id=device, device_id_type=pl.DeviceIdType.MESH)
    pl.semaphore_wait(barrier, len(bits) + 1)
    for copy in loads:
        copy.wait()

    def remote(src, dst, slot, device):
        return pltpu.make_async_remote_copy(
            src_ref=src,
            dst_ref=dst,
            send_sem=send_sem.at[slot],
            recv_sem=recv_sem.at[slot],
            device_id=device,
            device_id_type=pl.DeviceIdType.MESH,
        )

    def sliced(count, body):
        step = next(r for r in (96, 48, 32, 16) if count % r == 0)

        def one(i, carry):
            body(pl.multiple_of(i * step, 16), step)
            return carry

        lax.fori_loop(0, count // step, one, 0)

    low = [jnp.int32(q * rows) for q in range(streams)]
    size = rows
    at = 0
    pending = [None] * streams
    slot = 0
    for t in range(len(bits)):
        size //= 2
        for q in range(streams):
            if pending[q] is not None:
                pending[q]()
            b = stages[q][t]
            bit = (seq // (1 << b)) % 2
            away = low[q] + (1 - bit) * size
            low[q] = low[q] + bit * size
            keep = low[q]
            for h in range(2):

                def pack(i, step, h=h):
                    send[q, h, pl.ds(at + i, step), :] = acc[
                        h, pl.ds(pl.multiple_of(away + i, 16), step), :
                    ].astype(BF16)

                sliced(size, pack)
            window = pl.ds(at, size)
            copy = remote(send.at[q, :, window, :], recv.at[q, :, window, :], slot, partner(b))
            copy.start()

            def finish(q=q, at=at, size=size, keep=keep, copy=copy):
                copy.wait()
                for h in range(2):

                    def add(i, step, h=h):
                        place = pl.ds(pl.multiple_of(keep + i, 16), step)
                        acc[h, place, :] += recv[q, h, pl.ds(at + i, step), :].astype(F32)

                    sliced(size, add)

            pending[q] = finish
            slot += 1
        at += size

    swaps = []
    for q in range(streams):
        pending[q]()
        swap[0, q] = acc[1 - ch, pl.ds(pl.multiple_of(low[q], 16), size), :].astype(BF16)
        copy = remote(swap.at[0, q], swap.at[1, q], slot, {"ch": 1 - ch})
        copy.start()
        swaps.append(copy)
        slot += 1
    waiting = [None] * streams
    for q in range(streams):
        swaps[q].wait()
        place = pl.ds(pl.multiple_of(low[q], 16), size)
        res[place, :] = (acc[ch, place, :] + swap[1, q].astype(F32)).astype(BF16)
    for t in reversed(range(len(bits))):
        for q in range(streams):
            if waiting[q] is not None:
                waiting[q].wait()
            b = stages[q][t]
            place = pl.ds(pl.multiple_of(low[q], 16), size)
            copy = remote(res.at[place, :], res.at[place, :], slot, partner(b))
            copy.start()
            waiting[q] = copy
            low[q] = low[q] - ((seq // (1 << b)) % 2) * size
            slot += 1
        size *= 2
    for q in range(streams):
        waiting[q].wait()
    done = pltpu.make_async_copy(res, out_ref, load_sem.at[0])
    done.start()
    done.wait()


def reduce_call(gcw, gwi, gwo, small, seq_count):
    half_rows = INNER // 2
    levels = seq_count.bit_length() - 1
    used = half_rows * (KERNEL + 2 * D // INNER) + small.shape[1]
    unit = 2 * seq_count * 16
    rows = -(-used // unit) * unit
    order = list(range(levels))
    stages = (tuple(order), tuple(order[:1] + order[2:] + order[1:2]))
    streams = len(stages)
    moved = rows // streams - rows // streams // seq_count
    last = rows // streams // seq_count
    slots = streams * (2 * levels + 1)
    any_spec = pl.BlockSpec(memory_space=pl.ANY)
    return pl.pallas_call(
        functools.partial(reduce_kernel, stages, half_rows),
        in_specs=[any_spec] * 4,
        out_specs=any_spec,
        out_shape=sds((rows, INNER), BF16),
        scratch_shapes=[
            pltpu.VMEM((2, rows, INNER), F32),
            pltpu.VMEM((streams, 2, moved, INNER), BF16),
            pltpu.VMEM((streams, 2, moved, INNER), BF16),
            pltpu.VMEM((2, streams, last, INNER), BF16),
            pltpu.VMEM((rows, INNER), BF16),
            pltpu.SemaphoreType.DMA((2 * (KERNEL + 2 * D // INNER + 1),)),
            pltpu.SemaphoreType.DMA((slots,)),
            pltpu.SemaphoreType.DMA((slots,)),
        ],
        cost_estimate=cost_of(0, rows * INNER * 12),
        compiler_params=pltpu.CompilerParams(vmem_limit_bytes=VMEM_BYTES, collective_id=2, has_side_effects=True),
    )(gcw, gwi, gwo, small)


def rotate(value, axis, count, by):
    return lax.ppermute(value, axis, [(i, (i + by) % count) for i in range(count)])


def shift(value, by):
    count = lax.axis_size("seq")
    pairs = [(i, i + by) for i in range(count) if 0 <= i + by < count]
    return lax.ppermute(value, "seq", pairs)


def rims(lead, trail):
    return shift(trail, 1), shift(lead, -1)


def own_slice(value, width, dim):
    return lax.dynamic_slice_in_dim(value, lax.axis_index("ch") * width, width, dim)


def lane_copies(vectors):
    return jnp.broadcast_to(vectors[..., None], vectors.shape + (LANES,))


def body(
    tokens,
    pad_mask,
    cotangent,
    ln1_gain,
    first_norm_bias,
    w_in,
    b_in,
    ln2_gain,
    ln2_bias,
    conv_w,
    conv_b,
    ln3_gain,
    ln3_bias,
    w_out,
    b_out,
):
    chs = lax.axis_size("ch")
    ch = lax.axis_index("ch")
    seqs, _, length = tokens.shape
    share = b_out.shape[0]
    part = b_in.shape[0]
    n = seqs // chs
    group = min(4, n)
    starts = [((ch + chs - r) % chs) * n for r in range(1, chs)]
    pre = jnp.stack([ch * n, ch] + starts).astype(jnp.int32)
    pair = chs == 2

    p1 = lane_copies(jnp.stack([ln1_gain, first_norm_bias]))
    bo = lane_copies(b_out)
    vec = jnp.stack([b_in, ln2_gain, ln2_bias, conv_b, ln3_gain, ln3_bias, b_in, b_in])
    if pair:
        first, stat, w_in_full, conv_full, w_out_full, vec_full = first_call(
            pre, tokens, p1, (w_in, conv_w, w_out), vec
        )
        inner = vec_full.transpose(1, 0, 2).reshape(8, INNER)[:6]
    else:
        first, stat = first_call(pre, tokens, p1, None, None)
        w_in_full = lax.all_gather(w_in, "ch", axis=0, tiled=True)
        conv_full = lax.all_gather(conv_w, "ch", axis=1, tiled=True)
        w_out_full = lax.all_gather(w_out, "ch", axis=0, tiled=True)
        inner = lax.all_gather(vec, "ch", axis=1, tiled=True)[:6]

    others = []
    for r in range(1, chs):
        block = lax.dynamic_slice_in_dim(cotangent, ((ch + r) % chs) * n, n, 0)
        block, _ = lax.optimization_barrier((block, stat))
        others.append(rotate(block, "ch", chs, r))
    p2 = lane_copies(inner)
    wc, wc_t = turn_call(pre, conv_full)
    wi_t = w_in_full.T
    wo_t = lax.dynamic_slice_in_dim(w_out_full, ch * share, share, 1).T

    mid_own, lead, trail, hat_mid, gp_mid, scale_mid = middle_call(
        pre, first, pad_mask, w_in_full, p2[0:3], n, 0, group, True
    )
    before, after = rims(lead, trail)
    mid_oth, lead, trail = middle_call(pre, first, pad_mask, w_in_full, p2[0:3], seqs - n, n, group, False)
    before_oth, after_oth = rims(lead, trail)
    mixed, hat_out, gp_out, scale_out, last_own = last_call(
        pre, mid_own, before, after, tokens, wc, wo_t, p2[3:6], bo, n, 0, group, True, None
    )
    dconv, lead, trail, gg3, gb3, gcb, gwo, gbo = rear_call(
        pre, cotangent, others, w_out_full, hat_out, gp_out, last_own, scale_out, p2[4:5], 0, n, group
    )
    lead, trail = rims(lead, trail)
    gt, *rest = front_call(
        pre, dconv, lead, trail, mid_own, hat_mid, gp_mid, scale_mid, tokens, stat, cotangent,
        wc_t, wi_t, p2[1:2], p1, chs, 0, n, group, None,
    )
    sends = [rotate(v, "ch", chs, r + 1) for r, v in enumerate(rest[: chs - 1])]
    gcw, gwi, gg2, gb2, gbi, gg1, gb1 = rest[chs - 1 :]
    mixed, = last_call(
        pre, mid_oth, before_oth, after_oth, tokens, wc, wo_t, p2[3:6], bo, seqs - n, n, group, False, mixed
    )
    gcw = gcw.reshape(KERNEL, INNER, INNER)
    inner_sums = jnp.stack([v.sum(1) for v in (gbi, gg2, gb2, gcb, gg3, gb3)])
    outer_sums = jnp.stack([v.sum(1) for v in (gg1, gb1, gbo)])

    if pair:
        small = jnp.concatenate(
            [
                inner_sums.reshape(6, 2, part).transpose(1, 0, 2).reshape(2, 3, INNER),
                outer_sums.reshape(3, 2, share).transpose(1, 0, 2),
                jnp.zeros((2, 10, INNER), F32),
            ],
            axis=1,
        )
        total = reduce_call(gcw, gwi, gwo, small, lax.axis_size("seq"))
        gcw = total[: KERNEL * part].reshape(KERNEL, part, INNER).astype(F32)
        base = KERNEL * part
        wide = []
        for k in range(2):
            blocks = [total[base + (2 * k + j) * part : base + (2 * k + j + 1) * part] for j in range(2)]
            wide.append(jnp.concatenate(blocks, axis=1).astype(F32))
        gwi, gwo = wide
        base += 4 * part
        inner_sums = total[base : base + 3].reshape(6, part).astype(F32)
        outer_sums = total[base + 3 : base + 6].astype(F32)
    else:
        gcw, gwi, gwo, inner_sums, outer_sums = lax.psum((gcw, gwi, gwo, inner_sums, outer_sums), ("seq", "ch"))
        gcw = own_slice(gcw, part, 1)
        gwi = own_slice(gwi, part, 0)
        gwo = own_slice(gwo, part, 0)
        inner_sums = own_slice(inner_sums, part, 1)
        outer_sums = own_slice(outer_sums, share, 1)
    for r in range(chs - 1):
        gt = add_call(pre, sends[r], cotangent, gt, 2 + r)
    return (
        mixed,
        gt,
        outer_sums[0],
        outer_sums[1],
        gwi,
        inner_sums[0],
        inner_sums[1],
        inner_sums[2],
        gcw,
        inner_sums[3],
        inner_sums[4],
        inner_sums[5],
        gwo,
        outer_sums[2],
    )


def solution(mesh):
    in_specs = (
        P(None, None, "seq"),
        P(None, "seq"),
        P(None, "ch", "seq"),
        P(),
        P(),
        P("ch", None),
        P("ch"),
        P("ch"),
        P("ch"),
        P(None, "ch", None),
        P("ch"),
        P("ch"),
        P("ch"),
        P("ch", None),
        P("ch"),
    )
    out_specs = (
        P(None, "ch", "seq"),
        P(None, "ch", "seq"),
        P("ch"),
        P("ch"),
        P("ch", None),
        P("ch"),
        P("ch"),
        P("ch"),
        P(None, "ch", None),
        P("ch"),
        P("ch"),
        P("ch"),
        P("ch", None),
        P("ch"),
    )
    return jax.shard_map(body, mesh=mesh, in_specs=in_specs, out_specs=out_specs, check_vma=False)
```

```python
import functools
import math

import jax
import jax.numpy as jnp
from jax import lax
from jax.experimental import pallas as pl
from jax.experimental.pallas import tpu as pltpu
from jax.sharding import PartitionSpec as P

D = 1280
INNER = 640
KERNEL = 5
DILATION = 16
REACH = KERNEL // 2 * DILATION
EPS = 1e-05
HALF_ROOT = math.sqrt(0.5)
DENSITY = 1.0 / math.sqrt(2.0 * math.pi)
F32 = jnp.float32
BF16 = jnp.bfloat16
LANES = 128
VMEM_BYTES = 60 * 1024 * 1024


TWO = 2


def rows_of(width):
    return next(r for r in (64, 32, 16) if width % r == 0)


def straight(width, length, body, init):
    rows = next(r for r in (64, 32, 16) if width % r == 0 and r * length <= 64 * 256 or r == 16)
    for i in range(width // rows):
        init = body(pl.ds(i * rows, rows), init)
    return init


def fold_rows(v):
    return v.reshape(v.shape[0] // 8, 8, v.shape[1]).sum(0)


def fold_lanes(v):
    out = v[:, :LANES]
    for j in range(1, v.shape[1] // LANES):
        out = out + v[:, j * LANES : (j + 1) * LANES]
    return out


def spread(p, length):
    return jnp.concatenate([p] * (length // LANES), axis=1)


def loop(width, body, init):
    rows = rows_of(width)

    def step(i, carry):
        return body(pl.ds(pl.multiple_of(i * rows, rows), rows), carry)

    return lax.fori_loop(0, width // rows, step, init)


def norm_stats(load, width, length, rolled=False):
    def over(body, init):
        return loop(width, body, init) if rolled else straight(width, length, body, init)

    zero = jnp.zeros((8, length), F32)
    total = over(lambda sl, a: a + fold_rows(load(sl)), zero)
    mean = total.sum(0, keepdims=True) / width

    def square(sl, a):
        c = load(sl) - mean
        return a + fold_rows(c * c)

    total = over(square, zero)
    return mean, lax.rsqrt(total.sum(0, keepdims=True) / width + EPS)


def cdf(p):
    return 0.5 + 0.5 * lax.erf(p * HALF_ROOT)


def slope(p, phi):
    return phi + p * (DENSITY * jnp.exp(p * p * -0.5))


def call(kernel, grid, in_specs, out_specs, out_shape, scratch=(), prefetch=1, aliases=None, cost=None):
    return pl.pallas_call(
        kernel,
        grid_spec=pltpu.PrefetchScalarGridSpec(
            num_scalar_prefetch=prefetch,
            grid=grid,
            in_specs=in_specs,
            out_specs=out_specs,
            scratch_shapes=list(scratch),
        ),
        out_shape=out_shape,
        input_output_aliases=aliases or {},
        cost_estimate=cost,
        compiler_params=pltpu.CompilerParams(vmem_limit_bytes=VMEM_BYTES),
    )


def cost_of(macs, bytes_accessed):
    return pl.CostEstimate(flops=int(2 * macs), bytes_accessed=int(bytes_accessed), transcendentals=0)


def whole(shape):
    return pl.BlockSpec(shape, lambda i, pre: (0,) * len(shape), pipeline_mode=pl.Buffered(1))


def sds(shape, dtype):
    return jax.ShapeDtypeStruct(shape, dtype)


def weight_copies(own_refs, full_refs, sems):
    seq, ch = lax.axis_index("seq"), lax.axis_index("ch")
    core, row = seq % 2, (seq // 2) % 2
    send_sem, recv_sem = sems
    across, along, beside = {"ch": 1 - ch}, {"seq": seq + 2 - 4 * row}, {"seq": seq + 1 - 2 * core}

    def part(ref, at, size):
        at = pl.multiple_of(at, 16)
        return ref.at[:, pl.ds(at, size), :] if len(ref.shape) == 3 else ref.at[pl.ds(at, size), :]

    (w_in, conv, w_out), (w_in_full, conv_full, w_out_full) = own_refs, full_refs
    items = [
        (w_in, w_in_full),
        (conv.at[pl.ds(0, 2)], conv_full.at[pl.ds(0, 2)]),
        (conv.at[pl.ds(2, 3)], conv_full.at[pl.ds(2, 3)]),
        (w_out, w_out_full),
    ]
    local, first_hop, second_hop, third_hop = [], [], [], []
    for k, (own, full) in enumerate(items):
        half = own.shape[-2]
        size = half // 4

        def remote(src, dst, slot, device):
            return pltpu.make_async_remote_copy(
                src_ref=src,
                dst_ref=dst,
                send_sem=send_sem.at[k, slot],
                recv_sem=recv_sem.at[k, slot],
                device_id=device,
                device_id_type=pl.DeviceIdType.MESH,
            )

        quarter = (row * 2 + core) * size
        local.append(remote(own, part(full, ch * half, half), 4, beside))
        first_hop.append(remote(part(own, quarter, size), part(full, ch * half + quarter, size), 0, across))
        landed = (1 - ch) * half
        mine = part(full, landed + quarter, size)
        second_hop.append(remote(mine, mine, 1, along))
        both = []
        for j, r in enumerate((row, 1 - row)):
            piece = part(full, landed + (r * 2 + core) * size, size)
            both.append(remote(piece, piece, 2 + j, beside))
        third_hop.append(both)
    return local, first_hop, second_hop, third_hop


def first_kernel(comm, pre, x_ref, p_ref, *rest):
    if comm:
        own_refs, own_vec, first_ref, stat_ref = rest[:3], rest[3], rest[4], rest[5]
        full_refs, full_vec = rest[6:9], rest[9]
        exchange(own_refs, own_vec, full_refs, full_vec, rest[10:12], rest[12:])
    else:
        first_ref, stat_ref = rest
    length = x_ref.shape[2]
    mean, scale = norm_stats(lambda sl: x_ref[0, sl, :].astype(F32), D, length, True)
    stat_ref[0, 0:1, :] = mean
    stat_ref[0, 1:2, :] = scale

    def body(sl, carry):
        hat = (x_ref[0, sl, :].astype(F32) - mean) * scale
        point = hat * spread(p_ref[0, sl, :], length) + spread(p_ref[1, sl, :], length)
        first_ref[0, sl, :] = (point * cdf(point)).astype(BF16)
        return carry

    loop(D, body, 0)


def exchange(own_refs, own_vec, full_refs, full_vec, sems, vec_sems):
    step, steps = pl.program_id(0), pl.num_programs(0)
    seq, ch = lax.axis_index("seq"), lax.axis_index("ch")
    core, row = seq % 2, (seq // 2) % 2
    local, first_hop, second_hop, third_hop = weight_copies(own_refs, full_refs, sems)
    vec_local = pltpu.make_async_copy(own_vec, full_vec.at[ch], vec_sems[0])
    vec_remote = pltpu.make_async_remote_copy(
        src_ref=own_vec,
        dst_ref=full_vec.at[ch],
        send_sem=vec_sems[1],
        recv_sem=vec_sems[2],
        device_id={"ch": 1 - ch},
        device_id_type=pl.DeviceIdType.MESH,
    )

    @pl.when(step == 0)
    def _():
        barrier = pltpu.get_barrier_semaphore()
        for device in ({"ch": 1 - ch}, {"seq": seq + 2 - 4 * row}, {"seq": seq + 1 - 2 * core}):
            pl.semaphore_signal(barrier, inc=1, device_id=device, device_id_type=pl.DeviceIdType.MESH)
        pl.semaphore_wait(barrier, 3)
        vec_remote.start()
        first_hop[0].start()
        vec_local.start()
        for copy in local:
            copy.start()

    for k in range(4):

        if k > 0:

            @pl.when(step == (0, 1, 4, 7)[k])
            def _():
                first_hop[k].start()

        @pl.when(step == (4, 7, 10, 12)[k])
        def _():
            first_hop[k].wait()
            second_hop[k].start()
            third_hop[k][0].start()

        @pl.when(step == (7, 10, 14, 15)[k])
        def _():
            second_hop[k].wait()
            third_hop[k][1].start()

    @pl.when(step == steps - 1)
    def _():
        vec_remote.wait()
        vec_local.wait()
        for k in range(4):
            local[k].wait()
            third_hop[k][0].wait()
            third_hop[k][1].wait()


def first_call(pre, tokens, p1, weights, vec):
    seqs, _, length = tokens.shape
    comm = weights is not None
    any_spec = pl.BlockSpec(memory_space=pl.ANY)
    in_specs = [pl.BlockSpec((1, D, length), lambda i, pre: ((pre[0] + i) % seqs, 0, 0)), whole((2, D, LANES))]
    out_specs = [
        pl.BlockSpec((1, D, length), lambda i, pre: (i, 0, 0)),
        pl.BlockSpec((1, 2, length), lambda i, pre: (i, 0, 0)),
    ]
    shapes = [sds((seqs, D, length), BF16), sds((seqs, 2, length), F32)]
    args, scratch = [pre, tokens, p1], []
    if comm:
        in_specs += [any_spec] * 4
        out_specs += [any_spec] * 4
        shapes += [sds(w.shape[:-2] + (2 * w.shape[-2], w.shape[-1]), BF16) for w in weights]
        shapes.append(sds((2,) + vec.shape, F32))
        args += list(weights) + [vec]
        dma = pltpu.SemaphoreType.DMA
        scratch = [dma((4, 5)), dma((4, 5)), dma, dma, dma]

    def kernel(*refs):
        first_kernel(comm, *refs)

    if comm:

        def at(i):
            return ((lax.axis_index("ch") * (seqs // 2) + i) % seqs, 0, 0)

        return pl.pallas_call(
            lambda *refs: first_kernel(True, None, *refs),
            grid=(seqs,),
            in_specs=[
                pl.BlockSpec((1, D, length), at),
                pl.BlockSpec((2, D, LANES), lambda i: (0, 0, 0), pipeline_mode=pl.Buffered(1)),
            ]
            + [any_spec] * 4,
            out_specs=tuple(
                [pl.BlockSpec((1, D, length), lambda i: (i, 0, 0)), pl.BlockSpec((1, 2, length), lambda i: (i, 0, 0))]
                + [any_spec] * 4
            ),
            out_shape=tuple(shapes),
            scratch_shapes=scratch,
            cost_estimate=cost_of(seqs * D * length * 40, seqs * D * length * 4),
            compiler_params=pltpu.CompilerParams(
                vmem_limit_bytes=VMEM_BYTES, collective_id=1, has_side_effects=True
            ),
        )(*args[1:])
    return call(kernel, (seqs,), in_specs, tuple(out_specs), tuple(shapes))(*args)


def put_edges(group, ref, lead_ref, trail_ref):
    length = ref.shape[2]
    place = pl.program_id(0) % (group // TWO)
    for k in range(group // TWO):

        @pl.when(place == k)
        def _():
            for j in range(TWO):
                lanes = slice((k * TWO + j) * REACH, (k * TWO + j + 1) * REACH)
                lead_ref[0, :, lanes] = ref[j, :, :REACH]
                trail_ref[0, :, lanes] = ref[j, :, length - REACH :]


def middle_kernel(group, keep, pre, first_ref, mask_ref, w_ref, p_ref, mid_ref, lead_ref, trail_ref, *rest):
    nar_refs = rest[-TWO:]
    length = first_ref.shape[2]
    for j in range(TWO):
        nar = jnp.dot(w_ref[...], first_ref[j], preferred_element_type=F32)
        nar_refs[j][...] = nar + spread(p_ref[0], length)
    for j in range(TWO):
        nar_ref = nar_refs[j]
        mean, scale = norm_stats(lambda sl: nar_ref[sl, :], INNER, length)
        mask = mask_ref[j].astype(F32)

        def body(sl, carry):
            hat = (nar_ref[sl, :] - mean) * scale
            point = hat * spread(p_ref[1, sl, :], length) + spread(p_ref[2, sl, :], length)
            phi = cdf(point)
            mid_ref[j, sl, :] = (point * phi * mask).astype(BF16)
            if keep:
                rest[0][j, sl, :] = hat.astype(BF16)
                rest[1][j, sl, :] = slope(point, phi) * mask
            return carry

        straight(INNER, length, body, 0)
        if keep:
            rest[2][j] = scale
    put_edges(group, mid_ref, lead_ref, trail_ref)


def middle_call(pre, first, mask, w_in, p2, count, offset, group, keep):
    _, _, length = first.shape
    seqs = mask.shape[0]
    edge = pl.BlockSpec((1, INNER, group * REACH), lambda i, pre: (i // (group // TWO), 0, 0))
    edge_shape = sds((count // group, INNER, group * REACH), BF16)
    own = pl.BlockSpec((TWO, INNER, length), lambda i, pre: (i, 0, 0))
    outs = [own, edge, edge]
    shapes = [sds((count, INNER, length), BF16), edge_shape, edge_shape]
    if keep:
        outs += [own, own, pl.BlockSpec((TWO, 1, length), lambda i, pre: (i, 0, 0))]
        shapes += [
            sds((count, INNER, length), BF16),
            sds((count, INNER, length), F32),
            sds((count, 1, length), F32),
        ]
    return call(
        functools.partial(middle_kernel, group, keep),
        (count // TWO,),
        [
            pl.BlockSpec((TWO, D, length), lambda i, pre: (offset // TWO + i, 0, 0)),
            pl.BlockSpec((TWO, 1, length), lambda i, pre: (((pre[0] + offset) // TWO + i) % (seqs // TWO), 0, 0)),
            whole((INNER, D)),
            whole((3, INNER, LANES)),
        ],
        tuple(outs),
        tuple(shapes),
        scratch=[pltpu.VMEM((INNER, length), F32)] * TWO,
        cost=cost_of(count * INNER * D * length * 1.5, count * (D + INNER * 3) * length * 2),
    )(pre, first, mask.reshape(seqs, 1, length), w_in, p2)


def gather_windows(group, body_ref, before_ref, after_ref, pad_ref, cat_refs, order):
    width, length = body_ref.shape[1], body_ref.shape[2]
    place = pl.program_id(0) % (group // TWO)
    for k in range(group // TWO):

        @pl.when(place == k)
        def _():
            for j in range(TWO):
                lanes = slice((k * TWO + j) * REACH, (k * TWO + j + 1) * REACH)
                pad_ref[j, :, LANES - REACH : LANES] = before_ref[0, :, lanes]
                pad_ref[j, :, LANES + length : LANES + length + REACH] = after_ref[0, :, lanes]

    for j in range(TWO):
        pad_ref[j, :, LANES : LANES + length] = body_ref[j]
        for tap in range(KERNEL):
            start = LANES + order * (tap - KERNEL // 2) * DILATION
            cat_refs[j][tap * width : (tap + 1) * width, :] = pad_ref[j, :, start : start + length]


def last_kernel(
    group, keep, pre, mid_ref, before_ref, after_ref, x_ref, wc_ref, wo_ref, p_ref, b_ref, *rest
):
    if keep:
        mixed_ref, hat_ref, gp_ref, scale_ref, last_out = rest[:5]
        last_refs = [last_out.at[j] for j in range(TWO)]
    else:
        mixed_ref = rest[1]
        last_refs = rest[-TWO:]
        rest = rest[:-TWO]
    pad_ref, cat_refs, conv_refs = rest[-1 - 2 * TWO], rest[-2 * TWO : -TWO], rest[-TWO:]
    length = mid_ref.shape[2]
    gather_windows(group, mid_ref, before_ref, after_ref, pad_ref, cat_refs, 1)
    for j in range(TWO):
        conv = jnp.dot(wc_ref[...], cat_refs[j][...], preferred_element_type=F32)
        conv_refs[j][...] = conv + spread(p_ref[0], length)
    for j in range(TWO):
        conv_ref, last_ref = conv_refs[j], last_refs[j]
        mean, scale = norm_stats(lambda sl: conv_ref[sl, :], INNER, length)

        def body(sl, carry):
            hat = (conv_ref[sl, :] - mean) * scale
            point = hat * spread(p_ref[1, sl, :], length) + spread(p_ref[2, sl, :], length)
            phi = cdf(point)
            last_ref[sl, :] = (point * phi).astype(BF16)
            if keep:
                hat_ref[j, sl, :] = hat.astype(BF16)
                gp_ref[j, sl, :] = slope(point, phi)
            return carry

        straight(INNER, length, body, 0)
        if keep:
            scale_ref[j] = scale
        branch = jnp.dot(wo_ref[...], last_ref[...], preferred_element_type=F32)
        mixed_ref[j] = (x_ref[j].astype(F32) + branch + spread(b_ref[...], length)).astype(BF16)


def last_call(pre, mid, before, after, tokens, wc, wo_t, p2, b_out, count, offset, group, keep, mixed):
    _, _, length = mid.shape
    seqs, share = tokens.shape[0], wo_t.shape[0]
    edge = pl.BlockSpec((1, INNER, group * REACH), lambda i, pre: (i // (group // TWO), 0, 0))
    own = pl.BlockSpec((TWO, INNER, length), lambda i, pre: (i, 0, 0))

    def pair_at(i, pre):
        return ((pre[0] + offset) // TWO + i) % (seqs // TWO)

    outs = [pl.BlockSpec((TWO, share, length), lambda i, pre: (pair_at(i, pre), 0, 0))]
    shapes = [sds((seqs, share, length), BF16)]
    in_specs = [
        own,
        edge,
        edge,
        pl.BlockSpec((TWO, share, length), lambda i, pre: (pair_at(i, pre), pre[1], 0)),
        whole((INNER, KERNEL * INNER)),
        whole((share, INNER)),
        whole((3, INNER, LANES)),
        whole((share, LANES)),
    ]
    args = [pre, mid, before, after, tokens, wc, wo_t, p2, b_out]
    aliases = None
    scratch = [pltpu.VMEM((TWO, INNER, length + 2 * LANES), BF16)]
    scratch += [pltpu.VMEM((KERNEL * INNER, length), BF16)] * TWO
    scratch += [pltpu.VMEM((INNER, length), F32)] * TWO
    if keep:
        outs += [own, own, pl.BlockSpec((TWO, 1, length), lambda i, pre: (i, 0, 0)), own]
        saved = sds((count, INNER, length), BF16)
        shapes += [saved, sds((count, INNER, length), F32), sds((count, 1, length), F32), saved]
    else:
        scratch += [pltpu.VMEM((INNER, length), BF16)] * TWO
        in_specs.append(pl.BlockSpec(memory_space=pl.ANY))
        args.append(mixed)
        aliases = {len(args) - 1: 0}
    return call(
        functools.partial(last_kernel, group, keep),
        (count // TWO,),
        in_specs,
        tuple(outs),
        tuple(shapes),
        scratch=scratch,
        aliases=aliases,
        cost=cost_of(count * INNER * (KERNEL * INNER + share) * length * 1.3, count * share * 6 * length * 2),
    )(*args)


def side(ref, sl):
    return jnp.concatenate([ref[j, sl, :].astype(F32) for j in range(TWO)], axis=1)


def across(ref, row):
    return jnp.concatenate([ref[j, row : row + 1, :] for j in range(TWO)], axis=1)


def norm_back(d_ref, gp_ref, hat_ref, scale, gain_ref, gg_ref, gb_ref, sum_ref, put):
    wide = d_ref.shape[1]
    zero = jnp.zeros((8, wide), F32)

    def body(sl, carry):
        d_pre = d_ref[sl, :] * side(gp_ref, sl)
        hat = side(hat_ref, sl)
        gg_ref[sl, :] += fold_lanes(d_pre * hat)
        gb_ref[sl, :] += fold_lanes(d_pre)
        e = d_pre * spread(gain_ref[0, sl, :], wide)
        d_ref[sl, :] = e
        return carry[0] + fold_rows(e), carry[1] + fold_rows(e * hat)

    total, dot = straight(INNER, wide, body, (zero, zero))
    total = total.sum(0, keepdims=True) * (scale / INNER)
    dot = dot.sum(0, keepdims=True) * (scale / INNER)

    def finish(sl, carry):
        v = (d_ref[sl, :] * scale - total - side(hat_ref, sl) * dot).astype(BF16)
        put(sl, v)
        sum_ref[sl, :] += fold_lanes(v.astype(F32))
        return carry

    straight(INNER, wide, finish, 0)


def rear_kernel(group, chs, pre, *refs):
    dy_refs = refs[:chs]
    w_ref, hat_ref, gp_ref, last_ref, scale_ref, p_ref = refs[chs : chs + 6]
    dconv_ref, lead_ref, trail_ref, gg_ref, gb_ref, gc_ref, gw_ref, go_ref = refs[chs + 6 : chs + 14]
    dy_ref, d_ref = refs[chs + 14 :]
    share, length = dy_refs[0].shape[1], dy_refs[0].shape[2]

    @pl.when(pl.program_id(0) == 0)
    def _():
        for ref in (gg_ref, gb_ref, gc_ref, gw_ref, go_ref):
            ref[...] = jnp.zeros_like(ref)

    for r in range(chs):
        at = pl.multiple_of(((pre[1] + chs - r) % chs) * share, share)
        for j in range(TWO):
            dy_ref[pl.ds(at, share), j * length : (j + 1) * length] = dy_refs[r][j]
    d_ref[...] = jnp.dot(w_ref[...], dy_ref[...], preferred_element_type=F32)
    last = jnp.concatenate([last_ref[j] for j in range(TWO)], axis=1)
    gw_ref[...] += lax.dot_general(last, dy_ref[...], (((1,), (1,)), ((), ())), preferred_element_type=F32)
    go_ref[...] += fold_lanes(dy_ref[...].astype(F32))

    def put(sl, v):
        for j in range(TWO):
            dconv_ref[j, sl, :] = v[:, j * length : (j + 1) * length]

    norm_back(d_ref, gp_ref, hat_ref, across(scale_ref, 0), p_ref, gg_ref, gb_ref, gc_ref, put)
    put_edges(group, dconv_ref, lead_ref, trail_ref)


def const(shape):
    return pl.BlockSpec(shape, lambda i, pre: (0,) * len(shape), pipeline_mode=pl.Buffered(1))


def rear_call(pre, cot, others, w_out, hat, gp, last, scale, p2, group):
    seqs, share, length = cot.shape
    count = hat.shape[0]
    chs = 1 + len(others)
    edge = pl.BlockSpec((1, INNER, group * REACH), lambda i, pre: (i // (group // TWO), 0, 0))
    edge_shape = sds((count // group, INNER, group * REACH), BF16)
    own = pl.BlockSpec((TWO, INNER, length), lambda i, pre: (i, 0, 0))
    sums = [(INNER, LANES)] * 3 + [(INNER, D), (D, LANES)]
    return call(
        functools.partial(rear_kernel, group, chs),
        (count // TWO,),
        [pl.BlockSpec((TWO, share, length), lambda i, pre: (pre[0] // TWO + i, 0, 0))]
        + [pl.BlockSpec((TWO, share, length), lambda i, pre: (i, 0, 0))] * (chs - 1)
        + [
            whole((INNER, D)),
            own,
            own,
            own,
            pl.BlockSpec((TWO, 1, length), lambda i, pre: (i, 0, 0)),
            whole((1, INNER, LANES)),
        ],
        tuple([own, edge, edge] + [const(v) for v in sums]),
        tuple([sds((count, INNER, length), BF16), edge_shape, edge_shape] + [sds(v, F32) for v in sums]),
        scratch=[pltpu.VMEM((D, TWO * length), BF16), pltpu.VMEM((INNER, TWO * length), F32)],
        cost=cost_of(count * INNER * D * length * 2.5, count * INNER * 5 * length * 2),
    )(pre, cot, *others, w_out, hat, gp, last, scale, p2)


def front_kernel(group, chs, pre, *refs):
    dconv_ref, before_ref, after_ref, mid_ref, hat_ref, gp_ref, scale_ref = refs[:7]
    x_ref, stat_ref, dy_ref, wc_ref, wi_ref, p2_ref, p1_ref = refs[7:14]
    refs = refs[14:]
    gt_ref = refs[0]
    send_refs = refs[1:chs]
    gcw_ref, gwi_ref, gg2_ref, gb2_ref, gbi_ref, gg1_ref, gb1_ref = refs[chs : chs + 7]
    pad_ref, cat_ref, d_ref, dn_ref, df_ref, first_ref = refs[chs + 7 :]
    share, length = dy_ref.shape[1], dy_ref.shape[2]
    wide = TWO * length

    @pl.when(pl.program_id(0) == 0)
    def _():
        for ref in (gcw_ref, gwi_ref, gg2_ref, gb2_ref, gbi_ref, gg1_ref, gb1_ref):
            ref[...] = jnp.zeros_like(ref)

    cats = [cat_ref.at[:, j * length : (j + 1) * length] for j in range(TWO)]
    gather_windows(group, dconv_ref, before_ref, after_ref, pad_ref, cats, -1)
    d_ref[...] = jnp.dot(wc_ref[...], cat_ref[...], preferred_element_type=F32)
    mid = jnp.concatenate([mid_ref[j] for j in range(TWO)], axis=1)
    gcw_ref[...] += lax.dot_general(cat_ref[...], mid, (((1,), (1,)), ((), ())), preferred_element_type=F32)

    def put(sl, v):
        dn_ref[sl, :] = v

    norm_back(d_ref, gp_ref, hat_ref, across(scale_ref, 0), p2_ref, gg2_ref, gb2_ref, gbi_ref, put)
    df_ref[...] = jnp.dot(wi_ref[...], dn_ref[...], preferred_element_type=F32)
    mean_in, scale_in = across(stat_ref, 0), across(stat_ref, 1)
    zero = jnp.zeros((8, wide), F32)

    def inner(sl, carry):
        hat = (side(x_ref, sl) - mean_in) * scale_in
        gain = spread(p1_ref[0, sl, :], wide)
        point = hat * gain + spread(p1_ref[1, sl, :], wide)
        phi = cdf(point)
        first_ref[sl, :] = (point * phi).astype(BF16)
        d_pre = df_ref[sl, :] * slope(point, phi)
        gg1_ref[sl, :] += fold_lanes(d_pre * hat)
        gb1_ref[sl, :] += fold_lanes(d_pre)
        e = d_pre * gain
        df_ref[sl, :] = e
        return carry[0] + fold_rows(e), carry[1] + fold_rows(e * hat)

    total, dot = straight(D, wide, inner, (zero, zero))
    total = total.sum(0, keepdims=True) * (scale_in / D)
    dot = dot.sum(0, keepdims=True) * (scale_in / D)
    gwi_ref[...] += lax.dot_general(
        dn_ref[...], first_ref[...], (((1,), (1,)), ((), ())), preferred_element_type=F32
    )
    for r in range(chs):
        base = ((pre[1] + r) % chs) * share

        def out(to, carry):
            rows = pl.ds(pl.multiple_of(base + to.start, 16), to.size)
            hat = (side(x_ref, rows) - mean_in) * scale_in
            v = df_ref[rows, :] * scale_in - total - hat * dot
            for j in range(TWO):
                half = v[:, j * length : (j + 1) * length]
                if r == 0:
                    gt_ref[j, to, :] = half + dy_ref[j, to, :].astype(F32)
                else:
                    send_refs[r - 1][j, to, :] = half.astype(BF16)
            return carry

        straight(share, wide, out, 0)


def front_call(pre, dconv, before, after, mid, hat, gp, scale, tokens, stat, cot, wc_t, wi_t, p2, p1, chs, group):
    seqs, share, length = cot.shape
    count = dconv.shape[0]
    edge = pl.BlockSpec((1, INNER, group * REACH), lambda i, pre: (i // (group // TWO), 0, 0))
    own = pl.BlockSpec((TWO, INNER, length), lambda i, pre: (i, 0, 0))

    def seq_block(rows):
        return pl.BlockSpec((TWO, rows, length), lambda i, pre: (pre[0] // TWO + i, 0, 0))

    inner_part, outer_part = (INNER, LANES), (D, LANES)
    sums = [(KERNEL * INNER, INNER), (INNER, D), inner_part, inner_part, inner_part, outer_part, outer_part]
    wide = TWO * length
    return call(
        functools.partial(front_kernel, group, chs),
        (count // TWO,),
        [
            own,
            edge,
            edge,
            own,
            own,
            own,
            pl.BlockSpec((TWO, 1, length), lambda i, pre: (i, 0, 0)),
            seq_block(D),
            pl.BlockSpec((TWO, 2, length), lambda i, pre: (i, 0, 0)),
            seq_block(share),
            whole((INNER, KERNEL * INNER)),
            whole((D, INNER)),
            whole((1, INNER, LANES)),
            whole((2, D, LANES)),
        ],
        tuple(
            [seq_block(share)]
            + [pl.BlockSpec((TWO, share, length), lambda i, pre: (i, 0, 0))] * (chs - 1)
            + [const(v) for v in sums]
        ),
        tuple(
            [sds((seqs, share, length), F32)]
            + [sds((count, share, length), BF16)] * (chs - 1)
            + [sds(v, F32) for v in sums]
        ),
        scratch=[
            pltpu.VMEM((TWO, INNER, length + 2 * LANES), BF16),
            pltpu.VMEM((KERNEL * INNER, wide), BF16),
            pltpu.VMEM((INNER, wide), F32),
            pltpu.VMEM((INNER, wide), BF16),
            pltpu.VMEM((D, wide), F32),
            pltpu.VMEM((D, wide), BF16),
        ],
        cost=cost_of(count * INNER * (2 * KERNEL * INNER + 2 * D) * length * 1.3, count * D * 8 * length * 2),
    )(pre, dconv, before, after, mid, hat, gp, scale, tokens, stat, cot, wc_t, wi_t, p2, p1)


def add_kernel(pre, part_ref, dy_ref, _, gt_ref):
    gt_ref[...] = part_ref[...].astype(F32) + dy_ref[...].astype(F32)


def add_call(pre, part, cot, gt, start):
    seqs, share, length = cot.shape
    count = part.shape[0]
    at = lambda i, pre: (pre[start] + i, 0, 0)
    return call(
        add_kernel,
        (count,),
        [
            pl.BlockSpec((1, share, length), lambda i, pre: (i, 0, 0)),
            pl.BlockSpec((1, share, length), at),
            pl.BlockSpec(memory_space=pl.ANY),
        ],
        pl.BlockSpec((1, share, length), at),
        sds((seqs, share, length), F32),
        aliases={3: 0},
        cost=cost_of(count * share * length, count * share * length * 8),
    )(pre, part, cot, gt)


def turn_kernel(pre, w_ref, flat_ref, turned_ref):
    unit = (
        lax.broadcasted_iota(jnp.int32, (INNER, INNER), 0) == lax.broadcasted_iota(jnp.int32, (INNER, INNER), 1)
    ).astype(F32).astype(BF16)
    flat_ref[...] = w_ref[0]
    turned_ref[...] = lax.dot_general(
        unit, w_ref[0], (((1,), (1,)), ((), ())), preferred_element_type=F32
    ).astype(BF16)


def turn_call(pre, conv):
    block = pl.BlockSpec((INNER, INNER), lambda k, pre: (0, k))
    shape = sds((INNER, KERNEL * INNER), BF16)
    return call(
        turn_kernel,
        (KERNEL,),
        [pl.BlockSpec((1, INNER, INNER), lambda k, pre: (k, 0, 0))],
        (block, block),
        (shape, shape),
        cost=cost_of(KERNEL * INNER**3, KERNEL * INNER * INNER * 6),
    )(pre, conv)


def reduce_ticks(stages, starts, half_rows, refs):
    gcw_ref, gwi_ref, gwo_ref, small_ref, out_ref = refs[:5]
    acc, send, recv, swap, res, load_sem, send_sem, recv_sem = refs[5:]
    seq, ch = lax.axis_index("seq"), lax.axis_index("ch")
    streams, levels = len(stages), len(stages[0])
    rows = acc.shape[1] // streams
    size = [rows >> (t + 1) for t in range(levels)]
    at = [rows - (rows >> t) for t in range(levels)]

    def bit(b):
        return (seq // (1 << b)) % 2

    def partner(b):
        return {"seq": seq + (1 - 2 * bit(b)) * (1 << b)}

    low = []
    for q in range(streams):
        place = [q * rows]
        for t in range(levels):
            place.append(place[-1] + bit(stages[q][t]) * size[t])
        low.append(place)

    def loads():
        out = []
        for h in range(2):
            mine = pl.ds(h * half_rows, half_rows)
            pieces = [gcw_ref.at[k, mine, :] for k in range(KERNEL)]
            for ref in (gwi_ref, gwo_ref):
                pieces += [ref.at[mine, pl.ds(j * INNER, INNER)] for j in range(D // INNER)]
            for j, piece in enumerate(pieces):
                out.append((piece, acc.at[h, pl.ds(j * half_rows, half_rows), :]))
            used = len(pieces) * half_rows
            out.append((small_ref.at[h], acc.at[h, pl.ds(used, small_ref.shape[1]), :]))
        return [pltpu.make_async_copy(a, b, load_sem.at[j]) for j, (a, b) in enumerate(out)]

    def begin():
        used = half_rows * (KERNEL + 2 * D // INNER) + small_ref.shape[1]
        for h in range(2):
            acc[h, used:, :] = jnp.zeros((acc.shape[1] - used, INNER), F32)
        for copy in loads():
            copy.start()
        barrier = pltpu.get_barrier_semaphore()
        for device in [partner(b) for b in sorted(stages[0])] + [{"ch": 1 - ch}]:
            pl.semaphore_signal(barrier, inc=1, device_id=device, device_id_type=pl.DeviceIdType.MESH)
        pl.semaphore_wait(barrier, levels + 1)

    def remote(src, dst, q, k, device):
        slot = q * (2 * levels + 1) + k
        return pltpu.make_async_remote_copy(
            src_ref=src,
            dst_ref=dst,
            send_sem=send_sem.at[slot],
            recv_sem=recv_sem.at[slot],
            device_id=device,
            device_id_type=pl.DeviceIdType.MESH,
        )

    def sliced(count, body):
        step = next(r for r in (96, 48, 32, 16) if count % r == 0)

        def one(i, carry):
            body(pl.multiple_of(i * step, 16), step)
            return carry

        lax.fori_loop(0, count // step, one, 0)

    def spot(base, i, step):
        return pl.ds(pl.multiple_of(base + i, 16), step)

    def copy_of(q, k):
        if k < levels:
            window = pl.ds(at[k], size[k])
            return remote(send.at[q, :, window, :], recv.at[q, :, window, :], q, k, partner(stages[q][k]))
        if k == levels:
            return remote(swap.at[0, q], swap.at[1, q], q, k, {"ch": 1 - ch})
        t = 2 * levels - k
        place = pl.ds(pl.multiple_of(low[q][t + 1], 16), size[t])
        return remote(res.at[place, :], res.at[place, :], q, k, partner(stages[q][t]))

    def start(q, k):
        if k < levels:
            away = low[q][k] + (1 - bit(stages[q][k])) * size[k]
            for h in range(2):

                def pack(i, step, h=h):
                    send[q, h, spot(at[k], i, step), :] = acc[h, spot(away, i, step), :].astype(BF16)

                sliced(size[k], pack)
        elif k == levels:
            place = spot(low[q][levels], 0, size[-1])
            swap[0, q] = acc[1 - ch, place, :].astype(BF16)
        copy_of(q, k).start()

    def finish(q, k):
        copy_of(q, k).wait()
        if k < levels:
            for h in range(2):

                def add(i, step, h=h):
                    place = spot(low[q][k + 1], i, step)
                    acc[h, place, :] += recv[q, h, spot(at[k], i, step), :].astype(F32)

                sliced(size[k], add)
        elif k == levels:
            place = spot(low[q][levels], 0, size[-1])
            res[place, :] = (acc[ch, place, :] + swap[1, q].astype(F32)).astype(BF16)

    def tick(now):
        if now == 0:
            for copy in loads():
                copy.wait()
        for q in range(streams):
            k = now - starts[q]
            if 1 <= k <= 2 * levels + 1:
                finish(q, k - 1)
            if 0 <= k <= 2 * levels:
                start(q, k)

    def end():
        done = pltpu.make_async_copy(res, out_ref, load_sem.at[0])
        done.start()
        done.wait()

    return (
        [begin]
        + [functools.partial(tick, now) for now in range(max(starts) + 2 * levels + 2)]
        + [end]
    )


def reduce_plan(small, seq_count):
    half_rows = INNER // 2
    levels = seq_count.bit_length() - 1
    order = list(range(levels))
    one, two = tuple(order), tuple(order[:1] + order[2:] + order[1:2])
    stages, starts = streams_of(one, two)
    streams = len(stages)
    used = half_rows * (KERNEL + 2 * D // INNER) + small.shape[1]
    unit = streams * seq_count * 16
    rows = -(-used // unit) * unit
    each = rows // streams
    slots = streams * (2 * levels + 1)
    dma = pltpu.SemaphoreType.DMA
    scratch = [
        pltpu.VMEM((2, rows, INNER), F32),
        pltpu.VMEM((streams, 2, each - each // seq_count, INNER), BF16),
        pltpu.VMEM((streams, 2, each - each // seq_count, INNER), BF16),
        pltpu.VMEM((2, streams, each // seq_count, INNER), BF16),
        pltpu.VMEM((rows, INNER), BF16),
        dma((2 * (KERNEL + 2 * D // INNER + 1),)),
        dma((slots,)),
        dma((slots,)),
    ]
    return stages, starts, half_rows, rows, scratch


def streams_of(one, two):
    return (one, one, two, one), (0, 1, 0, 2)


def tail_kernel(plan, group, mid_ref, before_ref, after_ref, x_ref, wc_ref, wo_ref, p_ref, b_ref, *rest):
    mixed_in, sums, mixed_ref, total_ref = rest[0], rest[1:5], rest[5], rest[6]
    ticks = reduce_ticks(*plan, (*sums, total_ref, *rest[7:15]))
    step = pl.program_id(0)
    last = 3
    for i in range(last + 1):

        @pl.when(step == i)
        def _():
            ticks[i]()

    last_kernel(
        group, False, None, mid_ref, before_ref, after_ref, x_ref, wc_ref, wo_ref, p_ref, b_ref,
        mixed_in, mixed_ref, *rest[15:],
    )

    @pl.when(step == last)
    def _():
        for tick in ticks[last + 1 :]:
            tick()


def tail_call(mid, before, after, tokens, wc, wo_t, p2, b_out, mixed, sums, group):
    count, _, length = mid.shape
    seqs, share = tokens.shape[0], wo_t.shape[0]
    stages, starts, half_rows, rows, scratch = reduce_plan(sums[3], lax.axis_size("seq"))
    any_spec = pl.BlockSpec(memory_space=pl.ANY)

    def pair_at(i):
        return ((lax.axis_index("ch") + 1) * (seqs // 2 // TWO) + i) % (seqs // TWO)

    def fixed(shape):
        return pl.BlockSpec(shape, lambda i: (0,) * len(shape), pipeline_mode=pl.Buffered(1))

    edge = pl.BlockSpec((1, INNER, group * REACH), lambda i: (i // (group // TWO), 0, 0))
    return pl.pallas_call(
        functools.partial(tail_kernel, (stages, starts, half_rows), group),
        grid=(count // TWO,),
        in_specs=[
            pl.BlockSpec((TWO, INNER, length), lambda i: (i, 0, 0)),
            edge,
            edge,
            pl.BlockSpec((TWO, share, length), lambda i: (pair_at(i), lax.axis_index("ch"), 0)),
            fixed((INNER, KERNEL * INNER)),
            fixed((share, INNER)),
            fixed((3, INNER, LANES)),
            fixed((share, LANES)),
        ]
        + [any_spec] * 5,
        out_specs=(pl.BlockSpec((TWO, share, length), lambda i: (pair_at(i), 0, 0)), any_spec),
        out_shape=(sds((seqs, share, length), BF16), sds((rows, INNER), BF16)),
        scratch_shapes=scratch
        + [pltpu.VMEM((TWO, INNER, length + 2 * LANES), BF16)]
        + [pltpu.VMEM((KERNEL * INNER, length), BF16)] * TWO
        + [pltpu.VMEM((INNER, length), F32)] * TWO
        + [pltpu.VMEM((INNER, length), BF16)] * TWO,
        input_output_aliases={8: 0},
        cost_estimate=cost_of(count * INNER * (KERNEL * INNER + share) * length * 4, rows * INNER * 12),
        compiler_params=pltpu.CompilerParams(vmem_limit_bytes=VMEM_BYTES, collective_id=2, has_side_effects=True),
    )(mid, before, after, tokens, wc, wo_t, p2, b_out, mixed, *sums)


def reduce_kernel(plan, *refs):
    for tick in reduce_ticks(*plan, refs):
        tick()


def reduce_call(sums, seq_count):
    stages, starts, half_rows, rows, scratch = reduce_plan(sums[3], seq_count)
    any_spec = pl.BlockSpec(memory_space=pl.ANY)
    return pl.pallas_call(
        functools.partial(reduce_kernel, (stages, starts, half_rows)),
        in_specs=[any_spec] * 4,
        out_specs=any_spec,
        out_shape=sds((rows, INNER), BF16),
        scratch_shapes=scratch,
        compiler_params=pltpu.CompilerParams(vmem_limit_bytes=VMEM_BYTES, collective_id=2, has_side_effects=True),
    )(*sums)


def rotate(value, axis, count, by):
    return lax.ppermute(value, axis, [(i, (i + by) % count) for i in range(count)])


def shift(value, by):
    count = lax.axis_size("seq")
    pairs = [(i, i + by) for i in range(count) if 0 <= i + by < count]
    return lax.ppermute(value, "seq", pairs)


def rims(lead, trail):
    return shift(trail, 1), shift(lead, -1)


def own_slice(value, width, dim):
    return lax.dynamic_slice_in_dim(value, lax.axis_index("ch") * width, width, dim)


def lane_copies(vectors):
    return jnp.broadcast_to(vectors[..., None], vectors.shape + (LANES,))


def body(
    tokens,
    pad_mask,
    cotangent,
    ln1_gain,
    first_norm_bias,
    w_in,
    b_in,
    ln2_gain,
    ln2_bias,
    conv_w,
    conv_b,
    ln3_gain,
    ln3_bias,
    w_out,
    b_out,
):
    chs = lax.axis_size("ch")
    ch = lax.axis_index("ch")
    seqs, _, length = tokens.shape
    share = b_out.shape[0]
    part = b_in.shape[0]
    n = seqs // chs
    group = min(4, n)
    starts = [((ch + chs - r) % chs) * n for r in range(1, chs)]
    pre = jnp.stack([ch * n, ch] + starts).astype(jnp.int32)
    pair = chs == 2

    p1 = lane_copies(jnp.stack([ln1_gain, first_norm_bias]))
    bo = lane_copies(b_out)
    vec = jnp.stack([b_in, ln2_gain, ln2_bias, conv_b, ln3_gain, ln3_bias, b_in, b_in])
    if pair:
        first, stat, w_in_full, conv_full, w_out_full, vec_full = first_call(
            pre, tokens, p1, (w_in, conv_w, w_out), vec
        )
        inner = vec_full.transpose(1, 0, 2).reshape(8, INNER)[:6]
    else:
        first, stat = first_call(pre, tokens, p1, None, None)
        w_in_full = lax.all_gather(w_in, "ch", axis=0, tiled=True)
        conv_full = lax.all_gather(conv_w, "ch", axis=1, tiled=True)
        w_out_full = lax.all_gather(w_out, "ch", axis=0, tiled=True)
        inner = lax.all_gather(vec, "ch", axis=1, tiled=True)[:6]

    others = []
    for r in range(1, chs):
        block = lax.dynamic_slice_in_dim(cotangent, ((ch + r) % chs) * n, n, 0)
        block, _ = lax.optimization_barrier((block, stat))
        others.append(rotate(block, "ch", chs, r))
    p2 = lane_copies(inner)
    wc, wc_t = turn_call(pre, conv_full)
    wi_t = w_in_full.T
    wo_t = lax.dynamic_slice_in_dim(w_out_full, ch * share, share, 1).T

    mid_own, lead, trail, hat_mid, gp_mid, scale_mid = middle_call(
        pre, first, pad_mask, w_in_full, p2[0:3], n, 0, group, True
    )
    before, after = rims(lead, trail)
    mid_oth, lead, trail = middle_call(pre, first, pad_mask, w_in_full, p2[0:3], seqs - n, n, group, False)
    before_oth, after_oth = rims(lead, trail)
    mixed, hat_out, gp_out, scale_out, last_own = last_call(
        pre, mid_own, before, after, tokens, wc, wo_t, p2[3:6], bo, n, 0, group, True, None
    )
    dconv, lead, trail, gg3, gb3, gcb, gwo, gbo = rear_call(
        pre, cotangent, others, w_out_full, hat_out, gp_out, last_own, scale_out, p2[4:5], group
    )
    lead, trail = rims(lead, trail)
    gt, *rest = front_call(
        pre, dconv, lead, trail, mid_own, hat_mid, gp_mid, scale_mid, tokens, stat, cotangent,
        wc_t, wi_t, p2[1:2], p1, chs, group,
    )
    sends = [rotate(v, "ch", chs, r + 1) for r, v in enumerate(rest[: chs - 1])]
    gcw, gwi, gg2, gb2, gbi, gg1, gb1 = rest[chs - 1 :]
    gcw = gcw.reshape(KERNEL, INNER, INNER)
    inner_sums = jnp.stack([v.sum(1) for v in (gbi, gg2, gb2, gcb, gg3, gb3)])
    outer_sums = jnp.stack([v.sum(1) for v in (gg1, gb1, gbo)])

    if pair:
        small = jnp.concatenate(
            [
                inner_sums.reshape(6, 2, part).transpose(1, 0, 2).reshape(2, 3, INNER),
                outer_sums.reshape(3, 2, share).transpose(1, 0, 2),
                jnp.zeros((2, 10, INNER), F32),
            ],
            axis=1,
        )
        mixed, total = tail_call(
            mid_oth, before_oth, after_oth, tokens, wc, wo_t, p2[3:6], bo, mixed, (gcw, gwi, gwo, small), group
        )
        gcw = total[: KERNEL * part].reshape(KERNEL, part, INNER).astype(F32)
        base = KERNEL * part
        wide = []
        for k in range(2):
            blocks = [total[base + (2 * k + j) * part : base + (2 * k + j + 1) * part] for j in range(2)]
            wide.append(jnp.concatenate(blocks, axis=1).astype(F32))
        gwi, gwo = wide
        base += 4 * part
        inner_sums = total[base : base + 3].reshape(6, part).astype(F32)
        outer_sums = total[base + 3 : base + 6].astype(F32)
    else:
        mixed, = last_call(
            pre, mid_oth, before_oth, after_oth, tokens, wc, wo_t, p2[3:6], bo, seqs - n, n, group, False, mixed
        )
        gcw, gwi, gwo, inner_sums, outer_sums = lax.psum((gcw, gwi, gwo, inner_sums, outer_sums), ("seq", "ch"))
        gcw = own_slice(gcw, part, 1)
        gwi = own_slice(gwi, part, 0)
        gwo = own_slice(gwo, part, 0)
        inner_sums = own_slice(inner_sums, part, 1)
        outer_sums = own_slice(outer_sums, share, 1)
    for r in range(chs - 1):
        gt = add_call(pre, sends[r], cotangent, gt, 2 + r)
    return (
        mixed,
        gt,
        outer_sums[0],
        outer_sums[1],
        gwi,
        inner_sums[0],
        inner_sums[1],
        inner_sums[2],
        gcw,
        inner_sums[3],
        inner_sums[4],
        inner_sums[5],
        gwo,
        outer_sums[2],
    )


def solution(mesh):
    in_specs = (
        P(None, None, "seq"),
        P(None, "seq"),
        P(None, "ch", "seq"),
        P(),
        P(),
        P("ch", None),
        P("ch"),
        P("ch"),
        P("ch"),
        P(None, "ch", None),
        P("ch"),
        P("ch"),
        P("ch"),
        P("ch", None),
        P("ch"),
    )
    out_specs = (
        P(None, "ch", "seq"),
        P(None, "ch", "seq"),
        P("ch"),
        P("ch"),
        P("ch", None),
        P("ch"),
        P("ch"),
        P("ch"),
        P(None, "ch", None),
        P("ch"),
        P("ch"),
        P("ch"),
        P("ch", None),
        P("ch"),
    )
    return jax.shard_map(body, mesh=mesh, in_specs=in_specs, out_specs=out_specs, check_vma=False)
```

```python
import functools
import math

import jax
import jax.numpy as jnp
from jax import lax
from jax.experimental import pallas as pl
from jax.experimental.pallas import tpu as pltpu
from jax.sharding import PartitionSpec as P

D = 1280
INNER = 640
KERNEL = 5
DILATION = 16
REACH = KERNEL // 2 * DILATION
EPS = 1e-05
HALF_ROOT = math.sqrt(0.5)
DENSITY = 1.0 / math.sqrt(2.0 * math.pi)
F32 = jnp.float32
BF16 = jnp.bfloat16
LANES = 128
VMEM_BYTES = 60 * 1024 * 1024


TWO = 2


def rows_of(width):
    return next(r for r in (64, 32, 16) if width % r == 0)


def straight(width, length, body, init):
    rows = next(r for r in (64, 32, 16) if width % r == 0 and r * length <= 64 * 256 or r == 16)
    for i in range(width // rows):
        init = body(pl.ds(i * rows, rows), init)
    return init


def fold_rows(v):
    return v.reshape(v.shape[0] // 8, 8, v.shape[1]).sum(0)


def fold_lanes(v):
    out = v[:, :LANES]
    for j in range(1, v.shape[1] // LANES):
        out = out + v[:, j * LANES : (j + 1) * LANES]
    return out


def spread(p, length):
    return jnp.concatenate([p] * (length // LANES), axis=1)


def loop(width, body, init):
    rows = rows_of(width)

    def step(i, carry):
        return body(pl.ds(pl.multiple_of(i * rows, rows), rows), carry)

    return lax.fori_loop(0, width // rows, step, init)


def norm_stats(load, width, length, rolled=False):
    def over(body, init):
        return loop(width, body, init) if rolled else straight(width, length, body, init)

    zero = jnp.zeros((8, length), F32)
    total = over(lambda sl, a: a + fold_rows(load(sl)), zero)
    mean = total.sum(0, keepdims=True) / width

    def square(sl, a):
        c = load(sl) - mean
        return a + fold_rows(c * c)

    total = over(square, zero)
    return mean, lax.rsqrt(total.sum(0, keepdims=True) / width + EPS)


def cdf(p):
    return 0.5 + 0.5 * lax.erf(p * HALF_ROOT)


def slope(p, phi):
    return phi + p * (DENSITY * jnp.exp(p * p * -0.5))


def call(kernel, grid, in_specs, out_specs, out_shape, scratch=(), prefetch=1, aliases=None, cost=None):
    return pl.pallas_call(
        kernel,
        grid_spec=pltpu.PrefetchScalarGridSpec(
            num_scalar_prefetch=prefetch,
            grid=grid,
            in_specs=in_specs,
            out_specs=out_specs,
            scratch_shapes=list(scratch),
        ),
        out_shape=out_shape,
        input_output_aliases=aliases or {},
        cost_estimate=cost,
        compiler_params=pltpu.CompilerParams(vmem_limit_bytes=VMEM_BYTES),
    )


def cost_of(macs, bytes_accessed):
    return pl.CostEstimate(flops=int(2 * macs), bytes_accessed=int(bytes_accessed), transcendentals=0)


def whole(shape, at=0):
    return pl.BlockSpec(shape, lambda i, pre: (at,) + (0,) * (len(shape) - 1), pipeline_mode=pl.Buffered(1))


def sds(shape, dtype):
    return jax.ShapeDtypeStruct(shape, dtype)


def weight_copies(own_refs, full_refs, sems):
    seq, ch = lax.axis_index("seq"), lax.axis_index("ch")
    core, row = seq % 2, (seq // 2) % 2
    send_sem, recv_sem = sems
    across, along, beside = {"ch": 1 - ch}, {"seq": seq + 2 - 4 * row}, {"seq": seq + 1 - 2 * core}

    def part(ref, at, size):
        at = pl.multiple_of(at, 16)
        return ref.at[:, pl.ds(at, size), :] if len(ref.shape) == 3 else ref.at[pl.ds(at, size), :]

    (w_in, conv, w_out), (w_in_full, conv_full, w_out_full) = own_refs, full_refs
    items = [
        (w_in, w_in_full),
        (conv.at[pl.ds(0, 2)], conv_full.at[pl.ds(0, 2)]),
        (conv.at[pl.ds(2, 3)], conv_full.at[pl.ds(2, 3)]),
        (w_out, w_out_full),
    ]
    local, first_hop, second_hop, third_hop = [], [], [], []
    for k, (own, full) in enumerate(items):
        half = own.shape[-2]
        size = half // 4

        def remote(src, dst, slot, device):
            return pltpu.make_async_remote_copy(
                src_ref=src,
                dst_ref=dst,
                send_sem=send_sem.at[k, slot],
                recv_sem=recv_sem.at[k, slot],
                device_id=device,
                device_id_type=pl.DeviceIdType.MESH,
            )

        quarter = (row * 2 + core) * size
        local.append(remote(own, part(full, ch * half, half), 4, beside))
        first_hop.append(remote(part(own, quarter, size), part(full, ch * half + quarter, size), 0, across))
        landed = (1 - ch) * half
        mine = part(full, landed + quarter, size)
        second_hop.append(remote(mine, mine, 1, along))
        both = []
        for j, r in enumerate((row, 1 - row)):
            piece = part(full, landed + (r * 2 + core) * size, size)
            both.append(remote(piece, piece, 2 + j, beside))
        third_hop.append(both)
    return local, first_hop, second_hop, third_hop


def first_kernel(comm, pre, x_ref, p_ref, *rest):
    if comm:
        own_refs, own_vec, cot_ref, first_ref, stat_ref = rest[:3], rest[3], rest[4], rest[5], rest[6]
        full_refs, full_vec, away_ref = rest[7:10], rest[10], rest[11]
        exchange(own_refs, own_vec, full_refs, full_vec, rest[12:14], rest[14:])

        @pl.when(pl.program_id(0) < pl.num_programs(0) // 2)
        def _():
            away_ref[...] = cot_ref[...]

    else:
        first_ref, stat_ref = rest
    length = x_ref.shape[2]
    mean, scale = norm_stats(lambda sl: x_ref[0, sl, :].astype(F32), D, length, True)
    stat_ref[0, 0:1, :] = mean
    stat_ref[0, 1:2, :] = scale

    def body(sl, carry):
        hat = (x_ref[0, sl, :].astype(F32) - mean) * scale
        point = hat * spread(p_ref[0, sl, :], length) + spread(p_ref[1, sl, :], length)
        first_ref[0, sl, :] = (point * cdf(point)).astype(BF16)
        return carry

    loop(D, body, 0)


def exchange(own_refs, own_vec, full_refs, full_vec, sems, vec_sems):
    step, steps = pl.program_id(0), pl.num_programs(0)
    seq, ch = lax.axis_index("seq"), lax.axis_index("ch")
    core, row = seq % 2, (seq // 2) % 2
    local, first_hop, second_hop, third_hop = weight_copies(own_refs, full_refs, sems)
    vec_local = pltpu.make_async_copy(own_vec, full_vec.at[ch], vec_sems[0])
    vec_remote = pltpu.make_async_remote_copy(
        src_ref=own_vec,
        dst_ref=full_vec.at[ch],
        send_sem=vec_sems[1],
        recv_sem=vec_sems[2],
        device_id={"ch": 1 - ch},
        device_id_type=pl.DeviceIdType.MESH,
    )

    @pl.when(step == 0)
    def _():
        barrier = pltpu.get_barrier_semaphore()
        for device in ({"ch": 1 - ch}, {"seq": seq + 2 - 4 * row}, {"seq": seq + 1 - 2 * core}):
            pl.semaphore_signal(barrier, inc=1, device_id=device, device_id_type=pl.DeviceIdType.MESH)
        pl.semaphore_wait(barrier, 3)
        vec_remote.start()
        first_hop[0].start()
        vec_local.start()
        for copy in local:
            copy.start()

    for k in range(4):

        if k > 0:

            @pl.when(step == (0, 1, 4, 7)[k])
            def _():
                first_hop[k].start()

        @pl.when(step == (4, 7, 10, 12)[k])
        def _():
            first_hop[k].wait()
            second_hop[k].start()
            third_hop[k][0].start()

        @pl.when(step == (7, 10, 14, 15)[k])
        def _():
            second_hop[k].wait()
            third_hop[k][1].start()

    @pl.when(step == steps - 1)
    def _():
        vec_remote.wait()
        vec_local.wait()
        for k in range(4):
            local[k].wait()
            third_hop[k][0].wait()
            third_hop[k][1].wait()


def first_call(pre, tokens, p1, weights, vec, cot=None):
    seqs, _, length = tokens.shape
    comm = weights is not None
    any_spec = pl.BlockSpec(memory_space=pl.ANY)
    in_specs = [pl.BlockSpec((1, D, length), lambda i, pre: ((pre[0] + i) % seqs, 0, 0)), whole((2, D, LANES))]
    out_specs = [
        pl.BlockSpec((1, D, length), lambda i, pre: (i, 0, 0)),
        pl.BlockSpec((1, 2, length), lambda i, pre: (i, 0, 0)),
    ]
    shapes = [sds((seqs, D, length), BF16), sds((seqs, 2, length), F32)]
    args, scratch = [pre, tokens, p1], []
    if comm:
        in_specs += [any_spec] * 4
        out_specs += [any_spec] * 4
        shapes += [sds(w.shape[:-2] + (2 * w.shape[-2], w.shape[-1]), BF16) for w in weights]
        shapes.append(sds((2,) + vec.shape, F32))
        args += list(weights) + [vec]
        dma = pltpu.SemaphoreType.DMA
        scratch = [dma((4, 5)), dma((4, 5)), dma, dma, dma]

    def kernel(*refs):
        first_kernel(comm, *refs)

    if comm:

        def at(i):
            return ((lax.axis_index("ch") * (seqs // 2) + i) % seqs, 0, 0)

        n, share = seqs // 2, cot.shape[1]

        def away(i):
            return ((1 - lax.axis_index("ch")) * n + jnp.minimum(i, n - 1), 0, 0)

        shapes.append(sds((n, share, length), BF16))
        args.append(cot)

        return pl.pallas_call(
            lambda *refs: first_kernel(True, None, *refs),
            grid=(seqs,),
            in_specs=[
                pl.BlockSpec((1, D, length), at),
                pl.BlockSpec((2, D, LANES), lambda i: (0, 0, 0), pipeline_mode=pl.Buffered(1)),
            ]
            + [any_spec] * 4
            + [pl.BlockSpec((1, share, length), away)],
            out_specs=tuple(
                [pl.BlockSpec((1, D, length), lambda i: (i, 0, 0)), pl.BlockSpec((1, 2, length), lambda i: (i, 0, 0))]
                + [any_spec] * 4
                + [pl.BlockSpec((1, share, length), lambda i: (jnp.minimum(i, n - 1), 0, 0))]
            ),
            out_shape=tuple(shapes),
            scratch_shapes=scratch,
            cost_estimate=cost_of(seqs * D * length * 40, seqs * D * length * 4),
            compiler_params=pltpu.CompilerParams(
                vmem_limit_bytes=VMEM_BYTES, collective_id=1, has_side_effects=True
            ),
        )(*args[1:])
    return call(kernel, (seqs,), in_specs, tuple(out_specs), tuple(shapes))(*args)


def put_edges(group, ref, lead_ref, trail_ref):
    length = ref.shape[2]
    place = pl.program_id(0) % (group // TWO)
    for k in range(group // TWO):

        @pl.when(place == k)
        def _():
            for j in range(TWO):
                lanes = slice((k * TWO + j) * REACH, (k * TWO + j + 1) * REACH)
                lead_ref[0, :, lanes] = ref[j, :, :REACH]
                trail_ref[0, :, lanes] = ref[j, :, length - REACH :]


def middle_kernel(group, keep, pre, first_ref, mask_ref, w_ref, p_ref, mid_ref, lead_ref, trail_ref, *rest):
    nar_refs = rest[-TWO:]
    length = first_ref.shape[2]
    for j in range(TWO):
        nar = jnp.dot(w_ref[...], first_ref[j], preferred_element_type=F32)
        nar_refs[j][...] = nar + spread(p_ref[0], length)
    for j in range(TWO):
        nar_ref = nar_refs[j]
        mean, scale = norm_stats(lambda sl: nar_ref[sl, :], INNER, length)
        mask = mask_ref[j].astype(F32)

        def body(sl, carry):
            hat = (nar_ref[sl, :] - mean) * scale
            point = hat * spread(p_ref[1, sl, :], length) + spread(p_ref[2, sl, :], length)
            phi = cdf(point)
            mid_ref[j, sl, :] = (point * phi * mask).astype(BF16)
            if keep:
                rest[0][j, sl, :] = hat.astype(BF16)
                rest[1][j, sl, :] = slope(point, phi) * mask
            return carry

        straight(INNER, length, body, 0)
        if keep:
            rest[2][j] = scale
    put_edges(group, mid_ref, lead_ref, trail_ref)


def middle_call(pre, first, mask, w_in, p2, count, offset, group, keep):
    _, _, length = first.shape
    seqs = mask.shape[0]
    edge = pl.BlockSpec((1, INNER, group * REACH), lambda i, pre: (i // (group // TWO), 0, 0))
    edge_shape = sds((count // group, INNER, group * REACH), BF16)
    own = pl.BlockSpec((TWO, INNER, length), lambda i, pre: (i, 0, 0))
    outs = [own, edge, edge]
    shapes = [sds((count, INNER, length), BF16), edge_shape, edge_shape]
    if keep:
        outs += [own, own, pl.BlockSpec((TWO, 1, length), lambda i, pre: (i, 0, 0))]
        shapes += [
            sds((count, INNER, length), BF16),
            sds((count, INNER, length), F32),
            sds((count, 1, length), F32),
        ]
    return call(
        functools.partial(middle_kernel, group, keep),
        (count // TWO,),
        [
            pl.BlockSpec((TWO, D, length), lambda i, pre: (offset // TWO + i, 0, 0)),
            pl.BlockSpec((TWO, 1, length), lambda i, pre: (((pre[0] + offset) // TWO + i) % (seqs // TWO), 0, 0)),
            whole((INNER, D)),
            whole((3, INNER, LANES)),
        ],
        tuple(outs),
        tuple(shapes),
        scratch=[pltpu.VMEM((INNER, length), F32)] * TWO,
        cost=cost_of(count * INNER * D * length * 1.5, count * (D + INNER * 3) * length * 2),
    )(pre, first, mask.reshape(seqs, 1, length), w_in, p2)


def gather_windows(group, body_ref, before_ref, after_ref, pad_ref, cat_refs, order, step=None):
    width, length, count = body_ref.shape[1], body_ref.shape[2], len(cat_refs)
    place = (pl.program_id(0) if step is None else step) % (group // count)
    for k in range(group // count):

        @pl.when(place == k)
        def _():
            for j in range(count):
                lanes = slice((k * count + j) * REACH, (k * count + j + 1) * REACH)
                pad_ref[j, :, LANES - REACH : LANES] = before_ref[0, :, lanes]
                pad_ref[j, :, LANES + length : LANES + length + REACH] = after_ref[0, :, lanes]

    for j in range(count):
        pad_ref[j, :, LANES : LANES + length] = body_ref[j]
        for tap in range(KERNEL):
            start = LANES + order * (tap - KERNEL // 2) * DILATION
            cat_refs[j][tap * width : (tap + 1) * width, :] = pad_ref[j, :, start : start + length]


def last_kernel(
    group, keep, pre, mid_ref, before_ref, after_ref, x_ref, wc_ref, wo_ref, p_ref, b_ref, *rest
):
    if keep:
        mixed_ref, hat_ref, gp_ref, scale_ref, last_out = rest[:5]
        last_refs = [last_out.at[j] for j in range(TWO)]
    else:
        mixed_ref = rest[1]
        last_refs = rest[-TWO:]
        rest = rest[:-TWO]
    pad_ref, cat_refs, conv_refs = rest[-1 - 2 * TWO], rest[-2 * TWO : -TWO], rest[-TWO:]
    length = mid_ref.shape[2]
    gather_windows(group, mid_ref, before_ref, after_ref, pad_ref, cat_refs, 1)
    for j in range(TWO):
        conv = jnp.dot(wc_ref[...], cat_refs[j][...], preferred_element_type=F32)
        conv_refs[j][...] = conv + spread(p_ref[0], length)
    for j in range(TWO):
        conv_ref, last_ref = conv_refs[j], last_refs[j]
        mean, scale = norm_stats(lambda sl: conv_ref[sl, :], INNER, length)

        def body(sl, carry):
            hat = (conv_ref[sl, :] - mean) * scale
            point = hat * spread(p_ref[1, sl, :], length) + spread(p_ref[2, sl, :], length)
            phi = cdf(point)
            last_ref[sl, :] = (point * phi).astype(BF16)
            if keep:
                hat_ref[j, sl, :] = hat.astype(BF16)
                gp_ref[j, sl, :] = slope(point, phi)
            return carry

        straight(INNER, length, body, 0)
        if keep:
            scale_ref[j] = scale
        branch = jnp.dot(wo_ref[...], last_ref[...], preferred_element_type=F32)
        mixed_ref[j] = (x_ref[j].astype(F32) + branch + spread(b_ref[...], length)).astype(BF16)


def last_call(pre, mid, before, after, tokens, wc, wo_t, p2, b_out, count, offset, group, keep, mixed):
    _, _, length = mid.shape
    seqs, share = tokens.shape[0], wo_t.shape[0]
    edge = pl.BlockSpec((1, INNER, group * REACH), lambda i, pre: (i // (group // TWO), 0, 0))
    own = pl.BlockSpec((TWO, INNER, length), lambda i, pre: (i, 0, 0))

    def pair_at(i, pre):
        return ((pre[0] + offset) // TWO + i) % (seqs // TWO)

    outs = [pl.BlockSpec((TWO, share, length), lambda i, pre: (pair_at(i, pre), 0, 0))]
    shapes = [sds((seqs, share, length), BF16)]
    in_specs = [
        own,
        edge,
        edge,
        pl.BlockSpec((TWO, share, length), lambda i, pre: (pair_at(i, pre), pre[1], 0)),
        whole((INNER, KERNEL * INNER)),
        whole((share, INNER)),
        whole((3, INNER, LANES), 1),
        whole((share, LANES)),
    ]
    args = [pre, mid, before, after, tokens, wc, wo_t, p2, b_out]
    aliases = None
    scratch = [pltpu.VMEM((TWO, INNER, length + 2 * LANES), BF16)]
    scratch += [pltpu.VMEM((KERNEL * INNER, length), BF16)] * TWO
    scratch += [pltpu.VMEM((INNER, length), F32)] * TWO
    if keep:
        outs += [own, own, pl.BlockSpec((TWO, 1, length), lambda i, pre: (i, 0, 0)), own]
        saved = sds((count, INNER, length), BF16)
        shapes += [saved, sds((count, INNER, length), F32), sds((count, 1, length), F32), saved]
    else:
        scratch += [pltpu.VMEM((INNER, length), BF16)] * TWO
        in_specs.append(pl.BlockSpec(memory_space=pl.ANY))
        args.append(mixed)
        aliases = {len(args) - 1: 0}
    return call(
        functools.partial(last_kernel, group, keep),
        (count // TWO,),
        in_specs,
        tuple(outs),
        tuple(shapes),
        scratch=scratch,
        aliases=aliases,
        cost=cost_of(count * INNER * (KERNEL * INNER + share) * length * 1.3, count * share * 6 * length * 2),
    )(*args)


def side(ref, sl):
    return jnp.concatenate([ref[j, sl, :].astype(F32) for j in range(ref.shape[0])], axis=1)


def across(ref, row):
    return jnp.concatenate([ref[j, row : row + 1, :] for j in range(ref.shape[0])], axis=1)


def row_sums(ref):
    ones = jnp.ones((8, LANES), F32)
    return lax.dot_general(
        ones, ref[...], (((1,), (1,)), ((), ())), precision=lax.Precision.HIGHEST, preferred_element_type=F32
    )


def norm_back(d_ref, gp_ref, hat_ref, scale, gain_ref, gg_ref, gb_ref, sum_ref, put):
    wide = d_ref.shape[1]
    zero = jnp.zeros((8, wide), F32)

    def body(sl, carry):
        d_pre = d_ref[sl, :] * side(gp_ref, sl)
        hat = side(hat_ref, sl)
        gg_ref[sl, :] += fold_lanes(d_pre * hat)
        gb_ref[sl, :] += fold_lanes(d_pre)
        e = d_pre * spread(gain_ref[0, sl, :], wide)
        d_ref[sl, :] = e
        return carry[0] + fold_rows(e), carry[1] + fold_rows(e * hat)

    total, dot = straight(INNER, wide, body, (zero, zero))
    total = total.sum(0, keepdims=True) * (scale / INNER)
    dot = dot.sum(0, keepdims=True) * (scale / INNER)

    def finish(sl, carry):
        v = (d_ref[sl, :] * scale - total - side(hat_ref, sl) * dot).astype(BF16)
        put(sl, v)
        sum_ref[sl, :] += fold_lanes(v.astype(F32))
        return carry

    straight(INNER, wide, finish, 0)


def rear_kernel(group, chs, pre, *refs):
    dy_refs = refs[:chs]
    w_ref, hat_ref, gp_ref, last_ref, scale_ref, p_ref = refs[chs : chs + 6]
    dconv_ref, lead_ref, trail_ref, gg_ref, gb_ref, gc_ref, gw_ref, go_ref = refs[chs + 6 : chs + 14]
    rows_ref, dy_ref, d_ref = refs[chs + 14 :]
    share, length = dy_refs[0].shape[1], dy_refs[0].shape[2]

    @pl.when(pl.program_id(0) == 0)
    def _():
        for ref in (gg_ref, gb_ref, gc_ref, gw_ref, go_ref):
            ref[...] = jnp.zeros_like(ref)

    for r in range(chs):
        at = pl.multiple_of(((pre[1] + chs - r) % chs) * share, share)
        for j in range(TWO):
            dy_ref[pl.ds(at, share), j * length : (j + 1) * length] = dy_refs[r][j]
    d_ref[...] = jnp.dot(w_ref[...], dy_ref[...], preferred_element_type=F32)
    last = jnp.concatenate([last_ref[j] for j in range(TWO)], axis=1)
    gw_ref[...] += lax.dot_general(last, dy_ref[...], (((1,), (1,)), ((), ())), preferred_element_type=F32)
    go_ref[...] += fold_lanes(dy_ref[...].astype(F32))

    def put(sl, v):
        for j in range(TWO):
            dconv_ref[j, sl, :] = v[:, j * length : (j + 1) * length]

    norm_back(d_ref, gp_ref, hat_ref, across(scale_ref, 0), p_ref, gg_ref, gb_ref, gc_ref, put)
    put_edges(group, dconv_ref, lead_ref, trail_ref)

    @pl.when(pl.program_id(0) == pl.num_programs(0) - 1)
    def _():
        for k, ref in enumerate((gc_ref, gg_ref, gb_ref)):
            rows_ref[:, k * INNER : (k + 1) * INNER] = row_sums(ref)
        rows_ref[:, 3 * INNER :] = row_sums(go_ref)


def const(shape):
    return pl.BlockSpec(shape, lambda i, pre: (0,) * len(shape), pipeline_mode=pl.Buffered(1))


def rear_call(pre, cot, others, w_out, hat, gp, last, scale, p2, group):
    seqs, share, length = cot.shape
    count = hat.shape[0]
    chs = 1 + len(others)
    edge = pl.BlockSpec((1, INNER, group * REACH), lambda i, pre: (i // (group // TWO), 0, 0))
    edge_shape = sds((count // group, INNER, group * REACH), BF16)
    own = pl.BlockSpec((TWO, INNER, length), lambda i, pre: (i, 0, 0))
    sums = [(INNER, LANES)] * 3 + [(INNER, D), (D, LANES), (8, 3 * INNER + D)]
    return call(
        functools.partial(rear_kernel, group, chs),
        (count // TWO,),
        [pl.BlockSpec((TWO, share, length), lambda i, pre: (pre[0] // TWO + i, 0, 0))]
        + [pl.BlockSpec((TWO, share, length), lambda i, pre: (i, 0, 0))] * (chs - 1)
        + [
            whole((INNER, D)),
            own,
            own,
            own,
            pl.BlockSpec((TWO, 1, length), lambda i, pre: (i, 0, 0)),
            whole((1, INNER, LANES), 4),
        ],
        tuple([own, edge, edge] + [const(v) for v in sums]),
        tuple([sds((count, INNER, length), BF16), edge_shape, edge_shape] + [sds(v, F32) for v in sums]),
        scratch=[pltpu.VMEM((D, TWO * length), BF16), pltpu.VMEM((INNER, TWO * length), F32)],
        cost=cost_of(count * INNER * D * length * 2.5, count * INNER * 5 * length * 2),
    )(pre, cot, *others, w_out, hat, gp, last, scale, p2)


def front_kernel(group, chs, pre, *refs):
    dconv_ref, before_ref, after_ref, mid_ref, hat_ref, gp_ref, scale_ref = refs[:7]
    x_ref, stat_ref, dy_ref, wc_ref, wi_ref, p2_ref, p1_ref = refs[7:14]
    refs = refs[14:]
    gt_ref = refs[0]
    send_refs = refs[1:chs]
    gcw_ref, gwi_ref, gg2_ref, gb2_ref, gbi_ref, gg1_ref, gb1_ref = refs[chs : chs + 7]
    pad_ref, cat_ref, d_ref, dn_ref, df_ref, first_ref = refs[chs + 7 :]
    share, length = dy_ref.shape[1], dy_ref.shape[2]
    wide = TWO * length

    @pl.when(pl.program_id(0) == 0)
    def _():
        for ref in (gcw_ref, gwi_ref, gg2_ref, gb2_ref, gbi_ref, gg1_ref, gb1_ref):
            ref[...] = jnp.zeros_like(ref)

    cats = [cat_ref.at[:, j * length : (j + 1) * length] for j in range(TWO)]
    gather_windows(group, dconv_ref, before_ref, after_ref, pad_ref, cats, -1)
    d_ref[...] = jnp.dot(wc_ref[...], cat_ref[...], preferred_element_type=F32)
    mid = jnp.concatenate([mid_ref[j] for j in range(TWO)], axis=1)
    gcw_ref[...] += lax.dot_general(cat_ref[...], mid, (((1,), (1,)), ((), ())), preferred_element_type=F32)

    def put(sl, v):
        dn_ref[sl, :] = v

    norm_back(d_ref, gp_ref, hat_ref, across(scale_ref, 0), p2_ref, gg2_ref, gb2_ref, gbi_ref, put)
    df_ref[...] = jnp.dot(wi_ref[...], dn_ref[...], preferred_element_type=F32)
    mean_in, scale_in = across(stat_ref, 0), across(stat_ref, 1)
    zero = jnp.zeros((8, wide), F32)

    def inner(sl, carry):
        hat = (side(x_ref, sl) - mean_in) * scale_in
        gain = spread(p1_ref[0, sl, :], wide)
        point = hat * gain + spread(p1_ref[1, sl, :], wide)
        phi = cdf(point)
        first_ref[sl, :] = (point * phi).astype(BF16)
        d_pre = df_ref[sl, :] * slope(point, phi)
        gg1_ref[sl, :] += fold_lanes(d_pre * hat)
        gb1_ref[sl, :] += fold_lanes(d_pre)
        e = d_pre * gain
        df_ref[sl, :] = e
        return carry[0] + fold_rows(e), carry[1] + fold_rows(e * hat)

    total, dot = straight(D, wide, inner, (zero, zero))
    total = total.sum(0, keepdims=True) * (scale_in / D)
    dot = dot.sum(0, keepdims=True) * (scale_in / D)
    gwi_ref[...] += lax.dot_general(
        dn_ref[...], first_ref[...], (((1,), (1,)), ((), ())), preferred_element_type=F32
    )
    for r in range(chs):
        base = ((pre[1] + r) % chs) * share

        def out(to, carry):
            rows = pl.ds(pl.multiple_of(base + to.start, 16), to.size)
            hat = (side(x_ref, rows) - mean_in) * scale_in
            v = df_ref[rows, :] * scale_in - total - hat * dot
            for j in range(TWO):
                half = v[:, j * length : (j + 1) * length]
                if r == 0:
                    gt_ref[j, to, :] = half + dy_ref[j, to, :].astype(F32)
                else:
                    send_refs[r - 1][j, to, :] = half.astype(BF16)
            return carry

        straight(share, wide, out, 0)


def front_call(pre, dconv, before, after, mid, hat, gp, scale, tokens, stat, cot, wc_t, wi_t, p2, p1, chs, group):
    seqs, share, length = cot.shape
    count = dconv.shape[0]
    edge = pl.BlockSpec((1, INNER, group * REACH), lambda i, pre: (i // (group // TWO), 0, 0))
    own = pl.BlockSpec((TWO, INNER, length), lambda i, pre: (i, 0, 0))

    def seq_block(rows):
        return pl.BlockSpec((TWO, rows, length), lambda i, pre: (pre[0] // TWO + i, 0, 0))

    inner_part, outer_part = (INNER, LANES), (D, LANES)
    sums = [(KERNEL * INNER, INNER), (INNER, D), inner_part, inner_part, inner_part, outer_part, outer_part]
    wide = TWO * length
    return call(
        functools.partial(front_kernel, group, chs),
        (count // TWO,),
        [
            own,
            edge,
            edge,
            own,
            own,
            own,
            pl.BlockSpec((TWO, 1, length), lambda i, pre: (i, 0, 0)),
            seq_block(D),
            pl.BlockSpec((TWO, 2, length), lambda i, pre: (i, 0, 0)),
            seq_block(share),
            whole((INNER, KERNEL * INNER)),
            whole((D, INNER)),
            whole((1, INNER, LANES), 1),
            whole((2, D, LANES)),
        ],
        tuple(
            [seq_block(share)]
            + [pl.BlockSpec((TWO, share, length), lambda i, pre: (i, 0, 0))] * (chs - 1)
            + [const(v) for v in sums]
        ),
        tuple(
            [sds((seqs, share, length), F32)]
            + [sds((count, share, length), BF16)] * (chs - 1)
            + [sds(v, F32) for v in sums]
        ),
        scratch=[
            pltpu.VMEM((TWO, INNER, length + 2 * LANES), BF16),
            pltpu.VMEM((KERNEL * INNER, wide), BF16),
            pltpu.VMEM((INNER, wide), F32),
            pltpu.VMEM((INNER, wide), BF16),
            pltpu.VMEM((D, wide), F32),
            pltpu.VMEM((D, wide), BF16),
        ],
        cost=cost_of(count * INNER * (2 * KERNEL * INNER + 2 * D) * length * 1.3, count * D * 8 * length * 2),
    )(pre, dconv, before, after, mid, hat, gp, scale, tokens, stat, cot, wc_t, wi_t, p2, p1)


def add_kernel(pre, part_ref, dy_ref, _, gt_ref):
    gt_ref[...] = part_ref[...].astype(F32) + dy_ref[...].astype(F32)


def add_call(pre, part, cot, gt, start):
    seqs, share, length = cot.shape
    count = part.shape[0]
    at = lambda i, pre: (pre[start] + i, 0, 0)
    return call(
        add_kernel,
        (count,),
        [
            pl.BlockSpec((1, share, length), lambda i, pre: (i, 0, 0)),
            pl.BlockSpec((1, share, length), at),
            pl.BlockSpec(memory_space=pl.ANY),
        ],
        pl.BlockSpec((1, share, length), at),
        sds((seqs, share, length), F32),
        aliases={3: 0},
        cost=cost_of(count * share * length, count * share * length * 8),
    )(pre, part, cot, gt)


def turn_kernel(pre, w_ref, flat_ref, turned_ref):
    unit = (
        lax.broadcasted_iota(jnp.int32, (INNER, INNER), 0) == lax.broadcasted_iota(jnp.int32, (INNER, INNER), 1)
    ).astype(F32).astype(BF16)
    flat_ref[...] = w_ref[0]
    turned_ref[...] = lax.dot_general(
        unit, w_ref[0], (((1,), (1,)), ((), ())), preferred_element_type=F32
    ).astype(BF16)


def turn_call(pre, conv):
    block = pl.BlockSpec((INNER, INNER), lambda k, pre: (0, k))
    shape = sds((INNER, KERNEL * INNER), BF16)
    return call(
        turn_kernel,
        (KERNEL,),
        [pl.BlockSpec((1, INNER, INNER), lambda k, pre: (k, 0, 0))],
        (block, block),
        (shape, shape),
        cost=cost_of(KERNEL * INNER**3, KERNEL * INNER * INNER * 6),
    )(pre, conv)


ORDERS = ((0, 1, 2, 3), (0, 1, 2, 3), (0, 2, 3, 1), (0, 2, 3, 1), (0, 1, 2, 3))
GIVE = 5
SCHEDULE = {
    1: [(2, 0)],
    2: [(0, 0), (2, 1)],
    3: [(0, 1)],
    6: [(2, 2)],
    9: [(5, 0), (3, 0), (0, 2), (1, 0)],
    10: [(3, 1), (1, 1), (2, 3), (5, 1)],
    13: [(0, 3), (2, 4)],
    14: [(5, 2)],
    15: [(3, 2), (1, 2)],
    16: [(5, 3), (4, 0), (2, 5)],
    17: [(4, 1), (2, 6), (3, 3), (4, 2), (0, 4), (5, 4), (1, 3), (2, 7)],
    19: [(4, 3), (3, 4), (0, 5), (1, 4), (5, 5), (3, 5), (1, 5)],
    20: [(0, 6)],
    21: [(1, 6), (4, 4), (3, 6), (5, 6), (2, 8), (4, 5), (0, 7)],
    22: [(4, 6), (1, 7), (4, 7), (3, 7), (0, 8), (5, 7)],
    23: [(4, 8), (1, 8), (3, 8), (2, 9)],
    24: [(3, 9), (4, 9), (1, 9), (5, 8), (0, 9)],
}


class Stream:
    def __init__(self, order, first, rows, arrays, slot):
        self.order, self.rows = order, rows
        self.acc, self.send, self.recv, self.swap, self.res, self.sems = arrays
        self.slot = slot
        self.levels = len(order)
        self.size = [rows >> (t + 1) for t in range(self.levels)]
        self.at = [rows - (rows >> t) for t in range(self.levels)]
        self.seq, self.ch = lax.axis_index("seq"), lax.axis_index("ch")
        self.low = [first]
        for t in range(self.levels):
            self.low.append(self.low[-1] + self.bit(order[t]) * self.size[t])

    def bit(self, b):
        return (self.seq // (1 << b)) % 2

    def partner(self, b):
        return {"seq": self.seq + (1 - 2 * self.bit(b)) * (1 << b)}

    def remote(self, src, dst, k, device):
        return pltpu.make_async_remote_copy(
            src_ref=src,
            dst_ref=dst,
            send_sem=self.sems[0].at[self.slot, k],
            recv_sem=self.sems[1].at[self.slot, k],
            device_id=device,
            device_id_type=pl.DeviceIdType.MESH,
        )

    def copy(self, k):
        if k < self.levels:
            window = pl.ds(self.at[k], self.size[k])
            held = self.send.at[:, pl.ds(0, self.size[k]), :]
            return self.remote(held, self.recv.at[:, window, :], k, self.partner(self.order[k]))
        if k == self.levels:
            return self.remote(self.swap.at[0], self.swap.at[1], k, {"ch": 1 - self.ch})
        t = 2 * self.levels - k
        place = spot(self.low[t + 1], 0, self.size[t])
        return self.remote(self.res.at[place, :], self.res.at[place, :], k, self.partner(self.order[t]))

    def start(self, k):
        if k < self.levels:
            away = self.low[k] + (1 - self.bit(self.order[k])) * self.size[k]
            for h in range(2):

                def pack(i, step, h=h):
                    self.send[h, spot(0, i, step), :] = self.acc[h, spot(away, i, step), :].astype(BF16)

                sliced(self.size[k], pack)
        elif k == self.levels:
            place = spot(self.low[-1], 0, self.size[-1])
            self.swap[0] = self.acc[1 - self.ch, place, :].astype(BF16)
        self.copy(k).start()

    def finish(self, k):
        self.copy(k).wait()
        if k < self.levels:
            for h in range(2):

                def add(i, step, h=h):
                    place = spot(self.low[k + 1], i, step)
                    self.acc[h, place, :] += self.recv[h, spot(self.at[k], i, step), :].astype(F32)

                sliced(self.size[k], add)
        elif k == self.levels:
            place = spot(self.low[-1], 0, self.size[-1])
            self.res[place, :] = (self.acc[self.ch, place, :] + self.swap[1].astype(F32)).astype(BF16)


def sliced(count, body):
    step = next(r for r in (96, 64, 48, 32, 16) if count % r == 0)

    def one(i, carry):
        body(pl.multiple_of(i * step, 16), step)
        return carry

    lax.fori_loop(0, count // step, one, 0)


def spot(base, i, step):
    return pl.ds(pl.multiple_of(base + i, 16), step)


HALF = INNER // 2
LEVELS = 4
EARLY_ROWS = HALF * (KERNEL + D // INNER)
ROWS = 768
SMALL_ROWS = 256


def stream_scratch():
    dma = pltpu.SemaphoreType.DMA
    out = [pltpu.VMEM((2, 4 * ROWS, INNER), F32)]
    moved = ROWS - (ROWS >> LEVELS)
    out += [pltpu.VMEM((2, ROWS // 2, INNER), BF16)] * 4
    out += [pltpu.VMEM((2, moved, INNER), BF16)] * 4
    out += [pltpu.VMEM((2, ROWS >> LEVELS, INNER), BF16)] * 4
    out += [pltpu.VMEM((4 * ROWS, INNER), BF16)]
    out += [
        pltpu.VMEM((2, SMALL_ROWS, LANES), F32),
        pltpu.VMEM((2, SMALL_ROWS // 2, LANES), BF16),
        pltpu.VMEM((2, SMALL_ROWS - (SMALL_ROWS >> LEVELS), LANES), BF16),
        pltpu.VMEM((2, SMALL_ROWS >> LEVELS, LANES), BF16),
        pltpu.VMEM((SMALL_ROWS, LANES), BF16),
    ]
    out += [dma((2 * (KERNEL + D // INNER),)), dma((5, 2 * LEVELS + 1)), dma((5, 2 * LEVELS + 1))]
    return out


def streams_of(refs):
    acc, send, recv, swap, res = refs[0], refs[1:5], refs[5:9], refs[9:13], refs[13]
    sems = refs[20:22]
    out = []
    for q, order in enumerate(ORDERS[:4]):
        out.append(Stream(order, q * ROWS, ROWS, (acc, send[q], recv[q], swap[q], res, sems), q))
    out.append(Stream(ORDERS[4], 0, SMALL_ROWS, (*refs[14:19], sems), 4))
    return out


def taps_kernel(group, pre, dconv_ref, before_ref, after_ref, mid_ref, gcw_ref, pad_ref, cat_ref):
    length = mid_ref.shape[2]

    @pl.when(pl.program_id(0) == 0)
    def _():
        gcw_ref[...] = jnp.zeros_like(gcw_ref)

    cats = [cat_ref.at[:, j * length : (j + 1) * length] for j in range(TWO)]
    gather_windows(group, dconv_ref, before_ref, after_ref, pad_ref, cats, -1)
    mid = jnp.concatenate([mid_ref[j] for j in range(TWO)], axis=1)
    gcw_ref[...] += lax.dot_general(cat_ref[...], mid, (((1,), (1,)), ((), ())), preferred_element_type=F32)


def taps_call(pre, dconv, before, after, mid, group):
    count, _, length = dconv.shape
    edge = pl.BlockSpec((1, INNER, group * REACH), lambda i, pre: (i // (group // TWO), 0, 0))
    own = pl.BlockSpec((TWO, INNER, length), lambda i, pre: (i, 0, 0))
    return call(
        functools.partial(taps_kernel, group),
        (count // TWO,),
        [own, edge, edge, own],
        const((KERNEL * INNER, INNER)),
        sds((KERNEL * INNER, INNER), F32),
        scratch=[
            pltpu.VMEM((TWO, INNER, length + 2 * LANES), BF16),
            pltpu.VMEM((KERNEL * INNER, TWO * length), BF16),
        ],
        cost=cost_of(count * KERNEL * INNER * INNER * length, KERNEL * INNER * INNER * 4),
    )(pre, dconv, before, after, mid)


def tail_kernel(group, *refs):
    dconv_ref, before_ref, after_ref, hat_ref, gp_ref, scale_ref, keep_ref, x_ref, stat_ref = refs[:9]
    mid_ref, before_oth, after_oth, wct_ref, wc_ref, wi_ref, p1_ref, p2_ref, rows_ref = refs[9:18]
    gcw_ref, gwo_ref = refs[18:20]
    mine_ref, last_ref, total_ref, small_ref, got_ref = refs[20:25]
    stream_refs = refs[25:47]
    pad_ref, cat_ref, d_ref, dn_ref, df_ref = refs[47:52]
    gg2_ref, gb2_ref, gbi_ref, gg1_ref, gb1_ref, give_send, give_recv = refs[52:]
    give_ref = dn_ref
    acc, small_acc, res, small_res, load_sem = (stream_refs[k] for k in (0, 14, 13, 18, 19))
    base = 3 * ROWS
    share, length = give_ref.shape[1], give_ref.shape[2]
    seq, ch = lax.axis_index("seq"), lax.axis_index("ch")
    step, steps = pl.program_id(0), pl.num_programs(0)
    count = give_ref.shape[0]
    streams = streams_of(stream_refs)

    def loads():
        out = []
        for h in range(2):
            mine = pl.ds(h * HALF, HALF)
            pieces = [gcw_ref.at[k, mine, :] for k in range(KERNEL)]
            pieces += [gwo_ref.at[mine, pl.ds(j * INNER, INNER)] for j in range(D // INNER)]
            for j, piece in enumerate(pieces):
                out.append((piece, acc.at[h, pl.ds(j * HALF, HALF), :]))
        return [pltpu.make_async_copy(a, b, load_sem.at[j]) for j, (a, b) in enumerate(out)]

    def give(i):
        return pltpu.make_async_remote_copy(
            src_ref=give_ref.at[i],
            dst_ref=got_ref.at[i],
            send_sem=give_send.at[i],
            recv_sem=give_recv.at[i],
            device_id={"ch": 1 - ch},
            device_id_type=pl.DeviceIdType.MESH,
        )

    def fill_inner():
        inner = [row_sums(ref)[0:1] for ref in (gbi_ref, gg2_ref, gb2_ref)]
        inner += [rows_ref[0:1, k * INNER : (k + 1) * INNER] for k in range(3)]
        at = base + HALF * D // INNER
        for h in range(2):
            for k, v in enumerate(inner):
                acc[h, at + k : at + k + 1, :HALF] = v[:, h * HALF : (h + 1) * HALF]

    def fill_outer():
        small_acc[...] = jnp.zeros_like(small_acc)
        outer = [row_sums(ref)[0:1] for ref in (gg1_ref, gb1_ref)] + [rows_ref[0:1, 3 * INNER :]]
        for h in range(2):
            for k, v in enumerate(outer):
                for j in range(INNER // LANES):
                    lanes = slice(h * INNER + j * LANES, h * INNER + (j + 1) * LANES)
                    row = k * (INNER // LANES) + j
                    small_acc[h, row : row + 1, :] = v[:, lanes]

    def act(actions):
        for q, k in actions:
            if q == GIVE:
                if k > 0:
                    give(k - 1).wait()
                if k < count:
                    give(k).start()
                continue
            if k > 0:
                streams[q].finish(k - 1)
            elif q == 3:
                fill_inner()
            elif q == 4:
                fill_outer()
            if k <= 2 * LEVELS:
                streams[q].start(k)

    @pl.when(step == 0)
    def _():
        for h in range(2):
            acc[h, EARLY_ROWS:, :] = jnp.zeros((4 * ROWS - EARLY_ROWS, INNER), F32)
        for copy in loads():
            copy.start()
        barrier = pltpu.get_barrier_semaphore()
        for device in [streams[0].partner(b) for b in range(LEVELS)] + [{"ch": 1 - ch}]:
            pl.semaphore_signal(barrier, inc=1, device_id=device, device_id_type=pl.DeviceIdType.MESH)
        pl.semaphore_wait(barrier, LEVELS + 1)
        for ref in (gg2_ref, gb2_ref, gbi_ref, gg1_ref, gb1_ref):
            ref[...] = jnp.zeros_like(ref)

    @pl.when(step == min(SCHEDULE))
    def _():
        for copy in loads():
            copy.wait()

    for at, actions in SCHEDULE.items():
        if at < 3 * count:

            @pl.when(step == at)
            def _():
                act(actions)

    @pl.when(step < count)
    def _():
        gather_windows(group, dconv_ref, before_ref, after_ref, pad_ref, [cat_ref], -1, step)
        d_ref[...] = jnp.dot(wct_ref[...], cat_ref[...], preferred_element_type=F32)

        def put(sl, v):
            dn_ref[step, sl, :] = v

        norm_back(d_ref, gp_ref, hat_ref, scale_ref[0], p2_ref.at[1:2], gg2_ref, gb2_ref, gbi_ref, put)
        for h in range(2):
            for j in range(D // INNER):
                part = lax.dot_general(
                    dn_ref[step, h * HALF : (h + 1) * HALF, :],
                    keep_ref[0, j * INNER : (j + 1) * INNER, :],
                    (((1,), (1,)), ((), ())),
                    preferred_element_type=F32,
                )
                acc[h, base + j * HALF : base + (j + 1) * HALF, :] += part

    @pl.when(jnp.logical_and(step >= count, step < 2 * count))
    def _():
        now = step - count
        df_ref[...] = jnp.dot(wi_ref[...], dn_ref[now], preferred_element_type=F32)
        mean_in, scale_in = stat_ref[0, 0:1, :], stat_ref[0, 1:2, :]
        zero = jnp.zeros((8, length), F32)

        def inner(sl, carry):
            hat = (x_ref[0, sl, :].astype(F32) - mean_in) * scale_in
            gain = spread(p1_ref[0, sl, :], length)
            point = hat * gain + spread(p1_ref[1, sl, :], length)
            d_pre = df_ref[sl, :] * slope(point, cdf(point))
            gg1_ref[sl, :] += fold_lanes(d_pre * hat)
            gb1_ref[sl, :] += fold_lanes(d_pre)
            e = d_pre * gain
            df_ref[sl, :] = e
            return carry[0] + fold_rows(e), carry[1] + fold_rows(e * hat)

        total, dot = straight(D, length, inner, (zero, zero))
        total = total.sum(0, keepdims=True) * (scale_in / D)
        dot = dot.sum(0, keepdims=True) * (scale_in / D)
        for r in range(2):
            start = ((ch + r) % 2) * share

            def out(to, carry):
                rows = pl.ds(pl.multiple_of(start + to.start, 16), to.size)
                hat = (x_ref[0, rows, :].astype(F32) - mean_in) * scale_in
                v = (df_ref[rows, :] * scale_in - total - hat * dot).astype(BF16)
                if r == 0:
                    mine_ref[0, to, :] = v
                else:
                    give_ref[now, to, :] = v
                return carry

            straight(share, length, out, 0)

    @pl.when(step >= 2 * count)
    def _():
        gather_windows(group, mid_ref, before_oth, after_oth, pad_ref, [cat_ref], 1, step)
        conv = jnp.dot(wc_ref[...], cat_ref[...], preferred_element_type=F32)
        d_ref[...] = conv + spread(p2_ref[3], length)
        mean, scale = norm_stats(lambda sl: d_ref[sl, :], INNER, length)

        def body(sl, carry):
            hat = (d_ref[sl, :] - mean) * scale
            point = hat * spread(p2_ref[4, sl, :], length) + spread(p2_ref[5, sl, :], length)
            last_ref[0, sl, :] = (point * cdf(point)).astype(BF16)
            return carry

        straight(INNER, length, body, 0)

    @pl.when(step == steps - 1)
    def _():
        act(SCHEDULE[max(SCHEDULE)])
        done = [
            pltpu.make_async_copy(res, total_ref, load_sem.at[0]),
            pltpu.make_async_copy(small_res, small_ref, load_sem.at[1]),
        ]
        for copy in done:
            copy.start()
        for copy in done:
            copy.wait()


def tail_call(dconv, rims_own, hat, gp, scale, first, tokens, stat, mid, rims_oth, wc_t, wc, wi_t, p1, p2, rows, gcw, gwo, group):
    count, _, length = dconv.shape
    share = D // 2
    any_spec = pl.BlockSpec(memory_space=pl.ANY)

    def fixed(shape):
        return pl.BlockSpec(shape, lambda i: (0,) * len(shape), pipeline_mode=pl.Buffered(1))

    def phase(k):
        return lambda i: jnp.clip(i - k * count, 0, count - 1)

    def block(k, width):
        return pl.BlockSpec((1, width, length), lambda i: (phase(k)(i), 0, 0))

    def edge(k):
        return pl.BlockSpec((1, INNER, group * REACH), lambda i: (phase(k)(i) // group, 0, 0))

    dma = pltpu.SemaphoreType.DMA
    return pl.pallas_call(
        functools.partial(tail_kernel, group),
        grid=(3 * count,),
        in_specs=[
            block(0, INNER),
            edge(0),
            edge(0),
            block(0, INNER),
            block(0, INNER),
            block(0, 1),
            block(0, D),
            pl.BlockSpec((1, D, length), lambda i: (lax.axis_index("ch") * count + phase(1)(i), 0, 0)),
            block(1, 2),
            block(2, INNER),
            edge(2),
            edge(2),
            fixed(wc_t.shape),
            fixed(wc.shape),
            fixed(wi_t.shape),
            fixed(p1.shape),
            fixed(p2.shape),
            fixed(rows.shape),
            any_spec,
            any_spec,
        ],
        out_specs=(block(1, share), block(2, INNER), any_spec, any_spec, any_spec),
        out_shape=(
            sds((count, share, length), BF16),
            sds((count, INNER, length), BF16),
            sds((4 * ROWS, INNER), BF16),
            sds((SMALL_ROWS, LANES), BF16),
            sds((count, share, length), BF16),
        ),
        scratch_shapes=stream_scratch()
        + [
            pltpu.VMEM((1, INNER, length + 2 * LANES), BF16),
            pltpu.VMEM((KERNEL * INNER, length), BF16),
            pltpu.VMEM((INNER, length), F32),
            pltpu.VMEM((count, INNER, length), BF16),
            pltpu.VMEM((D, length), F32),
            pltpu.VMEM((INNER, LANES), F32),
            pltpu.VMEM((INNER, LANES), F32),
            pltpu.VMEM((INNER, LANES), F32),
            pltpu.VMEM((D, LANES), F32),
            pltpu.VMEM((D, LANES), F32),
            dma((count,)),
            dma((count,)),
        ],
        cost_estimate=cost_of(count * INNER * (KERNEL * INNER + D) * length * 4, 4 * ROWS * INNER * 12),
        compiler_params=pltpu.CompilerParams(
            vmem_limit_bytes=TAIL_BYTES, collective_id=2, has_side_effects=True
        ),
    )(dconv, *rims_own, hat, gp, scale, first, tokens, stat, mid, *rims_oth, wc_t, wc, wi_t, p1, p2, rows, gcw, gwo)


TAIL_BYTES = 63 * 1024 * 1024


def finish_kernel(pre, mine_ref, got_ref, dy_ref, last_ref, x_ref, wo_ref, b_ref, total_ref, small_ref, _, *outs):
    gt_ref, mixed_ref, gcw_ref, gwi_ref, gwo_ref, inner_ref, outer_ref = outs
    length = dy_ref.shape[2]
    step, count = pl.program_id(0), pl.num_programs(0) // 2
    part = gcw_ref.shape[1]

    @pl.when(step < count)
    def _():
        gt_ref[...] = mine_ref[...].astype(F32) + dy_ref[...].astype(F32)

    @pl.when(step >= count)
    def _():
        gt_ref[...] = got_ref[...].astype(F32) + dy_ref[...].astype(F32)
        for j in range(TWO):
            branch = jnp.dot(wo_ref[...], last_ref[j], preferred_element_type=F32)
            mixed_ref[j] = (x_ref[j].astype(F32) + branch + spread(b_ref[...], length)).astype(BF16)

    for k in range(KERNEL):

        @pl.when(step == k // TWO)
        def _():
            gcw_ref[k] = total_ref[k * part : (k + 1) * part, :].astype(F32)

    for k, (ref, start) in enumerate(((gwo_ref, KERNEL * part), (gwi_ref, 3 * ROWS))):

        @pl.when(step == KERNEL // TWO + 1 + k)
        def _():
            for j in range(D // INNER):
                ref[:, j * INNER : (j + 1) * INNER] = total_ref[start + j * part : start + (j + 1) * part, :].astype(F32)

    @pl.when(step == 0)
    def _():
        at = 3 * ROWS + part * D // INNER
        inner_ref[...] = total_ref[at : at + 16, :].astype(F32)
        outer_ref[...] = small_ref[:16, :].astype(F32)


def finish_call(pre, mine, got, cot, last, tokens, wo_t, b_out, total, small, mixed, part):
    seqs, share, length = cot.shape
    count = got.shape[0] // TWO
    early = lambda i: jnp.minimum(i, count - 1)
    late = lambda i: jnp.maximum(i - count, 0)
    return call(
        finish_kernel,
        (2 * count,),
        [
            pl.BlockSpec((TWO, share, length), lambda i, pre: (early(i), 0, 0)),
            pl.BlockSpec((TWO, share, length), lambda i, pre: (late(i), 0, 0)),
            pl.BlockSpec((TWO, share, length), lambda i, pre: ((pre[0] // TWO + i) % (seqs // TWO), 0, 0)),
            pl.BlockSpec((TWO, INNER, length), lambda i, pre: (late(i), 0, 0)),
            pl.BlockSpec((TWO, share, length), lambda i, pre: (pre[2] // TWO + late(i), pre[1], 0)),
            whole(wo_t.shape),
            whole(b_out.shape),
            whole(total.shape),
            whole(small.shape),
            pl.BlockSpec(memory_space=pl.ANY),
        ],
        (
            pl.BlockSpec((TWO, share, length), lambda i, pre: ((pre[0] // TWO + i) % (seqs // TWO), 0, 0)),
            pl.BlockSpec((TWO, share, length), lambda i, pre: (pre[2] // TWO + late(i), 0, 0)),
            const((KERNEL, part, INNER)),
            const((part, D)),
            const((part, D)),
            const((16, INNER)),
            const((16, LANES)),
        ),
        (
            sds((seqs, share, length), F32),
            sds(mixed.shape, BF16),
            sds((KERNEL, part, INNER), F32),
            sds((part, D), F32),
            sds((part, D), F32),
            sds((16, INNER), F32),
            sds((16, LANES), F32),
        ),
        aliases={10: 1},
    )(pre, mine, got, cot, last, tokens, wo_t, b_out, total, small, mixed)


def rotate(value, axis, count, by):
    return lax.ppermute(value, axis, [(i, (i + by) % count) for i in range(count)])


def shift(value, by):
    count = lax.axis_size("seq")
    pairs = [(i, i + by) for i in range(count) if 0 <= i + by < count]
    return lax.ppermute(value, "seq", pairs)


def rims(lead, trail):
    return shift(trail, 1), shift(lead, -1)


def own_slice(value, width, dim):
    return lax.dynamic_slice_in_dim(value, lax.axis_index("ch") * width, width, dim)


def lane_copies(vectors):
    return jnp.broadcast_to(vectors[..., None], vectors.shape + (LANES,))


def body(
    tokens,
    pad_mask,
    cotangent,
    ln1_gain,
    first_norm_bias,
    w_in,
    b_in,
    ln2_gain,
    ln2_bias,
    conv_w,
    conv_b,
    ln3_gain,
    ln3_bias,
    w_out,
    b_out,
):
    chs = lax.axis_size("ch")
    ch = lax.axis_index("ch")
    seqs, _, length = tokens.shape
    share = b_out.shape[0]
    part = b_in.shape[0]
    n = seqs // chs
    group = min(4, n)
    starts = [((ch + chs - r) % chs) * n for r in range(1, chs)]
    pre = jnp.stack([ch * n, ch] + starts).astype(jnp.int32)
    pair = chs == 2 and lax.axis_size("seq") == 1 << LEVELS

    p1 = lane_copies(jnp.stack([ln1_gain, first_norm_bias]))
    bo = lane_copies(b_out)
    vec = jnp.stack([b_in, ln2_gain, ln2_bias, conv_b, ln3_gain, ln3_bias, b_in, b_in])
    if pair:
        first, stat, w_in_full, conv_full, w_out_full, vec_full, away = first_call(
            pre, tokens, p1, (w_in, conv_w, w_out), vec, cotangent
        )
        others = [rotate(away, "ch", chs, 1)]
        inner = vec_full.transpose(1, 0, 2).reshape(8, INNER)[:6]
    else:
        first, stat = first_call(pre, tokens, p1, None, None)
        w_in_full = lax.all_gather(w_in, "ch", axis=0, tiled=True)
        conv_full = lax.all_gather(conv_w, "ch", axis=1, tiled=True)
        w_out_full = lax.all_gather(w_out, "ch", axis=0, tiled=True)
        inner = lax.all_gather(vec, "ch", axis=1, tiled=True)[:6]
        others = []
        for r in range(1, chs):
            block = lax.dynamic_slice_in_dim(cotangent, ((ch + r) % chs) * n, n, 0)
            others.append(rotate(block, "ch", chs, r))

    p2 = lane_copies(inner)
    wc, wc_t = turn_call(pre, conv_full)
    wi_t = w_in_full.T
    wo_t = lax.dynamic_slice_in_dim(w_out_full, ch * share, share, 1).T

    mid_own, lead, trail, hat_mid, gp_mid, scale_mid = middle_call(
        pre, first, pad_mask, w_in_full, p2, n, 0, group, True
    )
    before, after = rims(lead, trail)
    mid_oth, lead, trail = middle_call(pre, first, pad_mask, w_in_full, p2, seqs - n, n, group, False)
    before_oth, after_oth = rims(lead, trail)
    mixed, hat_out, gp_out, scale_out, last_own = last_call(
        pre, mid_own, before, after, tokens, wc, wo_t, p2, bo, n, 0, group, True, None
    )
    dconv, lead, trail, gg3, gb3, gcb, gwo, gbo, rows = rear_call(
        pre, cotangent, others, w_out_full, hat_out, gp_out, last_own, scale_out, p2, group
    )
    lead, trail = rims(lead, trail)
    if pair:
        gcw = taps_call(pre, dconv, lead, trail, mid_own, group)
        mine, last_oth, total, small, got = tail_call(
            dconv, (lead, trail), hat_mid, gp_mid, scale_mid, first, tokens, stat, mid_oth, (before_oth, after_oth),
            wc_t, wc, wi_t, p1, p2, rows, gcw.reshape(KERNEL, INNER, INNER), gwo, group,
        )
        gt, mixed, gcw, gwi, gwo, inner_sums, outer_sums = finish_call(
            pre, mine, got, cotangent, last_oth, tokens, wo_t, bo, total, small, mixed, part
        )
        inner_sums, outer_sums = inner_sums[:6, :part], outer_sums[:15].reshape(3, share)
    else:
        gt, *rest = front_call(
            pre, dconv, lead, trail, mid_own, hat_mid, gp_mid, scale_mid, tokens, stat, cotangent,
            wc_t, wi_t, p2, p1, chs, group,
        )
        sends = [rotate(v, "ch", chs, r + 1) for r, v in enumerate(rest[: chs - 1])]
        gcw, gwi, gg2, gb2, gbi, gg1, gb1 = rest[chs - 1 :]
        gcw = gcw.reshape(KERNEL, INNER, INNER)
        inner_sums = jnp.stack([v.sum(1) for v in (gbi, gg2, gb2, gcb, gg3, gb3)])
        outer_sums = jnp.stack([v.sum(1) for v in (gg1, gb1, gbo)])
        mixed, = last_call(
            pre, mid_oth, before_oth, after_oth, tokens, wc, wo_t, p2, bo, seqs - n, n, group, False, mixed
        )
        gcw, gwi, gwo, inner_sums, outer_sums = lax.psum((gcw, gwi, gwo, inner_sums, outer_sums), ("seq", "ch"))
        gcw = own_slice(gcw, part, 1)
        gwi = own_slice(gwi, part, 0)
        gwo = own_slice(gwo, part, 0)
        inner_sums = own_slice(inner_sums, part, 1)
        outer_sums = own_slice(outer_sums, share, 1)
        for r in range(chs - 1):
            gt = add_call(pre, sends[r], cotangent, gt, 2 + r)
    return (
        mixed,
        gt,
        outer_sums[0],
        outer_sums[1],
        gwi,
        inner_sums[0],
        inner_sums[1],
        inner_sums[2],
        gcw,
        inner_sums[3],
        inner_sums[4],
        inner_sums[5],
        gwo,
        outer_sums[2],
    )


def solution(mesh):
    in_specs = (
        P(None, None, "seq"),
        P(None, "seq"),
        P(None, "ch", "seq"),
        P(),
        P(),
        P("ch", None),
        P("ch"),
        P("ch"),
        P("ch"),
        P(None, "ch", None),
        P("ch"),
        P("ch"),
        P("ch"),
        P("ch", None),
        P("ch"),
    )
    out_specs = (
        P(None, "ch", "seq"),
        P(None, "ch", "seq"),
        P("ch"),
        P("ch"),
        P("ch", None),
        P("ch"),
        P("ch"),
        P("ch"),
        P(None, "ch", None),
        P("ch"),
        P("ch"),
        P("ch"),
        P("ch", None),
        P("ch"),
    )
    return jax.shard_map(body, mesh=mesh, in_specs=in_specs, out_specs=out_specs, check_vma=False)
```

```python
import functools
import math

import jax
import jax.numpy as jnp
from jax import lax
from jax.experimental import pallas as pl
from jax.experimental.pallas import tpu as pltpu
from jax.sharding import PartitionSpec as P

D = 1280
INNER = 640
KERNEL = 5
DILATION = 16
REACH = KERNEL // 2 * DILATION
EPS = 1e-05
HALF_ROOT = math.sqrt(0.5)
DENSITY = 1.0 / math.sqrt(2.0 * math.pi)
F32 = jnp.float32
BF16 = jnp.bfloat16
LANES = 128
VMEM_BYTES = 60 * 1024 * 1024


TWO = 2


def rows_of(width):
    return next(r for r in (64, 32, 16) if width % r == 0)


def straight(width, length, body, init):
    rows = next(r for r in (64, 32, 16) if width % r == 0 and r * length <= 64 * 256 or r == 16)
    for i in range(width // rows):
        init = body(pl.ds(i * rows, rows), init)
    return init


def fold_rows(v):
    return v.reshape(v.shape[0] // 8, 8, v.shape[1]).sum(0)


def fold_lanes(v):
    out = v[:, :LANES]
    for j in range(1, v.shape[1] // LANES):
        out = out + v[:, j * LANES : (j + 1) * LANES]
    return out


def spread(p, length):
    return jnp.concatenate([p] * (length // LANES), axis=1)


def loop(width, body, init):
    rows = rows_of(width)

    def step(i, carry):
        return body(pl.ds(pl.multiple_of(i * rows, rows), rows), carry)

    return lax.fori_loop(0, width // rows, step, init)


def norm_stats(load, width, length, rolled=False):
    def over(body, init):
        return loop(width, body, init) if rolled else straight(width, length, body, init)

    zero = jnp.zeros((8, length), F32)
    total = over(lambda sl, a: a + fold_rows(load(sl)), zero)
    mean = total.sum(0, keepdims=True) / width

    def square(sl, a):
        c = load(sl) - mean
        return a + fold_rows(c * c)

    total = over(square, zero)
    return mean, lax.rsqrt(total.sum(0, keepdims=True) / width + EPS)


def cdf(p):
    return 0.5 + 0.5 * lax.erf(p * HALF_ROOT)


def slope(p, phi):
    return phi + p * (DENSITY * jnp.exp(p * p * -0.5))


def call(kernel, grid, in_specs, out_specs, out_shape, scratch=(), prefetch=1, aliases=None, cost=None):
    return pl.pallas_call(
        kernel,
        grid_spec=pltpu.PrefetchScalarGridSpec(
            num_scalar_prefetch=prefetch,
            grid=grid,
            in_specs=in_specs,
            out_specs=out_specs,
            scratch_shapes=list(scratch),
        ),
        out_shape=out_shape,
        input_output_aliases=aliases or {},
        cost_estimate=cost,
        compiler_params=pltpu.CompilerParams(vmem_limit_bytes=VMEM_BYTES),
    )


def cost_of(macs, bytes_accessed):
    return pl.CostEstimate(flops=int(2 * macs), bytes_accessed=int(bytes_accessed), transcendentals=0)


def whole(shape, at=0):
    return pl.BlockSpec(shape, lambda i, pre: (at,) + (0,) * (len(shape) - 1), pipeline_mode=pl.Buffered(1))


def sds(shape, dtype):
    return jax.ShapeDtypeStruct(shape, dtype)


def weight_copies(own_refs, full_refs, sems):
    seq, ch = lax.axis_index("seq"), lax.axis_index("ch")
    core, row = seq % 2, (seq // 2) % 2
    send_sem, recv_sem = sems
    across, along, beside = {"ch": 1 - ch}, {"seq": seq + 2 - 4 * row}, {"seq": seq + 1 - 2 * core}

    def part(ref, at, size):
        at = pl.multiple_of(at, 16)
        return ref.at[:, pl.ds(at, size), :] if len(ref.shape) == 3 else ref.at[pl.ds(at, size), :]

    (w_in, conv, w_out), (w_in_full, conv_full, w_out_full) = own_refs, full_refs
    items = [
        (w_in, w_in_full),
        (conv.at[pl.ds(0, 2)], conv_full.at[pl.ds(0, 2)]),
        (conv.at[pl.ds(2, 3)], conv_full.at[pl.ds(2, 3)]),
        (w_out, w_out_full),
    ]
    local, first_hop, second_hop, third_hop = [], [], [], []
    for k, (own, full) in enumerate(items):
        half = own.shape[-2]
        size = half // 4

        def remote(src, dst, slot, device):
            return pltpu.make_async_remote_copy(
                src_ref=src,
                dst_ref=dst,
                send_sem=send_sem.at[k, slot],
                recv_sem=recv_sem.at[k, slot],
                device_id=device,
                device_id_type=pl.DeviceIdType.MESH,
            )

        quarter = (row * 2 + core) * size
        local.append(remote(own, part(full, ch * half, half), 4, beside))
        first_hop.append(remote(part(own, quarter, size), part(full, ch * half + quarter, size), 0, across))
        landed = (1 - ch) * half
        mine = part(full, landed + quarter, size)
        second_hop.append(remote(mine, mine, 1, along))
        both = []
        for j, r in enumerate((row, 1 - row)):
            piece = part(full, landed + (r * 2 + core) * size, size)
            both.append(remote(piece, piece, 2 + j, beside))
        third_hop.append(both)
    return local, first_hop, second_hop, third_hop


def first_kernel(comm, pre, x_ref, p_ref, *rest):
    if comm:
        own_refs, own_vec, cot_ref, first_ref, stat_ref = rest[:3], rest[3], rest[4], rest[5], rest[6]
        full_refs, full_vec, away_ref = rest[7:10], rest[10], rest[11]
        exchange(own_refs, own_vec, full_refs, full_vec, rest[12:14], rest[14:])

        @pl.when(pl.program_id(0) < pl.num_programs(0) // 2)
        def _():
            away_ref[...] = cot_ref[...]

    else:
        first_ref, stat_ref = rest
    length = x_ref.shape[2]
    mean, scale = norm_stats(lambda sl: x_ref[0, sl, :].astype(F32), D, length, True)
    stat_ref[0, 0:1, :] = mean
    stat_ref[0, 1:2, :] = scale

    def body(sl, carry):
        hat = (x_ref[0, sl, :].astype(F32) - mean) * scale
        point = hat * spread(p_ref[0, sl, :], length) + spread(p_ref[1, sl, :], length)
        first_ref[0, sl, :] = (point * cdf(point)).astype(BF16)
        return carry

    loop(D, body, 0)


def exchange(own_refs, own_vec, full_refs, full_vec, sems, vec_sems):
    step, steps = pl.program_id(0), pl.num_programs(0)
    seq, ch = lax.axis_index("seq"), lax.axis_index("ch")
    core, row = seq % 2, (seq // 2) % 2
    local, first_hop, second_hop, third_hop = weight_copies(own_refs, full_refs, sems)
    vec_local = pltpu.make_async_copy(own_vec, full_vec.at[ch], vec_sems[0])
    vec_remote = pltpu.make_async_remote_copy(
        src_ref=own_vec,
        dst_ref=full_vec.at[ch],
        send_sem=vec_sems[1],
        recv_sem=vec_sems[2],
        device_id={"ch": 1 - ch},
        device_id_type=pl.DeviceIdType.MESH,
    )

    @pl.when(step == 0)
    def _():
        barrier = pltpu.get_barrier_semaphore()
        for device in ({"ch": 1 - ch}, {"seq": seq + 2 - 4 * row}, {"seq": seq + 1 - 2 * core}):
            pl.semaphore_signal(barrier, inc=1, device_id=device, device_id_type=pl.DeviceIdType.MESH)
        pl.semaphore_wait(barrier, 3)
        vec_remote.start()
        first_hop[0].start()
        vec_local.start()
        for copy in local:
            copy.start()

    for k in range(4):

        if k > 0:

            @pl.when(step == (0, 1, 4, 7)[k])
            def _():
                first_hop[k].start()

        @pl.when(step == (4, 7, 10, 12)[k])
        def _():
            first_hop[k].wait()
            second_hop[k].start()
            third_hop[k][0].start()

        @pl.when(step == (7, 10, 14, 15)[k])
        def _():
            second_hop[k].wait()
            third_hop[k][1].start()

    @pl.when(step == steps - 1)
    def _():
        vec_remote.wait()
        vec_local.wait()
        for k in range(4):
            local[k].wait()
            third_hop[k][0].wait()
            third_hop[k][1].wait()


def first_call(pre, tokens, p1, weights, vec, cot=None):
    seqs, _, length = tokens.shape
    comm = weights is not None
    any_spec = pl.BlockSpec(memory_space=pl.ANY)
    in_specs = [pl.BlockSpec((1, D, length), lambda i, pre: ((pre[0] + i) % seqs, 0, 0)), whole((2, D, LANES))]
    out_specs = [
        pl.BlockSpec((1, D, length), lambda i, pre: (i, 0, 0)),
        pl.BlockSpec((1, 2, length), lambda i, pre: (i, 0, 0)),
    ]
    shapes = [sds((seqs, D, length), BF16), sds((seqs, 2, length), F32)]
    args, scratch = [pre, tokens, p1], []
    if comm:
        in_specs += [any_spec] * 4
        out_specs += [any_spec] * 4
        shapes += [sds(w.shape[:-2] + (2 * w.shape[-2], w.shape[-1]), BF16) for w in weights]
        shapes.append(sds((2,) + vec.shape, F32))
        args += list(weights) + [vec]
        dma = pltpu.SemaphoreType.DMA
        scratch = [dma((4, 5)), dma((4, 5)), dma, dma, dma]

    def kernel(*refs):
        first_kernel(comm, *refs)

    if comm:

        def at(i):
            return ((lax.axis_index("ch") * (seqs // 2) + i) % seqs, 0, 0)

        n, share = seqs // 2, cot.shape[1]

        def away(i):
            return ((1 - lax.axis_index("ch")) * n + jnp.minimum(i, n - 1), 0, 0)

        shapes.append(sds((n, share, length), BF16))
        args.append(cot)

        return pl.pallas_call(
            lambda *refs: first_kernel(True, None, *refs),
            grid=(seqs,),
            in_specs=[
                pl.BlockSpec((1, D, length), at),
                pl.BlockSpec((2, D, LANES), lambda i: (0, 0, 0), pipeline_mode=pl.Buffered(1)),
            ]
            + [any_spec] * 4
            + [pl.BlockSpec((1, share, length), away)],
            out_specs=tuple(
                [pl.BlockSpec((1, D, length), lambda i: (i, 0, 0)), pl.BlockSpec((1, 2, length), lambda i: (i, 0, 0))]
                + [any_spec] * 4
                + [pl.BlockSpec((1, share, length), lambda i: (jnp.minimum(i, n - 1), 0, 0))]
            ),
            out_shape=tuple(shapes),
            scratch_shapes=scratch,
            cost_estimate=cost_of(seqs * D * length * 40, seqs * D * length * 4),
            compiler_params=pltpu.CompilerParams(
                vmem_limit_bytes=VMEM_BYTES, collective_id=1, has_side_effects=True
            ),
        )(*args[1:])
    return call(kernel, (seqs,), in_specs, tuple(out_specs), tuple(shapes))(*args)


class Rims:
    def __init__(self, lead, trail, before, after, send_sem, recv_sem):
        self.seq, self.count = lax.axis_index("seq"), lax.axis_size("seq")
        self.before, self.after = before, after

        def remote(src, dst, k, by):
            return pltpu.make_async_remote_copy(
                src_ref=src,
                dst_ref=dst,
                send_sem=send_sem.at[k],
                recv_sem=recv_sem.at[k],
                device_id={"seq": self.seq + by},
                device_id_type=pl.DeviceIdType.MESH,
            )

        self.up = lambda: remote(trail, before, 0, 1)
        self.down = lambda: remote(lead, after, 1, -1)
        self.has_up, self.has_down = self.seq < self.count - 1, self.seq > 0

    def greet(self):
        barrier = pltpu.get_barrier_semaphore()
        for there, by in ((self.has_up, 1), (self.has_down, -1)):

            @pl.when(there)
            def _():
                pl.semaphore_signal(
                    barrier, inc=1, device_id={"seq": self.seq + by}, device_id_type=pl.DeviceIdType.MESH
                )
        return self.has_up.astype(jnp.int32) + self.has_down.astype(jnp.int32)

    def start(self):
        pl.when(self.has_up)(lambda: self.up().start())
        pl.when(self.has_down)(lambda: self.down().start())

    def wait(self):
        @pl.when(self.has_up)
        def _():
            self.up().wait_send()
            self.down().wait_recv()

        @pl.when(self.has_down)
        def _():
            self.down().wait_send()
            self.up().wait_recv()


def rim_steps(lead, trail, before, after, zeros, send_sem, recv_sem, local_sem):
    rims = Rims(lead, trail, before, after, send_sem, recv_sem)
    step, steps = pl.program_id(0), pl.num_programs(0)
    ends = (
        (jnp.logical_not(rims.has_down), lambda: pltpu.make_async_copy(zeros, before, local_sem.at[0])),
        (jnp.logical_not(rims.has_up), lambda: pltpu.make_async_copy(zeros, after, local_sem.at[1])),
    )

    @pl.when(step == 0)
    def _():
        zeros[...] = jnp.zeros_like(zeros)
        pl.semaphore_wait(pltpu.get_barrier_semaphore(), rims.greet())
        rims.start()
        for there, copy in ends:
            pl.when(there)(lambda: copy().start())

    def last():
        rims.wait()
        for there, copy in ends:
            pl.when(there)(lambda: copy().wait())

    pl.when(step == steps - 1)(last)


def rim_scratch(shape):
    dma = pltpu.SemaphoreType.DMA
    return [pltpu.VMEM(shape, BF16), dma((2,)), dma((2,)), dma((2,))]


def put_edges(group, ref, lead_ref, trail_ref):
    length = ref.shape[2]
    place = pl.program_id(0) % (group // TWO)
    for k in range(group // TWO):

        @pl.when(place == k)
        def _():
            for j in range(TWO):
                lanes = slice((k * TWO + j) * REACH, (k * TWO + j + 1) * REACH)
                lead_ref[0, :, lanes] = ref[j, :, :REACH]
                trail_ref[0, :, lanes] = ref[j, :, length - REACH :]


def middle_rims_kernel(group, lead_in, trail_in, first_ref, mask_ref, w_ref, p_ref, *rest):
    rim_steps(lead_in, trail_in, *rest[3:5], *rest[5:9])
    middle_kernel(group, False, None, first_ref, mask_ref, w_ref, p_ref, *rest[:3], *rest[9:])


def middle_rims_call(edges, first, mask, w_in, p2, count, group):
    _, _, length = first.shape
    seqs = mask.shape[0]
    edge = pl.BlockSpec((1, INNER, group * REACH), lambda i: (i // (group // TWO), 0, 0))
    edge_shape = sds((count // group, INNER, group * REACH), BF16)
    any_spec = pl.BlockSpec(memory_space=pl.ANY)

    def fixed(shape):
        return pl.BlockSpec(shape, lambda i: (0,) * len(shape), pipeline_mode=pl.Buffered(1))

    def mask_at(i):
        return (((lax.axis_index("ch") + 1) * (count // TWO) + i) % (seqs // TWO), 0, 0)

    return pl.pallas_call(
        functools.partial(middle_rims_kernel, group),
        grid=(count // TWO,),
        in_specs=[
            any_spec,
            any_spec,
            pl.BlockSpec((TWO, D, length), lambda i: (count // TWO + i, 0, 0)),
            pl.BlockSpec((TWO, 1, length), mask_at),
            fixed((INNER, D)),
            fixed((3, INNER, LANES)),
        ],
        out_specs=(pl.BlockSpec((TWO, INNER, length), lambda i: (i, 0, 0)), edge, edge, any_spec, any_spec),
        out_shape=(sds((count, INNER, length), BF16), *[edge_shape] * 4),
        scratch_shapes=rim_scratch(edge_shape.shape) + [pltpu.VMEM((INNER, length), F32)] * TWO,
        cost_estimate=cost_of(count * INNER * D * length * 1.5, count * (D + INNER * 3) * length * 2),
        compiler_params=pltpu.CompilerParams(vmem_limit_bytes=VMEM_BYTES, collective_id=4, has_side_effects=True),
    )(*edges, first, mask.reshape(seqs, 1, length), w_in, p2)


def middle_kernel(group, keep, pre, first_ref, mask_ref, w_ref, p_ref, mid_ref, lead_ref, trail_ref, *rest):
    nar_refs = rest[-TWO:]
    length = first_ref.shape[2]
    for j in range(TWO):
        nar = jnp.dot(w_ref[...], first_ref[j], preferred_element_type=F32)
        nar_refs[j][...] = nar + spread(p_ref[0], length)
    for j in range(TWO):
        nar_ref = nar_refs[j]
        mean, scale = norm_stats(lambda sl: nar_ref[sl, :], INNER, length)
        mask = mask_ref[j].astype(F32)

        def body(sl, carry):
            hat = (nar_ref[sl, :] - mean) * scale
            point = hat * spread(p_ref[1, sl, :], length) + spread(p_ref[2, sl, :], length)
            phi = cdf(point)
            mid_ref[j, sl, :] = (point * phi * mask).astype(BF16)
            if keep:
                rest[0][j, sl, :] = hat.astype(BF16)
                rest[1][j, sl, :] = slope(point, phi) * mask
            return carry

        straight(INNER, length, body, 0)
        if keep:
            rest[2][j] = scale
    put_edges(group, mid_ref, lead_ref, trail_ref)


def middle_call(pre, first, mask, w_in, p2, count, offset, group, keep):
    _, _, length = first.shape
    seqs = mask.shape[0]
    edge = pl.BlockSpec((1, INNER, group * REACH), lambda i, pre: (i // (group // TWO), 0, 0))
    edge_shape = sds((count // group, INNER, group * REACH), BF16)
    own = pl.BlockSpec((TWO, INNER, length), lambda i, pre: (i, 0, 0))
    outs = [own, edge, edge]
    shapes = [sds((count, INNER, length), BF16), edge_shape, edge_shape]
    if keep:
        outs += [own, own, pl.BlockSpec((TWO, 1, length), lambda i, pre: (i, 0, 0))]
        shapes += [
            sds((count, INNER, length), BF16),
            sds((count, INNER, length), F32),
            sds((count, 1, length), F32),
        ]
    return call(
        functools.partial(middle_kernel, group, keep),
        (count // TWO,),
        [
            pl.BlockSpec((TWO, D, length), lambda i, pre: (offset // TWO + i, 0, 0)),
            pl.BlockSpec((TWO, 1, length), lambda i, pre: (((pre[0] + offset) // TWO + i) % (seqs // TWO), 0, 0)),
            whole((INNER, D)),
            whole((3, INNER, LANES)),
        ],
        tuple(outs),
        tuple(shapes),
        scratch=[pltpu.VMEM((INNER, length), F32)] * TWO,
        cost=cost_of(count * INNER * D * length * 1.5, count * (D + INNER * 3) * length * 2),
    )(pre, first, mask.reshape(seqs, 1, length), w_in, p2)


def gather_windows(group, body_ref, before_ref, after_ref, pad_ref, cat_refs, order, step=None):
    width, length, count = body_ref.shape[1], body_ref.shape[2], len(cat_refs)
    place = (pl.program_id(0) if step is None else step) % (group // count)
    for k in range(group // count):

        @pl.when(place == k)
        def _():
            for j in range(count):
                lanes = slice((k * count + j) * REACH, (k * count + j + 1) * REACH)
                pad_ref[j, :, LANES - REACH : LANES] = before_ref[0, :, lanes]
                pad_ref[j, :, LANES + length : LANES + length + REACH] = after_ref[0, :, lanes]

    for j in range(count):
        pad_ref[j, :, LANES : LANES + length] = body_ref[j]
        for tap in range(KERNEL):
            start = LANES + order * (tap - KERNEL // 2) * DILATION
            cat_refs[j][tap * width : (tap + 1) * width, :] = pad_ref[j, :, start : start + length]


def last_kernel(
    group, keep, pre, mid_ref, before_ref, after_ref, x_ref, wc_ref, wo_ref, p_ref, b_ref, *rest
):
    if keep:
        mixed_ref, hat_ref, gp_ref, scale_ref, last_out = rest[:5]
        last_refs = [last_out.at[j] for j in range(TWO)]
    else:
        mixed_ref = rest[1]
        last_refs = rest[-TWO:]
        rest = rest[:-TWO]
    pad_ref, cat_refs, conv_refs = rest[-1 - 2 * TWO], rest[-2 * TWO : -TWO], rest[-TWO:]
    length = mid_ref.shape[2]
    gather_windows(group, mid_ref, before_ref, after_ref, pad_ref, cat_refs, 1)
    for j in range(TWO):
        conv = jnp.dot(wc_ref[...], cat_refs[j][...], preferred_element_type=F32)
        conv_refs[j][...] = conv + spread(p_ref[0], length)
    for j in range(TWO):
        conv_ref, last_ref = conv_refs[j], last_refs[j]
        mean, scale = norm_stats(lambda sl: conv_ref[sl, :], INNER, length)

        def body(sl, carry):
            hat = (conv_ref[sl, :] - mean) * scale
            point = hat * spread(p_ref[1, sl, :], length) + spread(p_ref[2, sl, :], length)
            phi = cdf(point)
            last_ref[sl, :] = (point * phi).astype(BF16)
            if keep:
                hat_ref[j, sl, :] = hat.astype(BF16)
                gp_ref[j, sl, :] = slope(point, phi)
            return carry

        straight(INNER, length, body, 0)
        if keep:
            scale_ref[j] = scale
        branch = jnp.dot(wo_ref[...], last_ref[...], preferred_element_type=F32)
        mixed_ref[j] = (x_ref[j].astype(F32) + branch + spread(b_ref[...], length)).astype(BF16)


def last_call(pre, mid, before, after, tokens, wc, wo_t, p2, b_out, count, offset, group, keep, mixed):
    _, _, length = mid.shape
    seqs, share = tokens.shape[0], wo_t.shape[0]
    edge = pl.BlockSpec((1, INNER, group * REACH), lambda i, pre: (i // (group // TWO), 0, 0))
    own = pl.BlockSpec((TWO, INNER, length), lambda i, pre: (i, 0, 0))

    def pair_at(i, pre):
        return ((pre[0] + offset) // TWO + i) % (seqs // TWO)

    outs = [pl.BlockSpec((TWO, share, length), lambda i, pre: (pair_at(i, pre), 0, 0))]
    shapes = [sds((seqs, share, length), BF16)]
    in_specs = [
        own,
        edge,
        edge,
        pl.BlockSpec((TWO, share, length), lambda i, pre: (pair_at(i, pre), pre[1], 0)),
        whole((INNER, KERNEL * INNER)),
        whole((share, INNER)),
        whole((3, INNER, LANES), 1),
        whole((share, LANES)),
    ]
    args = [pre, mid, before, after, tokens, wc, wo_t, p2, b_out]
    aliases = None
    scratch = [pltpu.VMEM((TWO, INNER, length + 2 * LANES), BF16)]
    scratch += [pltpu.VMEM((KERNEL * INNER, length), BF16)] * TWO
    scratch += [pltpu.VMEM((INNER, length), F32)] * TWO
    if keep:
        outs += [own, own, pl.BlockSpec((TWO, 1, length), lambda i, pre: (i, 0, 0)), own]
        saved = sds((count, INNER, length), BF16)
        shapes += [saved, sds((count, INNER, length), F32), sds((count, 1, length), F32), saved]
    else:
        scratch += [pltpu.VMEM((INNER, length), BF16)] * TWO
        in_specs.append(pl.BlockSpec(memory_space=pl.ANY))
        args.append(mixed)
        aliases = {len(args) - 1: 0}
    return call(
        functools.partial(last_kernel, group, keep),
        (count // TWO,),
        in_specs,
        tuple(outs),
        tuple(shapes),
        scratch=scratch,
        aliases=aliases,
        cost=cost_of(count * INNER * (KERNEL * INNER + share) * length * 1.3, count * share * 6 * length * 2),
    )(*args)


def side(ref, sl):
    return jnp.concatenate([ref[j, sl, :].astype(F32) for j in range(ref.shape[0])], axis=1)


def across(ref, row):
    return jnp.concatenate([ref[j, row : row + 1, :] for j in range(ref.shape[0])], axis=1)


def row_sums(ref):
    ones = jnp.ones((8, LANES), F32)
    return lax.dot_general(
        ones, ref[...], (((1,), (1,)), ((), ())), precision=lax.Precision.HIGHEST, preferred_element_type=F32
    )


def norm_back(d_ref, gp_ref, hat_ref, scale, gain_ref, gg_ref, gb_ref, sum_ref, put):
    wide = d_ref.shape[1]
    zero = jnp.zeros((8, wide), F32)

    def body(sl, carry):
        d_pre = d_ref[sl, :] * side(gp_ref, sl)
        hat = side(hat_ref, sl)
        gg_ref[sl, :] += fold_lanes(d_pre * hat)
        gb_ref[sl, :] += fold_lanes(d_pre)
        e = d_pre * spread(gain_ref[0, sl, :], wide)
        d_ref[sl, :] = e
        return carry[0] + fold_rows(e), carry[1] + fold_rows(e * hat)

    total, dot = straight(INNER, wide, body, (zero, zero))
    total = total.sum(0, keepdims=True) * (scale / INNER)
    dot = dot.sum(0, keepdims=True) * (scale / INNER)

    def finish(sl, carry):
        v = (d_ref[sl, :] * scale - total - side(hat_ref, sl) * dot).astype(BF16)
        put(sl, v)
        sum_ref[sl, :] += fold_lanes(v.astype(F32))
        return carry

    straight(INNER, wide, finish, 0)


def rear_kernel(group, chs, pre, *refs):
    dy_refs = refs[:chs]
    w_ref, hat_ref, gp_ref, last_ref, scale_ref, p_ref = refs[chs : chs + 6]
    dconv_ref, lead_ref, trail_ref, gg_ref, gb_ref, gc_ref, gw_ref, go_ref = refs[chs + 6 : chs + 14]
    rows_ref, dy_ref, d_ref = refs[chs + 14 :]
    share, length = dy_refs[0].shape[1], dy_refs[0].shape[2]

    @pl.when(pl.program_id(0) == 0)
    def _():
        for ref in (gg_ref, gb_ref, gc_ref, gw_ref, go_ref):
            ref[...] = jnp.zeros_like(ref)

    for r in range(chs):
        at = pl.multiple_of(((pre[1] + chs - r) % chs) * share, share)
        for j in range(TWO):
            dy_ref[pl.ds(at, share), j * length : (j + 1) * length] = dy_refs[r][j]
    d_ref[...] = jnp.dot(w_ref[...], dy_ref[...], preferred_element_type=F32)
    last = jnp.concatenate([last_ref[j] for j in range(TWO)], axis=1)
    gw_ref[...] += lax.dot_general(last, dy_ref[...], (((1,), (1,)), ((), ())), preferred_element_type=F32)
    go_ref[...] += fold_lanes(dy_ref[...].astype(F32))

    def put(sl, v):
        for j in range(TWO):
            dconv_ref[j, sl, :] = v[:, j * length : (j + 1) * length]

    norm_back(d_ref, gp_ref, hat_ref, across(scale_ref, 0), p_ref, gg_ref, gb_ref, gc_ref, put)
    put_edges(group, dconv_ref, lead_ref, trail_ref)

    @pl.when(pl.program_id(0) == pl.num_programs(0) - 1)
    def _():
        for k, ref in enumerate((gc_ref, gg_ref, gb_ref)):
            rows_ref[:, k * INNER : (k + 1) * INNER] = row_sums(ref)
        rows_ref[:, 3 * INNER :] = row_sums(go_ref)


def const(shape):
    return pl.BlockSpec(shape, lambda i, pre: (0,) * len(shape), pipeline_mode=pl.Buffered(1))


def rear_call(pre, cot, others, w_out, hat, gp, last, scale, p2, group):
    seqs, share, length = cot.shape
    count = hat.shape[0]
    chs = 1 + len(others)
    edge = pl.BlockSpec((1, INNER, group * REACH), lambda i, pre: (i // (group // TWO), 0, 0))
    edge_shape = sds((count // group, INNER, group * REACH), BF16)
    own = pl.BlockSpec((TWO, INNER, length), lambda i, pre: (i, 0, 0))
    sums = [(INNER, LANES)] * 3 + [(INNER, D), (D, LANES), (8, 3 * INNER + D)]
    return call(
        functools.partial(rear_kernel, group, chs),
        (count // TWO,),
        [pl.BlockSpec((TWO, share, length), lambda i, pre: (pre[0] // TWO + i, 0, 0))]
        + [pl.BlockSpec((TWO, share, length), lambda i, pre: (i, 0, 0))] * (chs - 1)
        + [
            whole((INNER, D)),
            own,
            own,
            own,
            pl.BlockSpec((TWO, 1, length), lambda i, pre: (i, 0, 0)),
            whole((1, INNER, LANES), 4),
        ],
        tuple([own, edge, edge] + [const(v) for v in sums]),
        tuple([sds((count, INNER, length), BF16), edge_shape, edge_shape] + [sds(v, F32) for v in sums]),
        scratch=[pltpu.VMEM((D, TWO * length), BF16), pltpu.VMEM((INNER, TWO * length), F32)],
        cost=cost_of(count * INNER * D * length * 2.5, count * INNER * 5 * length * 2),
    )(pre, cot, *others, w_out, hat, gp, last, scale, p2)


def front_kernel(group, chs, pre, *refs):
    dconv_ref, before_ref, after_ref, mid_ref, hat_ref, gp_ref, scale_ref = refs[:7]
    x_ref, stat_ref, dy_ref, wc_ref, wi_ref, p2_ref, p1_ref = refs[7:14]
    refs = refs[14:]
    gt_ref = refs[0]
    send_refs = refs[1:chs]
    gcw_ref, gwi_ref, gg2_ref, gb2_ref, gbi_ref, gg1_ref, gb1_ref = refs[chs : chs + 7]
    pad_ref, cat_ref, d_ref, dn_ref, df_ref, first_ref = refs[chs + 7 :]
    share, length = dy_ref.shape[1], dy_ref.shape[2]
    wide = TWO * length

    @pl.when(pl.program_id(0) == 0)
    def _():
        for ref in (gcw_ref, gwi_ref, gg2_ref, gb2_ref, gbi_ref, gg1_ref, gb1_ref):
            ref[...] = jnp.zeros_like(ref)

    cats = [cat_ref.at[:, j * length : (j + 1) * length] for j in range(TWO)]
    gather_windows(group, dconv_ref, before_ref, after_ref, pad_ref, cats, -1)
    d_ref[...] = jnp.dot(wc_ref[...], cat_ref[...], preferred_element_type=F32)
    mid = jnp.concatenate([mid_ref[j] for j in range(TWO)], axis=1)
    gcw_ref[...] += lax.dot_general(cat_ref[...], mid, (((1,), (1,)), ((), ())), preferred_element_type=F32)

    def put(sl, v):
        dn_ref[sl, :] = v

    norm_back(d_ref, gp_ref, hat_ref, across(scale_ref, 0), p2_ref, gg2_ref, gb2_ref, gbi_ref, put)
    df_ref[...] = jnp.dot(wi_ref[...], dn_ref[...], preferred_element_type=F32)
    mean_in, scale_in = across(stat_ref, 0), across(stat_ref, 1)
    zero = jnp.zeros((8, wide), F32)

    def inner(sl, carry):
        hat = (side(x_ref, sl) - mean_in) * scale_in
        gain = spread(p1_ref[0, sl, :], wide)
        point = hat * gain + spread(p1_ref[1, sl, :], wide)
        phi = cdf(point)
        first_ref[sl, :] = (point * phi).astype(BF16)
        d_pre = df_ref[sl, :] * slope(point, phi)
        gg1_ref[sl, :] += fold_lanes(d_pre * hat)
        gb1_ref[sl, :] += fold_lanes(d_pre)
        e = d_pre * gain
        df_ref[sl, :] = e
        return carry[0] + fold_rows(e), carry[1] + fold_rows(e * hat)

    total, dot = straight(D, wide, inner, (zero, zero))
    total = total.sum(0, keepdims=True) * (scale_in / D)
    dot = dot.sum(0, keepdims=True) * (scale_in / D)
    gwi_ref[...] += lax.dot_general(
        dn_ref[...], first_ref[...], (((1,), (1,)), ((), ())), preferred_element_type=F32
    )
    for r in range(chs):
        base = ((pre[1] + r) % chs) * share

        def out(to, carry):
            rows = pl.ds(pl.multiple_of(base + to.start, 16), to.size)
            hat = (side(x_ref, rows) - mean_in) * scale_in
            v = df_ref[rows, :] * scale_in - total - hat * dot
            for j in range(TWO):
                half = v[:, j * length : (j + 1) * length]
                if r == 0:
                    gt_ref[j, to, :] = half + dy_ref[j, to, :].astype(F32)
                else:
                    send_refs[r - 1][j, to, :] = half.astype(BF16)
            return carry

        straight(share, wide, out, 0)


def front_call(pre, dconv, before, after, mid, hat, gp, scale, tokens, stat, cot, wc_t, wi_t, p2, p1, chs, group):
    seqs, share, length = cot.shape
    count = dconv.shape[0]
    edge = pl.BlockSpec((1, INNER, group * REACH), lambda i, pre: (i // (group // TWO), 0, 0))
    own = pl.BlockSpec((TWO, INNER, length), lambda i, pre: (i, 0, 0))

    def seq_block(rows):
        return pl.BlockSpec((TWO, rows, length), lambda i, pre: (pre[0] // TWO + i, 0, 0))

    inner_part, outer_part = (INNER, LANES), (D, LANES)
    sums = [(KERNEL * INNER, INNER), (INNER, D), inner_part, inner_part, inner_part, outer_part, outer_part]
    wide = TWO * length
    return call(
        functools.partial(front_kernel, group, chs),
        (count // TWO,),
        [
            own,
            edge,
            edge,
            own,
            own,
            own,
            pl.BlockSpec((TWO, 1, length), lambda i, pre: (i, 0, 0)),
            seq_block(D),
            pl.BlockSpec((TWO, 2, length), lambda i, pre: (i, 0, 0)),
            seq_block(share),
            whole((INNER, KERNEL * INNER)),
            whole((D, INNER)),
            whole((1, INNER, LANES), 1),
            whole((2, D, LANES)),
        ],
        tuple(
            [seq_block(share)]
            + [pl.BlockSpec((TWO, share, length), lambda i, pre: (i, 0, 0))] * (chs - 1)
            + [const(v) for v in sums]
        ),
        tuple(
            [sds((seqs, share, length), F32)]
            + [sds((count, share, length), BF16)] * (chs - 1)
            + [sds(v, F32) for v in sums]
        ),
        scratch=[
            pltpu.VMEM((TWO, INNER, length + 2 * LANES), BF16),
            pltpu.VMEM((KERNEL * INNER, wide), BF16),
            pltpu.VMEM((INNER, wide), F32),
            pltpu.VMEM((INNER, wide), BF16),
            pltpu.VMEM((D, wide), F32),
            pltpu.VMEM((D, wide), BF16),
        ],
        cost=cost_of(count * INNER * (2 * KERNEL * INNER + 2 * D) * length * 1.3, count * D * 8 * length * 2),
    )(pre, dconv, before, after, mid, hat, gp, scale, tokens, stat, cot, wc_t, wi_t, p2, p1)


def add_kernel(pre, part_ref, dy_ref, _, gt_ref):
    gt_ref[...] = part_ref[...].astype(F32) + dy_ref[...].astype(F32)


def add_call(pre, part, cot, gt, start):
    seqs, share, length = cot.shape
    count = part.shape[0]
    at = lambda i, pre: (pre[start] + i, 0, 0)
    return call(
        add_kernel,
        (count,),
        [
            pl.BlockSpec((1, share, length), lambda i, pre: (i, 0, 0)),
            pl.BlockSpec((1, share, length), at),
            pl.BlockSpec(memory_space=pl.ANY),
        ],
        pl.BlockSpec((1, share, length), at),
        sds((seqs, share, length), F32),
        aliases={3: 0},
        cost=cost_of(count * share * length, count * share * length * 8),
    )(pre, part, cot, gt)


def turned(square):
    unit = (
        lax.broadcasted_iota(jnp.int32, (INNER, INNER), 0) == lax.broadcasted_iota(jnp.int32, (INNER, INNER), 1)
    ).astype(F32).astype(BF16)
    return lax.dot_general(unit, square, (((1,), (1,)), ((), ())), preferred_element_type=F32).astype(BF16)


def turn_kernel(pre, w_ref, flat_ref, turned_ref):
    flat_ref[...] = w_ref[0]
    turned_ref[...] = turned(w_ref[0])


def turn_rims_kernel(lead, trail, w_ref, flat_ref, turned_ref, *rest):
    rim_steps(lead, trail, *rest)
    turn_kernel(None, w_ref, flat_ref, turned_ref)


def turn_call(pre, conv, edges=None):
    shape = sds((INNER, KERNEL * INNER), BF16)
    if edges is not None:
        any_spec = pl.BlockSpec(memory_space=pl.ANY)
        column = pl.BlockSpec((INNER, INNER), lambda k: (0, k))
        return pl.pallas_call(
            turn_rims_kernel,
            grid=(KERNEL,),
            in_specs=[any_spec, any_spec, pl.BlockSpec((1, INNER, INNER), lambda k: (k, 0, 0))],
            out_specs=(column, column, any_spec, any_spec),
            out_shape=(shape, shape, *[sds(e.shape, BF16) for e in edges]),
            scratch_shapes=rim_scratch(edges[0].shape),
            cost_estimate=cost_of(KERNEL * INNER**3, KERNEL * INNER * INNER * 6),
            compiler_params=pltpu.CompilerParams(
                vmem_limit_bytes=VMEM_BYTES, collective_id=3, has_side_effects=True
            ),
        )(*edges, conv)
    block = pl.BlockSpec((INNER, INNER), lambda k, pre: (0, k))
    return call(
        turn_kernel,
        (KERNEL,),
        [pl.BlockSpec((1, INNER, INNER), lambda k, pre: (k, 0, 0))],
        (block, block),
        (shape, shape),
        cost=cost_of(KERNEL * INNER**3, KERNEL * INNER * INNER * 6),
    )(pre, conv)


ORDERS = ((0, 1, 2, 3), (0, 1, 2, 3), (0, 2, 3, 1), (0, 1, 2, 3), (0, 1, 2, 3))
GIVE = 5
SCHEDULE = {
    1: [(5, 0), (0, 0)],
    2: [(2, 0), (0, 1), (1, 0)],
    3: [(5, 1), (2, 1)],
    5: [(1, 1), (3, 0)],
    7: [(0, 2), (2, 2), (5, 2)],
    8: [(3, 1)],
    9: [(1, 2), (5, 3)],
    10: [(0, 3)],
    12: [(5, 4), (2, 3), (3, 2), (1, 3), (0, 4), (4, 0), (0, 5), (4, 1), (2, 4), (5, 5), (3, 3), (1, 4)],
    13: [(4, 2)],
    14: [(1, 5), (0, 6), (3, 4), (2, 5), (4, 3), (1, 6), (0, 7), (3, 5), (5, 6)],
    15: [(2, 6), (1, 7), (3, 6)],
    16: [(4, 4), (4, 5), (2, 7), (0, 8), (3, 7), (5, 7), (1, 8), (0, 9), (4, 6), (5, 8), (4, 7), (2, 8), (3, 8), (4, 8), (5, 9), (1, 9), (4, 9), (2, 9), (3, 9)],
}


class Stream:
    def __init__(self, order, first, rows, arrays, slot):
        self.order, self.rows = order, rows
        self.acc, self.send, self.recv, self.swap, self.res, self.sems = arrays
        self.slot = slot
        self.levels = len(order)
        self.size = [rows >> (t + 1) for t in range(self.levels)]
        self.at = [rows - (rows >> t) for t in range(self.levels)]
        self.seq, self.ch = lax.axis_index("seq"), lax.axis_index("ch")
        self.low = [first]
        for t in range(self.levels):
            self.low.append(self.low[-1] + self.bit(order[t]) * self.size[t])

    def bit(self, b):
        return (self.seq // (1 << b)) % 2

    def partner(self, b):
        return {"seq": self.seq + (1 - 2 * self.bit(b)) * (1 << b)}

    def remote(self, src, dst, k, device):
        return pltpu.make_async_remote_copy(
            src_ref=src,
            dst_ref=dst,
            send_sem=self.sems[0].at[self.slot, k],
            recv_sem=self.sems[1].at[self.slot, k],
            device_id=device,
            device_id_type=pl.DeviceIdType.MESH,
        )

    def copy(self, k):
        if k < self.levels:
            window = pl.ds(self.at[k], self.size[k])
            held = self.send.at[:, pl.ds(0, self.size[k]), :]
            return self.remote(held, self.recv.at[:, window, :], k, self.partner(self.order[k]))
        if k == self.levels:
            return self.remote(self.swap.at[0], self.swap.at[1], k, {"ch": 1 - self.ch})
        t = 2 * self.levels - k
        place = spot(self.low[t + 1], 0, self.size[t])
        return self.remote(self.res.at[place, :], self.res.at[place, :], k, self.partner(self.order[t]))

    def start(self, k):
        if k < self.levels:
            away = self.low[k] + (1 - self.bit(self.order[k])) * self.size[k]
            for h in range(2):

                def pack(i, step, h=h):
                    self.send[h, spot(0, i, step), :] = self.acc[h, spot(away, i, step), :].astype(BF16)

                sliced(self.size[k], pack)
        elif k == self.levels:
            place = spot(self.low[-1], 0, self.size[-1])
            self.swap[0] = self.acc[1 - self.ch, place, :].astype(BF16)
        self.copy(k).start()

    def finish(self, k):
        self.copy(k).wait()
        if k < self.levels:
            for h in range(2):

                def add(i, step, h=h):
                    place = spot(self.low[k + 1], i, step)
                    self.acc[h, place, :] += self.recv[h, spot(self.at[k], i, step), :].astype(F32)

                sliced(self.size[k], add)
        elif k == self.levels:
            place = spot(self.low[-1], 0, self.size[-1])
            self.res[place, :] = (self.acc[self.ch, place, :] + self.swap[1].astype(F32)).astype(BF16)


def sliced(count, body):
    step = next(r for r in (96, 64, 48, 32, 16) if count % r == 0)

    def one(i, carry):
        body(pl.multiple_of(i * step, 16), step)
        return carry

    lax.fori_loop(0, count // step, one, 0)


def spot(base, i, step):
    return pl.ds(pl.multiple_of(base + i, 16), step)


HALF = INNER // 2
LEVELS = 4
EARLY_ROWS = HALF * (KERNEL + D // INNER)
ROWS = 768
SMALL_ROWS = 256


def stream_scratch():
    dma = pltpu.SemaphoreType.DMA
    out = [pltpu.VMEM((2, 4 * ROWS, INNER), F32)]
    moved = ROWS - (ROWS >> LEVELS)
    out += [pltpu.VMEM((2, ROWS // 2, INNER), BF16)] * 4
    out += [pltpu.VMEM((2, moved, INNER), BF16)] * 4
    out += [pltpu.VMEM((2, ROWS >> LEVELS, INNER), BF16)] * 4
    out += [pltpu.VMEM((4 * ROWS, INNER), BF16)]
    out += [
        pltpu.VMEM((2, SMALL_ROWS, LANES), F32),
        pltpu.VMEM((2, SMALL_ROWS // 2, LANES), BF16),
        pltpu.VMEM((2, SMALL_ROWS - (SMALL_ROWS >> LEVELS), LANES), BF16),
        pltpu.VMEM((2, SMALL_ROWS >> LEVELS, LANES), BF16),
        pltpu.VMEM((SMALL_ROWS, LANES), BF16),
    ]
    out += [dma((2 * (KERNEL + 2 * D // INNER),)), dma((5, 2 * LEVELS + 1)), dma((5, 2 * LEVELS + 1))]
    return out


def streams_of(refs):
    acc, send, recv, swap, res = refs[0], refs[1:5], refs[5:9], refs[9:13], refs[13]
    sems = refs[20:22]
    out = []
    for q, order in enumerate(ORDERS[:4]):
        out.append(Stream(order, q * ROWS, ROWS, (acc, send[q], recv[q], swap[q], res, sems), q))
    out.append(Stream(ORDERS[4], 0, SMALL_ROWS, (*refs[14:19], sems), 4))
    return out


def inner_kernel(group, pre, *refs):
    dconv_ref, before_ref, after_ref, mid_ref, hat_ref, gp_ref, scale_ref, first_ref, wc_ref, p2_ref = refs[:10]
    dn_ref, gcw_ref, gwi_ref, rows_ref = refs[10:14]
    pad_ref, cat_ref, d_ref, gg_ref, gb_ref, gbi_ref = refs[14:]
    length = mid_ref.shape[2]

    @pl.when(pl.program_id(0) == 0)
    def _():
        for ref in (gcw_ref, gwi_ref, gg_ref, gb_ref, gbi_ref):
            ref[...] = jnp.zeros_like(ref)

    cats = [cat_ref.at[:, j * length : (j + 1) * length] for j in range(TWO)]
    gather_windows(group, dconv_ref, before_ref, after_ref, pad_ref, cats, -1)
    d_ref[...] = jnp.dot(wc_ref[...], cat_ref[...], preferred_element_type=F32)
    mid = jnp.concatenate([mid_ref[j] for j in range(TWO)], axis=1)
    gcw_ref[...] += lax.dot_general(cat_ref[...], mid, (((1,), (1,)), ((), ())), preferred_element_type=F32)

    def put(sl, v):
        for j in range(TWO):
            dn_ref[j, sl, :] = v[:, j * length : (j + 1) * length]

    norm_back(d_ref, gp_ref, hat_ref, across(scale_ref, 0), p2_ref, gg_ref, gb_ref, gbi_ref, put)
    dn = jnp.concatenate([dn_ref[j] for j in range(TWO)], axis=1)
    first = jnp.concatenate([first_ref[j] for j in range(TWO)], axis=1)
    gwi_ref[...] += lax.dot_general(dn, first, (((1,), (1,)), ((), ())), preferred_element_type=F32)

    @pl.when(pl.program_id(0) == pl.num_programs(0) - 1)
    def _():
        for k, ref in enumerate((gbi_ref, gg_ref, gb_ref)):
            rows_ref[:, k * INNER : (k + 1) * INNER] = row_sums(ref)


def inner_call(pre, dconv, before, after, mid, hat, gp, scale, first, wc_t, p2, group):
    count, _, length = dconv.shape
    edge = pl.BlockSpec((1, INNER, group * REACH), lambda i, pre: (i // (group // TWO), 0, 0))
    own = pl.BlockSpec((TWO, INNER, length), lambda i, pre: (i, 0, 0))
    sums = [(KERNEL * INNER, INNER), (INNER, D), (8, 3 * INNER)]
    return call(
        functools.partial(inner_kernel, group),
        (count // TWO,),
        [
            own,
            edge,
            edge,
            own,
            own,
            own,
            pl.BlockSpec((TWO, 1, length), lambda i, pre: (i, 0, 0)),
            pl.BlockSpec((TWO, D, length), lambda i, pre: (i, 0, 0)),
            whole(wc_t.shape),
            whole((1, INNER, LANES), 1),
        ],
        tuple([own] + [const(v) for v in sums]),
        tuple([sds(dconv.shape, BF16)] + [sds(v, F32) for v in sums]),
        scratch=[
            pltpu.VMEM((TWO, INNER, length + 2 * LANES), BF16),
            pltpu.VMEM((KERNEL * INNER, TWO * length), BF16),
            pltpu.VMEM((INNER, TWO * length), F32),
        ]
        + [pltpu.VMEM((INNER, LANES), F32)] * 3,
        cost=cost_of(count * (2 * KERNEL * INNER + D) * INNER * length, KERNEL * INNER * INNER * 4),
    )(pre, dconv, before, after, mid, hat, gp, scale, first, wc_t, p2)


KINDS = [0, 0, 0, 0, 0, 0, 1, 0, 0, 1, 1, 1, 1, 1, 1, 1]


def turn_of(kind, step):
    steps = [k for k, v in enumerate(KINDS) if v == kind]
    return sum((jnp.asarray(step >= k).astype(jnp.int32) for k in steps[1:]), jnp.int32(0))


def is_turn(kind, step):
    return functools.reduce(jnp.logical_or, (step == k for k, v in enumerate(KINDS) if v == kind))


def tail_kernel(group, *refs):
    dn_ref, x_ref, stat_ref, mid_ref, lead_oth, trail_oth, wc_ref, wi_ref, p1_ref, p2_ref = refs[:10]
    rows_ref, rows_in_ref, gcw_ref, gwo_ref, gwi_ref = refs[10:15]
    w_in_ref, wi_ref = wi_ref, refs[-1]
    refs = refs[:-1]
    mine_ref, last_ref, total_ref, small_ref, got_ref = refs[15:20]
    stream_refs = refs[20:42]
    pad_ref, cat_ref, d_ref, give_ref, df_ref = refs[42:47]
    gg1_ref, gb1_ref, give_send, give_recv = refs[47:51]
    before_oth, after_oth, rim_send, rim_recv = refs[51:]
    rims = Rims(lead_oth, trail_oth, before_oth, after_oth, rim_send, rim_recv)
    acc, small_acc, res, small_res, load_sem = (stream_refs[k] for k in (0, 14, 13, 18, 19))
    base = 3 * ROWS
    share, length = give_ref.shape[1], give_ref.shape[2]
    seq, ch = lax.axis_index("seq"), lax.axis_index("ch")
    step, steps = pl.program_id(0), pl.num_programs(0)
    count = give_ref.shape[0]
    streams = streams_of(stream_refs)
    outer_now, conv_now = turn_of(0, step), turn_of(1, step)

    def loads():
        out = []
        for h in range(2):
            mine = pl.ds(h * HALF, HALF)
            pieces = [gcw_ref.at[k, mine, :] for k in range(KERNEL)]
            pieces += [gwo_ref.at[mine, pl.ds(j * INNER, INNER)] for j in range(D // INNER)]
            for j, piece in enumerate(pieces):
                out.append((piece, acc.at[h, pl.ds(j * HALF, HALF), :]))
            for j in range(D // INNER):
                piece = gwi_ref.at[mine, pl.ds(j * INNER, INNER)]
                out.append((piece, acc.at[h, pl.ds(base + j * HALF, HALF), :]))
        return [pltpu.make_async_copy(a, b, load_sem.at[j]) for j, (a, b) in enumerate(out)]

    def give(i):
        return pltpu.make_async_remote_copy(
            src_ref=give_ref.at[i],
            dst_ref=got_ref.at[i],
            send_sem=give_send.at[i],
            recv_sem=give_recv.at[i],
            device_id={"ch": 1 - ch},
            device_id_type=pl.DeviceIdType.MESH,
        )

    def fill_inner():
        inner = [ref[0:1, k * INNER : (k + 1) * INNER] for ref in (rows_in_ref, rows_ref) for k in range(3)]
        at = base + HALF * D // INNER
        for h in range(2):
            for k, v in enumerate(inner):
                acc[h, at + k : at + k + 1, :HALF] = v[:, h * HALF : (h + 1) * HALF]

    def fill_outer():
        small_acc[...] = jnp.zeros_like(small_acc)
        outer = [row_sums(ref)[0:1] for ref in (gg1_ref, gb1_ref)] + [rows_ref[0:1, 3 * INNER :]]
        for h in range(2):
            for k, v in enumerate(outer):
                for j in range(INNER // LANES):
                    lanes = slice(h * INNER + j * LANES, h * INNER + (j + 1) * LANES)
                    row = k * (INNER // LANES) + j
                    small_acc[h, row : row + 1, :] = v[:, lanes]

    def act(actions):
        for q, k in actions:
            if q == GIVE:
                if k > 1:
                    give(k - 2).wait()
                if k < count:
                    give(k).start()
                continue
            if k > 0:
                streams[q].finish(k - 1)
            elif q == 3:
                fill_inner()
            elif q == 4:
                fill_outer()
            if k <= 2 * LEVELS:
                streams[q].start(k)

    @pl.when(step == 0)
    def _():
        for h in range(2):
            acc[h, EARLY_ROWS:base, :] = jnp.zeros((base - EARLY_ROWS, INNER), F32)
            used = base + HALF * D // INNER
            acc[h, used:, :] = jnp.zeros((4 * ROWS - used, INNER), F32)
        for copy in loads():
            copy.start()
        before_oth[...] = jnp.zeros_like(before_oth)
        after_oth[...] = jnp.zeros_like(after_oth)
        barrier = pltpu.get_barrier_semaphore()
        for device in [streams[0].partner(b) for b in range(LEVELS)] + [{"ch": 1 - ch}]:
            pl.semaphore_signal(barrier, inc=1, device_id=device, device_id_type=pl.DeviceIdType.MESH)
        pl.semaphore_wait(barrier, LEVELS + 1 + rims.greet())
        rims.start()
        for ref in (gg1_ref, gb1_ref):
            ref[...] = jnp.zeros_like(ref)
        for j in range(D // INNER):
            block = slice(j * INNER, (j + 1) * INNER)
            wi_ref[block, :] = turned(w_in_ref[:, block])

    @pl.when(step == min(SCHEDULE))
    def _():
        for copy in loads():
            copy.wait()

    for at, actions in SCHEDULE.items():
        if at < len(KINDS):

            @pl.when(step == at)
            def _():
                act(actions)

    @pl.when(is_turn(0, step))
    def _():
        now = outer_now
        df_ref[...] = jnp.dot(wi_ref[...], dn_ref[0], preferred_element_type=F32)
        mean_in, scale_in = stat_ref[0, 0:1, :], stat_ref[0, 1:2, :]
        zero = jnp.zeros((8, length), F32)

        def inner(sl, carry):
            hat = (x_ref[0, sl, :].astype(F32) - mean_in) * scale_in
            gain = spread(p1_ref[0, sl, :], length)
            point = hat * gain + spread(p1_ref[1, sl, :], length)
            d_pre = df_ref[sl, :] * slope(point, cdf(point))
            gg1_ref[sl, :] += fold_lanes(d_pre * hat)
            gb1_ref[sl, :] += fold_lanes(d_pre)
            e = d_pre * gain
            df_ref[sl, :] = e
            return carry[0] + fold_rows(e), carry[1] + fold_rows(e * hat)

        total, dot = straight(D, length, inner, (zero, zero))
        total = total.sum(0, keepdims=True) * (scale_in / D)
        dot = dot.sum(0, keepdims=True) * (scale_in / D)
        for r in range(2):
            start = ((ch + r) % 2) * share

            def out(to, carry):
                rows = pl.ds(pl.multiple_of(start + to.start, 16), to.size)
                hat = (x_ref[0, rows, :].astype(F32) - mean_in) * scale_in
                v = (df_ref[rows, :] * scale_in - total - hat * dot).astype(BF16)
                if r == 0:
                    mine_ref[0, to, :] = v
                else:
                    give_ref[now, to, :] = v
                return carry

            straight(share, length, out, 0)

    pl.when(step == KINDS.index(1))(rims.wait)

    @pl.when(is_turn(1, step))
    def _():
        held = pl.ds(conv_now // group, 1)
        gather_windows(group, mid_ref, before_oth.at[held], after_oth.at[held], pad_ref, [cat_ref], 1, conv_now)
        conv = jnp.dot(wc_ref[...], cat_ref[...], preferred_element_type=F32)
        d_ref[...] = conv + spread(p2_ref[3], length)
        mean, scale = norm_stats(lambda sl: d_ref[sl, :], INNER, length)

        def body(sl, carry):
            hat = (d_ref[sl, :] - mean) * scale
            point = hat * spread(p2_ref[4, sl, :], length) + spread(p2_ref[5, sl, :], length)
            last_ref[0, sl, :] = (point * cdf(point)).astype(BF16)
            return carry

        straight(INNER, length, body, 0)

    @pl.when(step == steps - 1)
    def _():
        act(SCHEDULE[max(SCHEDULE)])
        done = [
            pltpu.make_async_copy(res, total_ref, load_sem.at[0]),
            pltpu.make_async_copy(small_res, small_ref, load_sem.at[1]),
        ]
        for copy in done:
            copy.start()
        for copy in done:
            copy.wait()


def tail_call(dn, tokens, stat, mid, rims_oth, wc, w_in, p1, p2, rows, rows_in, gcw, gwo, gwi, group):
    count, _, length = dn.shape
    share = D // 2
    any_spec = pl.BlockSpec(memory_space=pl.ANY)

    def fixed(shape):
        return pl.BlockSpec(shape, lambda i: (0,) * len(shape), pipeline_mode=pl.Buffered(1))

    def block(k, width):
        return pl.BlockSpec((1, width, length), lambda i: (turn_of(k, i), 0, 0))

    dma = pltpu.SemaphoreType.DMA
    return pl.pallas_call(
        functools.partial(tail_kernel, group),
        grid=(len(KINDS),),
        in_specs=[
            block(0, INNER),
            pl.BlockSpec((1, D, length), lambda i: (lax.axis_index("ch") * count + turn_of(0, i), 0, 0)),
            block(0, 2),
            block(1, INNER),
            any_spec,
            any_spec,
            fixed(wc.shape),
            fixed(w_in.shape),
            fixed(p1.shape),
            fixed(p2.shape),
            fixed(rows.shape),
            fixed(rows_in.shape),
            any_spec,
            any_spec,
            any_spec,
        ],
        out_specs=(block(0, share), block(1, INNER), any_spec, any_spec, any_spec),
        out_shape=(
            sds((count, share, length), BF16),
            sds((count, INNER, length), BF16),
            sds((4 * ROWS, INNER), BF16),
            sds((SMALL_ROWS, LANES), BF16),
            sds((count, share, length), BF16),
        ),
        scratch_shapes=stream_scratch()
        + [
            pltpu.VMEM((1, INNER, length + 2 * LANES), BF16),
            pltpu.VMEM((KERNEL * INNER, length), BF16),
            pltpu.VMEM((INNER, length), F32),
            pltpu.VMEM((count, share, length), BF16),
            pltpu.VMEM((D, length), F32),
            pltpu.VMEM((D, LANES), F32),
            pltpu.VMEM((D, LANES), F32),
            dma((count,)),
            dma((count,)),
            pltpu.VMEM(rims_oth[0].shape, BF16),
            pltpu.VMEM(rims_oth[0].shape, BF16),
            dma((2,)),
            dma((2,)),
            pltpu.VMEM((D, INNER), BF16),
        ],
        cost_estimate=cost_of(count * INNER * (KERNEL * INNER + D) * length * 4, 4 * ROWS * INNER * 12),
        compiler_params=pltpu.CompilerParams(
            vmem_limit_bytes=TAIL_BYTES, collective_id=2, has_side_effects=True
        ),
    )(dn, tokens, stat, mid, *rims_oth, wc, w_in, p1, p2, rows, rows_in, gcw, gwo, gwi)


TAIL_BYTES = 63 * 1024 * 1024


def finish_kernel(pre, mine_ref, got_ref, dy_ref, last_ref, x_ref, wo_ref, b_ref, total_ref, small_ref, _, *outs):
    gt_ref, mixed_ref, gcw_ref, gwi_ref, gwo_ref, inner_ref, outer_ref = outs
    length = dy_ref.shape[2]
    step, count = pl.program_id(0), pl.num_programs(0) // 2
    part = gcw_ref.shape[1]

    @pl.when(step < count)
    def _():
        gt_ref[...] = mine_ref[...].astype(F32) + dy_ref[...].astype(F32)

    @pl.when(step >= count)
    def _():
        gt_ref[...] = got_ref[...].astype(F32) + dy_ref[...].astype(F32)
        for j in range(TWO):
            branch = jnp.dot(wo_ref[...], last_ref[j], preferred_element_type=F32)
            mixed_ref[j] = (x_ref[j].astype(F32) + branch + spread(b_ref[...], length)).astype(BF16)

    for k in range(KERNEL):

        @pl.when(step == k // TWO)
        def _():
            gcw_ref[k] = total_ref[k * part : (k + 1) * part, :].astype(F32)

    for k, (ref, start) in enumerate(((gwo_ref, KERNEL * part), (gwi_ref, 3 * ROWS))):

        @pl.when(step == KERNEL // TWO + 1 + k)
        def _():
            for j in range(D // INNER):
                ref[:, j * INNER : (j + 1) * INNER] = total_ref[start + j * part : start + (j + 1) * part, :].astype(F32)

    @pl.when(step == 0)
    def _():
        at = 3 * ROWS + part * D // INNER
        inner_ref[...] = total_ref[at : at + 16, :].astype(F32)
        outer_ref[...] = small_ref[:16, :].astype(F32)


def finish_call(pre, mine, got, cot, last, tokens, wo_t, b_out, total, small, mixed, part):
    seqs, share, length = cot.shape
    count = got.shape[0] // TWO
    early = lambda i: jnp.minimum(i, count - 1)
    late = lambda i: jnp.maximum(i - count, 0)
    return call(
        finish_kernel,
        (2 * count,),
        [
            pl.BlockSpec((TWO, share, length), lambda i, pre: (early(i), 0, 0)),
            pl.BlockSpec((TWO, share, length), lambda i, pre: (late(i), 0, 0)),
            pl.BlockSpec((TWO, share, length), lambda i, pre: ((pre[0] // TWO + i) % (seqs // TWO), 0, 0)),
            pl.BlockSpec((TWO, INNER, length), lambda i, pre: (late(i), 0, 0)),
            pl.BlockSpec((TWO, share, length), lambda i, pre: (pre[2] // TWO + late(i), pre[1], 0)),
            whole(wo_t.shape),
            whole(b_out.shape),
            whole(total.shape),
            whole(small.shape),
            pl.BlockSpec(memory_space=pl.ANY),
        ],
        (
            pl.BlockSpec((TWO, share, length), lambda i, pre: ((pre[0] // TWO + i) % (seqs // TWO), 0, 0)),
            pl.BlockSpec((TWO, share, length), lambda i, pre: (pre[2] // TWO + late(i), 0, 0)),
            const((KERNEL, part, INNER)),
            const((part, D)),
            const((part, D)),
            const((16, INNER)),
            const((16, LANES)),
        ),
        (
            sds((seqs, share, length), F32),
            sds(mixed.shape, BF16),
            sds((KERNEL, part, INNER), F32),
            sds((part, D), F32),
            sds((part, D), F32),
            sds((16, INNER), F32),
            sds((16, LANES), F32),
        ),
        aliases={10: 1},
    )(pre, mine, got, cot, last, tokens, wo_t, b_out, total, small, mixed)


def rotate(value, axis, count, by):
    return lax.ppermute(value, axis, [(i, (i + by) % count) for i in range(count)])


def shift(value, by):
    count = lax.axis_size("seq")
    pairs = [(i, i + by) for i in range(count) if 0 <= i + by < count]
    return lax.ppermute(value, "seq", pairs)


def rims(lead, trail):
    return shift(trail, 1), shift(lead, -1)


def own_slice(value, width, dim):
    return lax.dynamic_slice_in_dim(value, lax.axis_index("ch") * width, width, dim)


def lane_copies(vectors):
    return jnp.broadcast_to(vectors[..., None], vectors.shape + (LANES,))


def body(
    tokens,
    pad_mask,
    cotangent,
    ln1_gain,
    first_norm_bias,
    w_in,
    b_in,
    ln2_gain,
    ln2_bias,
    conv_w,
    conv_b,
    ln3_gain,
    ln3_bias,
    w_out,
    b_out,
):
    chs = lax.axis_size("ch")
    ch = lax.axis_index("ch")
    seqs, _, length = tokens.shape
    share = b_out.shape[0]
    part = b_in.shape[0]
    n = seqs // chs
    group = min(4, n)
    starts = [((ch + chs - r) % chs) * n for r in range(1, chs)]
    pre = jnp.stack([ch * n, ch] + starts).astype(jnp.int32)
    pair = chs == 2 and lax.axis_size("seq") == 1 << LEVELS

    p1 = lane_copies(jnp.stack([ln1_gain, first_norm_bias]))
    bo = lane_copies(b_out)
    vectors = [b_in, ln2_gain, ln2_bias, conv_b, ln3_gain, ln3_bias]
    if pair:
        vec = jnp.pad(jnp.concatenate(vectors), (0, 2048 - 6 * part)).reshape(16, LANES)
        first, stat, w_in_full, conv_full, w_out_full, vec_full, away = first_call(
            pre, tokens, p1, (w_in, conv_w, w_out), vec, cotangent
        )
        others = [rotate(away, "ch", chs, 1)]
        vec_full = vec_full.reshape(2, 2048)[:, : 6 * part].reshape(2, 6, part)
        inner = vec_full.transpose(1, 0, 2).reshape(6, INNER)
    else:
        first, stat = first_call(pre, tokens, p1, None, None)
        w_in_full = lax.all_gather(w_in, "ch", axis=0, tiled=True)
        conv_full = lax.all_gather(conv_w, "ch", axis=1, tiled=True)
        w_out_full = lax.all_gather(w_out, "ch", axis=0, tiled=True)
        inner = lax.all_gather(jnp.stack(vectors), "ch", axis=1, tiled=True)
        others = []
        for r in range(1, chs):
            block = lax.dynamic_slice_in_dim(cotangent, ((ch + r) % chs) * n, n, 0)
            others.append(rotate(block, "ch", chs, r))

    p2 = lane_copies(inner)
    wo_t = lax.dynamic_slice_in_dim(w_out_full, ch * share, share, 1).T

    mid_own, lead, trail, hat_mid, gp_mid, scale_mid = middle_call(
        pre, first, pad_mask, w_in_full, p2, n, 0, group, True
    )
    if pair:
        wc, wc_t, before, after = turn_call(pre, conv_full, (lead, trail))
    else:
        wc, wc_t = turn_call(pre, conv_full)
        before, after = rims(lead, trail)
        mid_oth, lead, trail = middle_call(pre, first, pad_mask, w_in_full, p2, seqs - n, n, group, False)
        rims_oth = rims(lead, trail)
    mixed, hat_out, gp_out, scale_out, last_own = last_call(
        pre, mid_own, before, after, tokens, wc, wo_t, p2, bo, n, 0, group, True, None
    )
    dconv, lead, trail, gg3, gb3, gcb, gwo, gbo, rows = rear_call(
        pre, cotangent, others, w_out_full, hat_out, gp_out, last_own, scale_out, p2, group
    )
    if pair:
        mid_oth, lead_oth, trail_oth, lead, trail = middle_rims_call(
            (lead, trail), first, pad_mask, w_in_full, p2, n, group
        )
        rims_oth = (lead_oth, trail_oth)
    else:
        lead, trail = rims(lead, trail)
    if pair:
        dn, gcw, gwi, rows_in = inner_call(
            pre, dconv, lead, trail, mid_own, hat_mid, gp_mid, scale_mid, first, wc_t, p2, group
        )
        mine, last_oth, total, small, got = tail_call(
            dn, tokens, stat, mid_oth, rims_oth, wc, w_in_full, p1, p2, rows, rows_in,
            gcw.reshape(KERNEL, INNER, INNER), gwo, gwi, group,
        )
        gt, mixed, gcw, gwi, gwo, inner_sums, outer_sums = finish_call(
            pre, mine, got, cotangent, last_oth, tokens, wo_t, bo, total, small, mixed, part
        )
        inner_sums, outer_sums = inner_sums[:6, :part], outer_sums[:15].reshape(3, share)
    else:
        gt, *rest = front_call(
            pre, dconv, lead, trail, mid_own, hat_mid, gp_mid, scale_mid, tokens, stat, cotangent,
            wc_t, w_in_full.T, p2, p1, chs, group,
        )
        sends = [rotate(v, "ch", chs, r + 1) for r, v in enumerate(rest[: chs - 1])]
        gcw, gwi, gg2, gb2, gbi, gg1, gb1 = rest[chs - 1 :]
        gcw = gcw.reshape(KERNEL, INNER, INNER)
        inner_sums = jnp.stack([v.sum(1) for v in (gbi, gg2, gb2, gcb, gg3, gb3)])
        outer_sums = jnp.stack([v.sum(1) for v in (gg1, gb1, gbo)])
        mixed, = last_call(
            pre, mid_oth, *rims_oth, tokens, wc, wo_t, p2, bo, seqs - n, n, group, False, mixed
        )
        gcw, gwi, gwo, inner_sums, outer_sums = lax.psum((gcw, gwi, gwo, inner_sums, outer_sums), ("seq", "ch"))
        gcw = own_slice(gcw, part, 1)
        gwi = own_slice(gwi, part, 0)
        gwo = own_slice(gwo, part, 0)
        inner_sums = own_slice(inner_sums, part, 1)
        outer_sums = own_slice(outer_sums, share, 1)
        for r in range(chs - 1):
            gt = add_call(pre, sends[r], cotangent, gt, 2 + r)
    return (
        mixed,
        gt,
        outer_sums[0],
        outer_sums[1],
        gwi,
        inner_sums[0],
        inner_sums[1],
        inner_sums[2],
        gcw,
        inner_sums[3],
        inner_sums[4],
        inner_sums[5],
        gwo,
        outer_sums[2],
    )


def solution(mesh):
    in_specs = (
        P(None, None, "seq"),
        P(None, "seq"),
        P(None, "ch", "seq"),
        P(),
        P(),
        P("ch", None),
        P("ch"),
        P("ch"),
        P("ch"),
        P(None, "ch", None),
        P("ch"),
        P("ch"),
        P("ch"),
        P("ch", None),
        P("ch"),
    )
    out_specs = (
        P(None, "ch", "seq"),
        P(None, "ch", "seq"),
        P("ch"),
        P("ch"),
        P("ch", None),
        P("ch"),
        P("ch"),
        P("ch"),
        P(None, "ch", None),
        P("ch"),
        P("ch"),
        P("ch"),
        P("ch", None),
        P("ch"),
    )
    return jax.shard_map(body, mesh=mesh, in_specs=in_specs, out_specs=out_specs, check_vma=False)
```

```python
import functools
import math

import jax
import jax.numpy as jnp
from jax import lax
from jax.experimental import pallas as pl
from jax.experimental.pallas import tpu as pltpu
from jax.sharding import PartitionSpec as P

D = 1280
INNER = 640
KERNEL = 5
DILATION = 16
REACH = KERNEL // 2 * DILATION
EPS = 1e-05
HALF_ROOT = math.sqrt(0.5)
DENSITY = 1.0 / math.sqrt(2.0 * math.pi)
F32 = jnp.float32
BF16 = jnp.bfloat16
LANES = 128
VMEM_BYTES = 60 * 1024 * 1024


TWO = 2


def rows_of(width):
    return next(r for r in (64, 32, 16) if width % r == 0)


def straight(width, length, body, init):
    rows = next(r for r in (64, 32, 16) if width % r == 0 and r * length <= 64 * 256 or r == 16)
    for i in range(width // rows):
        init = body(pl.ds(i * rows, rows), init)
    return init


def fold_rows(v):
    return v.reshape(v.shape[0] // 8, 8, v.shape[1]).sum(0)


def fold_lanes(v):
    out = v[:, :LANES]
    for j in range(1, v.shape[1] // LANES):
        out = out + v[:, j * LANES : (j + 1) * LANES]
    return out


def spread(p, length):
    return jnp.concatenate([p] * (length // LANES), axis=1)


def loop(width, body, init):
    rows = rows_of(width)

    def step(i, carry):
        return body(pl.ds(pl.multiple_of(i * rows, rows), rows), carry)

    return lax.fori_loop(0, width // rows, step, init)


def norm_stats(load, width, length, rolled=False):
    def over(body, init):
        return loop(width, body, init) if rolled else straight(width, length, body, init)

    zero = jnp.zeros((8, length), F32)
    total = over(lambda sl, a: a + fold_rows(load(sl)), zero)
    mean = total.sum(0, keepdims=True) / width

    def square(sl, a):
        c = load(sl) - mean
        return a + fold_rows(c * c)

    total = over(square, zero)
    return mean, lax.rsqrt(total.sum(0, keepdims=True) / width + EPS)


def cdf(p):
    return 0.5 + 0.5 * lax.erf(p * HALF_ROOT)


def slope(p, phi):
    return phi + p * (DENSITY * jnp.exp(p * p * -0.5))


def call(kernel, grid, in_specs, out_specs, out_shape, scratch=(), prefetch=1, aliases=None, cost=None):
    return pl.pallas_call(
        kernel,
        grid_spec=pltpu.PrefetchScalarGridSpec(
            num_scalar_prefetch=prefetch,
            grid=grid,
            in_specs=in_specs,
            out_specs=out_specs,
            scratch_shapes=list(scratch),
        ),
        out_shape=out_shape,
        input_output_aliases=aliases or {},
        cost_estimate=cost,
        compiler_params=pltpu.CompilerParams(vmem_limit_bytes=VMEM_BYTES),
    )


def cost_of(macs, bytes_accessed):
    return pl.CostEstimate(flops=int(2 * macs), bytes_accessed=int(bytes_accessed), transcendentals=0)


def whole(shape, at=0):
    return pl.BlockSpec(shape, lambda i, pre: (at,) + (0,) * (len(shape) - 1), pipeline_mode=pl.Buffered(1))


def sds(shape, dtype):
    return jax.ShapeDtypeStruct(shape, dtype)


def weight_copies(own_refs, full_refs, sems):
    seq, ch = lax.axis_index("seq"), lax.axis_index("ch")
    core, row = seq % 2, (seq // 2) % 2
    send_sem, recv_sem = sems
    across, along, beside = {"ch": 1 - ch}, {"seq": seq + 2 - 4 * row}, {"seq": seq + 1 - 2 * core}

    def part(ref, at, size):
        at = pl.multiple_of(at, 16)
        return ref.at[:, pl.ds(at, size), :] if len(ref.shape) == 3 else ref.at[pl.ds(at, size), :]

    (w_in, conv, w_out), (w_in_full, conv_full, w_out_full) = own_refs, full_refs
    items = [
        (w_in, w_in_full),
        (conv.at[pl.ds(0, 2)], conv_full.at[pl.ds(0, 2)]),
        (conv.at[pl.ds(2, 3)], conv_full.at[pl.ds(2, 3)]),
        (w_out, w_out_full),
    ]
    local, first_hop, second_hop, third_hop = [], [], [], []
    for k, (own, full) in enumerate(items):
        half = own.shape[-2]
        size = half // 4

        def remote(src, dst, slot, device):
            return pltpu.make_async_remote_copy(
                src_ref=src,
                dst_ref=dst,
                send_sem=send_sem.at[k, slot],
                recv_sem=recv_sem.at[k, slot],
                device_id=device,
                device_id_type=pl.DeviceIdType.MESH,
            )

        quarter = (row * 2 + core) * size
        local.append(remote(own, part(full, ch * half, half), 4, beside))
        first_hop.append(remote(part(own, quarter, size), part(full, ch * half + quarter, size), 0, across))
        landed = (1 - ch) * half
        mine = part(full, landed + quarter, size)
        second_hop.append(remote(mine, mine, 1, along))
        both = []
        for j, r in enumerate((row, 1 - row)):
            piece = part(full, landed + (r * 2 + core) * size, size)
            both.append(remote(piece, piece, 2 + j, beside))
        third_hop.append(both)
    return local, first_hop, second_hop, third_hop


def first_kernel(comm, pre, x_ref, p_ref, *rest):
    if comm:
        own_refs, own_vec, cot_ref, first_ref, stat_ref = rest[:3], rest[3], rest[4], rest[5], rest[6]
        full_refs, full_vec, away_ref = rest[7:10], rest[10], rest[11]
        exchange(own_refs, own_vec, full_refs, full_vec, rest[12:14], rest[14:])

        @pl.when(pl.program_id(0) < pl.num_programs(0) // 2)
        def _():
            away_ref[...] = cot_ref[...]

    else:
        first_ref, stat_ref = rest
    length = x_ref.shape[2]
    mean, scale = norm_stats(lambda sl: x_ref[0, sl, :].astype(F32), D, length, True)
    stat_ref[0, 0:1, :] = mean
    stat_ref[0, 1:2, :] = scale

    def body(sl, carry):
        hat = (x_ref[0, sl, :].astype(F32) - mean) * scale
        point = hat * spread(p_ref[0, sl, :], length) + spread(p_ref[1, sl, :], length)
        first_ref[0, sl, :] = (point * cdf(point)).astype(BF16)
        return carry

    loop(D, body, 0)


def exchange(own_refs, own_vec, full_refs, full_vec, sems, vec_sems):
    step, steps = pl.program_id(0), pl.num_programs(0)
    seq, ch = lax.axis_index("seq"), lax.axis_index("ch")
    core, row = seq % 2, (seq // 2) % 2
    local, first_hop, second_hop, third_hop = weight_copies(own_refs, full_refs, sems)
    vec_local = pltpu.make_async_copy(own_vec, full_vec.at[ch], vec_sems[0])
    vec_remote = pltpu.make_async_remote_copy(
        src_ref=own_vec,
        dst_ref=full_vec.at[ch],
        send_sem=vec_sems[1],
        recv_sem=vec_sems[2],
        device_id={"ch": 1 - ch},
        device_id_type=pl.DeviceIdType.MESH,
    )

    @pl.when(step == 0)
    def _():
        barrier = pltpu.get_barrier_semaphore()
        for device in ({"ch": 1 - ch}, {"seq": seq + 2 - 4 * row}, {"seq": seq + 1 - 2 * core}):
            pl.semaphore_signal(barrier, inc=1, device_id=device, device_id_type=pl.DeviceIdType.MESH)
        pl.semaphore_wait(barrier, 3)
        vec_remote.start()
        first_hop[0].start()
        vec_local.start()
        for copy in local:
            copy.start()

    for k in range(4):

        if k > 0:

            @pl.when(step == (0, 1, 4, 7)[k])
            def _():
                first_hop[k].start()

        @pl.when(step == (4, 7, 10, 12)[k])
        def _():
            first_hop[k].wait()
            second_hop[k].start()
            third_hop[k][0].start()

        @pl.when(step == (7, 10, 14, 15)[k])
        def _():
            second_hop[k].wait()
            third_hop[k][1].start()

    @pl.when(step == steps - 1)
    def _():
        vec_remote.wait()
        vec_local.wait()
        for k in range(4):
            local[k].wait()
            third_hop[k][0].wait()
            third_hop[k][1].wait()


def first_call(pre, tokens, p1, weights, vec, cot=None):
    seqs, _, length = tokens.shape
    comm = weights is not None
    any_spec = pl.BlockSpec(memory_space=pl.ANY)
    in_specs = [pl.BlockSpec((1, D, length), lambda i, pre: ((pre[0] + i) % seqs, 0, 0)), whole((2, D, LANES))]
    out_specs = [
        pl.BlockSpec((1, D, length), lambda i, pre: (i, 0, 0)),
        pl.BlockSpec((1, 2, length), lambda i, pre: (i, 0, 0)),
    ]
    shapes = [sds((seqs, D, length), BF16), sds((seqs, 2, length), F32)]
    args, scratch = [pre, tokens, p1], []
    if comm:
        in_specs += [any_spec] * 4
        out_specs += [any_spec] * 4
        shapes += [sds(w.shape[:-2] + (2 * w.shape[-2], w.shape[-1]), BF16) for w in weights]
        shapes.append(sds((2,) + vec.shape, F32))
        args += list(weights) + [vec]
        dma = pltpu.SemaphoreType.DMA
        scratch = [dma((4, 5)), dma((4, 5)), dma, dma, dma]

    def kernel(*refs):
        first_kernel(comm, *refs)

    if comm:

        def at(i):
            return ((lax.axis_index("ch") * (seqs // 2) + i) % seqs, 0, 0)

        n, share = seqs // 2, cot.shape[1]

        def away(i):
            return ((1 - lax.axis_index("ch")) * n + jnp.minimum(i, n - 1), 0, 0)

        shapes.append(sds((n, share, length), BF16))
        args.append(cot)

        return pl.pallas_call(
            lambda *refs: first_kernel(True, None, *refs),
            grid=(seqs,),
            in_specs=[
                pl.BlockSpec((1, D, length), at),
                pl.BlockSpec((2, D, LANES), lambda i: (0, 0, 0), pipeline_mode=pl.Buffered(1)),
            ]
            + [any_spec] * 4
            + [pl.BlockSpec((1, share, length), away)],
            out_specs=tuple(
                [pl.BlockSpec((1, D, length), lambda i: (i, 0, 0)), pl.BlockSpec((1, 2, length), lambda i: (i, 0, 0))]
                + [any_spec] * 4
                + [pl.BlockSpec((1, share, length), lambda i: (jnp.minimum(i, n - 1), 0, 0))]
            ),
            out_shape=tuple(shapes),
            scratch_shapes=scratch,
            cost_estimate=cost_of(seqs * D * length * 40, seqs * D * length * 4),
            compiler_params=pltpu.CompilerParams(
                vmem_limit_bytes=VMEM_BYTES, collective_id=1, has_side_effects=True
            ),
        )(*args[1:])
    return call(kernel, (seqs,), in_specs, tuple(out_specs), tuple(shapes))(*args)


class Rims:
    def __init__(self, lead, trail, before, after, send_sem, recv_sem):
        self.seq, self.count = lax.axis_index("seq"), lax.axis_size("seq")
        self.before, self.after = before, after

        def remote(src, dst, k, by):
            return pltpu.make_async_remote_copy(
                src_ref=src,
                dst_ref=dst,
                send_sem=send_sem.at[k],
                recv_sem=recv_sem.at[k],
                device_id={"seq": self.seq + by},
                device_id_type=pl.DeviceIdType.MESH,
            )

        self.up = lambda: remote(trail, before, 0, 1)
        self.down = lambda: remote(lead, after, 1, -1)
        self.has_up, self.has_down = self.seq < self.count - 1, self.seq > 0

    def greet(self):
        barrier = pltpu.get_barrier_semaphore()
        for there, by in ((self.has_up, 1), (self.has_down, -1)):

            @pl.when(there)
            def _():
                pl.semaphore_signal(
                    barrier, inc=1, device_id={"seq": self.seq + by}, device_id_type=pl.DeviceIdType.MESH
                )
        return self.has_up.astype(jnp.int32) + self.has_down.astype(jnp.int32)

    def start(self):
        pl.when(self.has_up)(lambda: self.up().start())
        pl.when(self.has_down)(lambda: self.down().start())

    def wait(self):
        @pl.when(self.has_up)
        def _():
            self.up().wait_send()
            self.down().wait_recv()

        @pl.when(self.has_down)
        def _():
            self.down().wait_send()
            self.up().wait_recv()


def rim_steps(lead, trail, before, after, zeros, send_sem, recv_sem, local_sem):
    rims = Rims(lead, trail, before, after, send_sem, recv_sem)
    step, steps = pl.program_id(0), pl.num_programs(0)
    ends = (
        (jnp.logical_not(rims.has_down), lambda: pltpu.make_async_copy(zeros, before, local_sem.at[0])),
        (jnp.logical_not(rims.has_up), lambda: pltpu.make_async_copy(zeros, after, local_sem.at[1])),
    )

    @pl.when(step == 0)
    def _():
        zeros[...] = jnp.zeros_like(zeros)
        pl.semaphore_wait(pltpu.get_barrier_semaphore(), rims.greet())
        rims.start()
        for there, copy in ends:
            pl.when(there)(lambda: copy().start())

    def last():
        rims.wait()
        for there, copy in ends:
            pl.when(there)(lambda: copy().wait())

    pl.when(step == steps - 1)(last)


def rim_scratch(shape):
    dma = pltpu.SemaphoreType.DMA
    return [pltpu.VMEM(shape, BF16), dma((2,)), dma((2,)), dma((2,))]


def put_edges(group, ref, lead_ref, trail_ref):
    length = ref.shape[2]
    place = pl.program_id(0) % (group // TWO)
    for k in range(group // TWO):

        @pl.when(place == k)
        def _():
            for j in range(TWO):
                lanes = slice((k * TWO + j) * REACH, (k * TWO + j + 1) * REACH)
                lead_ref[0, :, lanes] = ref[j, :, :REACH]
                trail_ref[0, :, lanes] = ref[j, :, length - REACH :]


def middle_rims_kernel(group, lead_in, trail_in, first_ref, mask_ref, w_ref, p_ref, *rest):
    rim_steps(lead_in, trail_in, *rest[3:5], *rest[5:9])
    middle_kernel(group, False, None, first_ref, mask_ref, w_ref, p_ref, *rest[:3], *rest[9:])


def middle_rims_call(edges, first, mask, w_in, p2, count, group):
    _, _, length = first.shape
    seqs = mask.shape[0]
    edge = pl.BlockSpec((1, INNER, group * REACH), lambda i: (i // (group // TWO), 0, 0))
    edge_shape = sds((count // group, INNER, group * REACH), BF16)
    any_spec = pl.BlockSpec(memory_space=pl.ANY)

    def fixed(shape):
        return pl.BlockSpec(shape, lambda i: (0,) * len(shape), pipeline_mode=pl.Buffered(1))

    def mask_at(i):
        return (((lax.axis_index("ch") + 1) * (count // TWO) + i) % (seqs // TWO), 0, 0)

    return pl.pallas_call(
        functools.partial(middle_rims_kernel, group),
        grid=(count // TWO,),
        in_specs=[
            any_spec,
            any_spec,
            pl.BlockSpec((TWO, D, length), lambda i: (count // TWO + i, 0, 0)),
            pl.BlockSpec((TWO, 1, length), mask_at),
            fixed((INNER, D)),
            fixed((3, INNER, LANES)),
        ],
        out_specs=(pl.BlockSpec((TWO, INNER, length), lambda i: (i, 0, 0)), edge, edge, any_spec, any_spec),
        out_shape=(sds((count, INNER, length), BF16), *[edge_shape] * 4),
        scratch_shapes=rim_scratch(edge_shape.shape) + [pltpu.VMEM((INNER, length), F32)] * TWO,
        cost_estimate=cost_of(count * INNER * D * length * 1.5, count * (D + INNER * 3) * length * 2),
        compiler_params=pltpu.CompilerParams(vmem_limit_bytes=VMEM_BYTES, collective_id=4, has_side_effects=True),
    )(*edges, first, mask.reshape(seqs, 1, length), w_in, p2)


def middle_kernel(group, keep, pre, first_ref, mask_ref, w_ref, p_ref, mid_ref, lead_ref, trail_ref, *rest):
    nar_refs = rest[-TWO:]
    length = first_ref.shape[2]
    for j in range(TWO):
        nar = jnp.dot(w_ref[...], first_ref[j], preferred_element_type=F32)
        nar_refs[j][...] = nar + spread(p_ref[0], length)
    for j in range(TWO):
        nar_ref = nar_refs[j]
        mean, scale = norm_stats(lambda sl: nar_ref[sl, :], INNER, length)
        mask = mask_ref[j].astype(F32)

        def body(sl, carry):
            hat = (nar_ref[sl, :] - mean) * scale
            point = hat * spread(p_ref[1, sl, :], length) + spread(p_ref[2, sl, :], length)
            phi = cdf(point)
            mid_ref[j, sl, :] = (point * phi * mask).astype(BF16)
            if keep:
                rest[0][j, sl, :] = hat.astype(BF16)
                rest[1][j, sl, :] = slope(point, phi) * mask
            return carry

        straight(INNER, length, body, 0)
        if keep:
            rest[2][j] = scale
    put_edges(group, mid_ref, lead_ref, trail_ref)


def middle_call(pre, first, mask, w_in, p2, count, offset, group, keep):
    _, _, length = first.shape
    seqs = mask.shape[0]
    edge = pl.BlockSpec((1, INNER, group * REACH), lambda i, pre: (i // (group // TWO), 0, 0))
    edge_shape = sds((count // group, INNER, group * REACH), BF16)
    own = pl.BlockSpec((TWO, INNER, length), lambda i, pre: (i, 0, 0))
    outs = [own, edge, edge]
    shapes = [sds((count, INNER, length), BF16), edge_shape, edge_shape]
    if keep:
        outs += [own, own, pl.BlockSpec((TWO, 1, length), lambda i, pre: (i, 0, 0))]
        shapes += [
            sds((count, INNER, length), BF16),
            sds((count, INNER, length), F32),
            sds((count, 1, length), F32),
        ]
    return call(
        functools.partial(middle_kernel, group, keep),
        (count // TWO,),
        [
            pl.BlockSpec((TWO, D, length), lambda i, pre: (offset // TWO + i, 0, 0)),
            pl.BlockSpec((TWO, 1, length), lambda i, pre: (((pre[0] + offset) // TWO + i) % (seqs // TWO), 0, 0)),
            whole((INNER, D)),
            whole((3, INNER, LANES)),
        ],
        tuple(outs),
        tuple(shapes),
        scratch=[pltpu.VMEM((INNER, length), F32)] * TWO,
        cost=cost_of(count * INNER * D * length * 1.5, count * (D + INNER * 3) * length * 2),
    )(pre, first, mask.reshape(seqs, 1, length), w_in, p2)


def gather_windows(group, body_ref, before_ref, after_ref, pad_ref, cat_refs, order, step=None):
    width, length, count = body_ref.shape[1], body_ref.shape[2], len(cat_refs)
    place = (pl.program_id(0) if step is None else step) % (group // count)
    for k in range(group // count):

        @pl.when(place == k)
        def _():
            for j in range(count):
                lanes = slice((k * count + j) * REACH, (k * count + j + 1) * REACH)
                pad_ref[j, :, LANES - REACH : LANES] = before_ref[0, :, lanes]
                pad_ref[j, :, LANES + length : LANES + length + REACH] = after_ref[0, :, lanes]

    for j in range(count):
        pad_ref[j, :, LANES : LANES + length] = body_ref[j]
        for tap in range(KERNEL):
            start = LANES + order * (tap - KERNEL // 2) * DILATION
            cat_refs[j][tap * width : (tap + 1) * width, :] = pad_ref[j, :, start : start + length]


def last_kernel(
    group, keep, pre, mid_ref, before_ref, after_ref, x_ref, wc_ref, wo_ref, p_ref, b_ref, *rest
):
    if keep:
        mixed_ref, hat_ref, gp_ref, scale_ref, last_out = rest[:5]
        last_refs = [last_out.at[j] for j in range(TWO)]
    else:
        mixed_ref = rest[1]
        last_refs = rest[-TWO:]
        rest = rest[:-TWO]
    pad_ref, cat_refs, conv_refs = rest[-1 - 2 * TWO], rest[-2 * TWO : -TWO], rest[-TWO:]
    length = mid_ref.shape[2]
    gather_windows(group, mid_ref, before_ref, after_ref, pad_ref, cat_refs, 1)
    for j in range(TWO):
        conv = jnp.dot(wc_ref[...], cat_refs[j][...], preferred_element_type=F32)
        conv_refs[j][...] = conv + spread(p_ref[0], length)
    for j in range(TWO):
        conv_ref, last_ref = conv_refs[j], last_refs[j]
        mean, scale = norm_stats(lambda sl: conv_ref[sl, :], INNER, length)

        def body(sl, carry):
            hat = (conv_ref[sl, :] - mean) * scale
            point = hat * spread(p_ref[1, sl, :], length) + spread(p_ref[2, sl, :], length)
            phi = cdf(point)
            last_ref[sl, :] = (point * phi).astype(BF16)
            if keep:
                hat_ref[j, sl, :] = hat.astype(BF16)
                gp_ref[j, sl, :] = slope(point, phi)
            return carry

        straight(INNER, length, body, 0)
        if keep:
            scale_ref[j] = scale
        branch = jnp.dot(wo_ref[...], last_ref[...], preferred_element_type=F32)
        mixed_ref[j] = (x_ref[j].astype(F32) + branch + spread(b_ref[...], length)).astype(BF16)


def last_call(pre, mid, before, after, tokens, wc, wo_t, p2, b_out, count, offset, group, keep, mixed):
    _, _, length = mid.shape
    seqs, share = tokens.shape[0], wo_t.shape[0]
    edge = pl.BlockSpec((1, INNER, group * REACH), lambda i, pre: (i // (group // TWO), 0, 0))
    own = pl.BlockSpec((TWO, INNER, length), lambda i, pre: (i, 0, 0))

    def pair_at(i, pre):
        return ((pre[0] + offset) // TWO + i) % (seqs // TWO)

    outs = [pl.BlockSpec((TWO, share, length), lambda i, pre: (pair_at(i, pre), 0, 0))]
    shapes = [sds((seqs, share, length), BF16)]
    in_specs = [
        own,
        edge,
        edge,
        pl.BlockSpec((TWO, share, length), lambda i, pre: (pair_at(i, pre), pre[1], 0)),
        whole((INNER, KERNEL * INNER)),
        whole((share, INNER)),
        whole((3, INNER, LANES), 1),
        whole((share, LANES)),
    ]
    args = [pre, mid, before, after, tokens, wc, wo_t, p2, b_out]
    aliases = None
    scratch = [pltpu.VMEM((TWO, INNER, length + 2 * LANES), BF16)]
    scratch += [pltpu.VMEM((KERNEL * INNER, length), BF16)] * TWO
    scratch += [pltpu.VMEM((INNER, length), F32)] * TWO
    if keep:
        outs += [own, own, pl.BlockSpec((TWO, 1, length), lambda i, pre: (i, 0, 0)), own]
        saved = sds((count, INNER, length), BF16)
        shapes += [saved, sds((count, INNER, length), F32), sds((count, 1, length), F32), saved]
    else:
        scratch += [pltpu.VMEM((INNER, length), BF16)] * TWO
        in_specs.append(pl.BlockSpec(memory_space=pl.ANY))
        args.append(mixed)
        aliases = {len(args) - 1: 0}
    return call(
        functools.partial(last_kernel, group, keep),
        (count // TWO,),
        in_specs,
        tuple(outs),
        tuple(shapes),
        scratch=scratch,
        aliases=aliases,
        cost=cost_of(count * INNER * (KERNEL * INNER + share) * length * 1.3, count * share * 6 * length * 2),
    )(*args)


def side(ref, sl):
    return jnp.concatenate([ref[j, sl, :].astype(F32) for j in range(ref.shape[0])], axis=1)


def across(ref, row):
    return jnp.concatenate([ref[j, row : row + 1, :] for j in range(ref.shape[0])], axis=1)


def row_sums(ref):
    ones = jnp.ones((8, LANES), F32)
    return lax.dot_general(
        ones, ref[...], (((1,), (1,)), ((), ())), precision=lax.Precision.HIGHEST, preferred_element_type=F32
    )


def norm_back(d_ref, gp_ref, hat_ref, scale, gain_ref, gg_ref, gb_ref, sum_ref, put):
    wide = d_ref.shape[1]
    zero = jnp.zeros((8, wide), F32)

    def body(sl, carry):
        d_pre = d_ref[sl, :] * side(gp_ref, sl)
        hat = side(hat_ref, sl)
        gg_ref[sl, :] += fold_lanes(d_pre * hat)
        gb_ref[sl, :] += fold_lanes(d_pre)
        e = d_pre * spread(gain_ref[0, sl, :], wide)
        d_ref[sl, :] = e
        return carry[0] + fold_rows(e), carry[1] + fold_rows(e * hat)

    total, dot = straight(INNER, wide, body, (zero, zero))
    total = total.sum(0, keepdims=True) * (scale / INNER)
    dot = dot.sum(0, keepdims=True) * (scale / INNER)

    def finish(sl, carry):
        v = (d_ref[sl, :] * scale - total - side(hat_ref, sl) * dot).astype(BF16)
        put(sl, v)
        sum_ref[sl, :] += fold_lanes(v.astype(F32))
        return carry

    straight(INNER, wide, finish, 0)


def rear_kernel(group, chs, pre, *refs):
    dy_refs = refs[:chs]
    w_ref, hat_ref, gp_ref, last_ref, scale_ref, p_ref = refs[chs : chs + 6]
    dconv_ref, lead_ref, trail_ref, gg_ref, gb_ref, gc_ref, gw_ref, go_ref = refs[chs + 6 : chs + 14]
    rows_ref, dy_ref, d_ref = refs[chs + 14 :]
    share, length = dy_refs[0].shape[1], dy_refs[0].shape[2]

    @pl.when(pl.program_id(0) == 0)
    def _():
        for ref in (gg_ref, gb_ref, gc_ref, gw_ref, go_ref):
            ref[...] = jnp.zeros_like(ref)

    for r in range(chs):
        at = pl.multiple_of(((pre[1] + chs - r) % chs) * share, share)
        for j in range(TWO):
            dy_ref[pl.ds(at, share), j * length : (j + 1) * length] = dy_refs[r][j]
    d_ref[...] = jnp.dot(w_ref[...], dy_ref[...], preferred_element_type=F32)
    last = jnp.concatenate([last_ref[j] for j in range(TWO)], axis=1)
    gw_ref[...] += lax.dot_general(last, dy_ref[...], (((1,), (1,)), ((), ())), preferred_element_type=F32)
    go_ref[...] += fold_lanes(dy_ref[...].astype(F32))

    def put(sl, v):
        for j in range(TWO):
            dconv_ref[j, sl, :] = v[:, j * length : (j + 1) * length]

    norm_back(d_ref, gp_ref, hat_ref, across(scale_ref, 0), p_ref, gg_ref, gb_ref, gc_ref, put)
    put_edges(group, dconv_ref, lead_ref, trail_ref)

    @pl.when(pl.program_id(0) == pl.num_programs(0) - 1)
    def _():
        for k, ref in enumerate((gc_ref, gg_ref, gb_ref)):
            rows_ref[:, k * INNER : (k + 1) * INNER] = row_sums(ref)
        rows_ref[:, 3 * INNER :] = row_sums(go_ref)


def const(shape):
    return pl.BlockSpec(shape, lambda i, pre: (0,) * len(shape), pipeline_mode=pl.Buffered(1))


def rear_call(pre, cot, others, w_out, hat, gp, last, scale, p2, group):
    seqs, share, length = cot.shape
    count = hat.shape[0]
    chs = 1 + len(others)
    edge = pl.BlockSpec((1, INNER, group * REACH), lambda i, pre: (i // (group // TWO), 0, 0))
    edge_shape = sds((count // group, INNER, group * REACH), BF16)
    own = pl.BlockSpec((TWO, INNER, length), lambda i, pre: (i, 0, 0))
    sums = [(INNER, LANES)] * 3 + [(INNER, D), (D, LANES), (8, 3 * INNER + D)]
    return call(
        functools.partial(rear_kernel, group, chs),
        (count // TWO,),
        [pl.BlockSpec((TWO, share, length), lambda i, pre: (pre[0] // TWO + i, 0, 0))]
        + [pl.BlockSpec((TWO, share, length), lambda i, pre: (i, 0, 0))] * (chs - 1)
        + [
            whole((INNER, D)),
            own,
            own,
            own,
            pl.BlockSpec((TWO, 1, length), lambda i, pre: (i, 0, 0)),
            whole((1, INNER, LANES), 4),
        ],
        tuple([own, edge, edge] + [const(v) for v in sums]),
        tuple([sds((count, INNER, length), BF16), edge_shape, edge_shape] + [sds(v, F32) for v in sums]),
        scratch=[pltpu.VMEM((D, TWO * length), BF16), pltpu.VMEM((INNER, TWO * length), F32)],
        cost=cost_of(count * INNER * D * length * 2.5, count * INNER * 5 * length * 2),
    )(pre, cot, *others, w_out, hat, gp, last, scale, p2)


def front_kernel(group, chs, pre, *refs):
    dconv_ref, before_ref, after_ref, mid_ref, hat_ref, gp_ref, scale_ref = refs[:7]
    x_ref, stat_ref, dy_ref, wc_ref, wi_ref, p2_ref, p1_ref = refs[7:14]
    refs = refs[14:]
    gt_ref = refs[0]
    send_refs = refs[1:chs]
    gcw_ref, gwi_ref, gg2_ref, gb2_ref, gbi_ref, gg1_ref, gb1_ref = refs[chs : chs + 7]
    pad_ref, cat_ref, d_ref, dn_ref, df_ref, first_ref = refs[chs + 7 :]
    share, length = dy_ref.shape[1], dy_ref.shape[2]
    wide = TWO * length

    @pl.when(pl.program_id(0) == 0)
    def _():
        for ref in (gcw_ref, gwi_ref, gg2_ref, gb2_ref, gbi_ref, gg1_ref, gb1_ref):
            ref[...] = jnp.zeros_like(ref)

    cats = [cat_ref.at[:, j * length : (j + 1) * length] for j in range(TWO)]
    gather_windows(group, dconv_ref, before_ref, after_ref, pad_ref, cats, -1)
    d_ref[...] = jnp.dot(wc_ref[...], cat_ref[...], preferred_element_type=F32)
    mid = jnp.concatenate([mid_ref[j] for j in range(TWO)], axis=1)
    gcw_ref[...] += lax.dot_general(cat_ref[...], mid, (((1,), (1,)), ((), ())), preferred_element_type=F32)

    def put(sl, v):
        dn_ref[sl, :] = v

    norm_back(d_ref, gp_ref, hat_ref, across(scale_ref, 0), p2_ref, gg2_ref, gb2_ref, gbi_ref, put)
    df_ref[...] = jnp.dot(wi_ref[...], dn_ref[...], preferred_element_type=F32)
    mean_in, scale_in = across(stat_ref, 0), across(stat_ref, 1)
    zero = jnp.zeros((8, wide), F32)

    def inner(sl, carry):
        hat = (side(x_ref, sl) - mean_in) * scale_in
        gain = spread(p1_ref[0, sl, :], wide)
        point = hat * gain + spread(p1_ref[1, sl, :], wide)
        phi = cdf(point)
        first_ref[sl, :] = (point * phi).astype(BF16)
        d_pre = df_ref[sl, :] * slope(point, phi)
        gg1_ref[sl, :] += fold_lanes(d_pre * hat)
        gb1_ref[sl, :] += fold_lanes(d_pre)
        e = d_pre * gain
        df_ref[sl, :] = e
        return carry[0] + fold_rows(e), carry[1] + fold_rows(e * hat)

    total, dot = straight(D, wide, inner, (zero, zero))
    total = total.sum(0, keepdims=True) * (scale_in / D)
    dot = dot.sum(0, keepdims=True) * (scale_in / D)
    gwi_ref[...] += lax.dot_general(
        dn_ref[...], first_ref[...], (((1,), (1,)), ((), ())), preferred_element_type=F32
    )
    for r in range(chs):
        base = ((pre[1] + r) % chs) * share

        def out(to, carry):
            rows = pl.ds(pl.multiple_of(base + to.start, 16), to.size)
            hat = (side(x_ref, rows) - mean_in) * scale_in
            v = df_ref[rows, :] * scale_in - total - hat * dot
            for j in range(TWO):
                half = v[:, j * length : (j + 1) * length]
                if r == 0:
                    gt_ref[j, to, :] = half + dy_ref[j, to, :].astype(F32)
                else:
                    send_refs[r - 1][j, to, :] = half.astype(BF16)
            return carry

        straight(share, wide, out, 0)


def front_call(pre, dconv, before, after, mid, hat, gp, scale, tokens, stat, cot, wc_t, wi_t, p2, p1, chs, group):
    seqs, share, length = cot.shape
    count = dconv.shape[0]
    edge = pl.BlockSpec((1, INNER, group * REACH), lambda i, pre: (i // (group // TWO), 0, 0))
    own = pl.BlockSpec((TWO, INNER, length), lambda i, pre: (i, 0, 0))

    def seq_block(rows):
        return pl.BlockSpec((TWO, rows, length), lambda i, pre: (pre[0] // TWO + i, 0, 0))

    inner_part, outer_part = (INNER, LANES), (D, LANES)
    sums = [(KERNEL * INNER, INNER), (INNER, D), inner_part, inner_part, inner_part, outer_part, outer_part]
    wide = TWO * length
    return call(
        functools.partial(front_kernel, group, chs),
        (count // TWO,),
        [
            own,
            edge,
            edge,
            own,
            own,
            own,
            pl.BlockSpec((TWO, 1, length), lambda i, pre: (i, 0, 0)),
            seq_block(D),
            pl.BlockSpec((TWO, 2, length), lambda i, pre: (i, 0, 0)),
            seq_block(share),
            whole((INNER, KERNEL * INNER)),
            whole((D, INNER)),
            whole((1, INNER, LANES), 1),
            whole((2, D, LANES)),
        ],
        tuple(
            [seq_block(share)]
            + [pl.BlockSpec((TWO, share, length), lambda i, pre: (i, 0, 0))] * (chs - 1)
            + [const(v) for v in sums]
        ),
        tuple(
            [sds((seqs, share, length), F32)]
            + [sds((count, share, length), BF16)] * (chs - 1)
            + [sds(v, F32) for v in sums]
        ),
        scratch=[
            pltpu.VMEM((TWO, INNER, length + 2 * LANES), BF16),
            pltpu.VMEM((KERNEL * INNER, wide), BF16),
            pltpu.VMEM((INNER, wide), F32),
            pltpu.VMEM((INNER, wide), BF16),
            pltpu.VMEM((D, wide), F32),
            pltpu.VMEM((D, wide), BF16),
        ],
        cost=cost_of(count * INNER * (2 * KERNEL * INNER + 2 * D) * length * 1.3, count * D * 8 * length * 2),
    )(pre, dconv, before, after, mid, hat, gp, scale, tokens, stat, cot, wc_t, wi_t, p2, p1)


def add_kernel(pre, part_ref, dy_ref, _, gt_ref):
    gt_ref[...] = part_ref[...].astype(F32) + dy_ref[...].astype(F32)


def add_call(pre, part, cot, gt, start):
    seqs, share, length = cot.shape
    count = part.shape[0]
    at = lambda i, pre: (pre[start] + i, 0, 0)
    return call(
        add_kernel,
        (count,),
        [
            pl.BlockSpec((1, share, length), lambda i, pre: (i, 0, 0)),
            pl.BlockSpec((1, share, length), at),
            pl.BlockSpec(memory_space=pl.ANY),
        ],
        pl.BlockSpec((1, share, length), at),
        sds((seqs, share, length), F32),
        aliases={3: 0},
        cost=cost_of(count * share * length, count * share * length * 8),
    )(pre, part, cot, gt)


def turned(square):
    unit = (
        lax.broadcasted_iota(jnp.int32, (INNER, INNER), 0) == lax.broadcasted_iota(jnp.int32, (INNER, INNER), 1)
    ).astype(F32).astype(BF16)
    return lax.dot_general(unit, square, (((1,), (1,)), ((), ())), preferred_element_type=F32).astype(BF16)


def turn_kernel(pre, w_ref, flat_ref, turned_ref):
    flat_ref[...] = w_ref[0]
    turned_ref[...] = turned(w_ref[0])


def turn_rims_kernel(lead, trail, w_ref, wo_ref, flat_ref, turned_ref, before, after, wo_t_ref, *rest):
    rim_steps(lead, trail, before, after, *rest)
    turn_kernel(None, w_ref, flat_ref, turned_ref)

    @pl.when(pl.program_id(0) == 0)
    def _():
        wo_t_ref[...] = turned(wo_ref[...])


def turn_call(pre, conv, edges=None, w_out=None):
    shape = sds((INNER, KERNEL * INNER), BF16)
    if edges is not None:
        any_spec = pl.BlockSpec(memory_space=pl.ANY)
        column = pl.BlockSpec((INNER, INNER), lambda k: (0, k))
        return pl.pallas_call(
            turn_rims_kernel,
            grid=(KERNEL,),
            in_specs=[
                any_spec,
                any_spec,
                pl.BlockSpec((1, INNER, INNER), lambda k: (k, 0, 0)),
                pl.BlockSpec((INNER, INNER), lambda k: (0, lax.axis_index("ch"))),
            ],
            out_specs=(column, column, any_spec, any_spec, pl.BlockSpec((INNER, INNER), lambda k: (0, 0))),
            out_shape=(shape, shape, *[sds(e.shape, BF16) for e in edges], sds((INNER, INNER), BF16)),
            scratch_shapes=rim_scratch(edges[0].shape),
            cost_estimate=cost_of(KERNEL * INNER**3, KERNEL * INNER * INNER * 6),
            compiler_params=pltpu.CompilerParams(
                vmem_limit_bytes=VMEM_BYTES, collective_id=3, has_side_effects=True
            ),
        )(*edges, conv, w_out)
    block = pl.BlockSpec((INNER, INNER), lambda k, pre: (0, k))
    return call(
        turn_kernel,
        (KERNEL,),
        [pl.BlockSpec((1, INNER, INNER), lambda k, pre: (k, 0, 0))],
        (block, block),
        (shape, shape),
        cost=cost_of(KERNEL * INNER**3, KERNEL * INNER * INNER * 6),
    )(pre, conv)


ORDERS = ((0, 1, 2, 3), (0, 1, 2, 3), (0, 2, 3, 1), (0, 1, 2, 3), (0, 1, 2, 3))
GIVE = 5
SCHEDULE = {
    1: [(5, 0), (0, 0)],
    2: [(2, 0), (0, 1), (1, 0)],
    3: [(5, 1), (2, 1)],
    5: [(1, 1), (3, 0)],
    7: [(0, 2), (2, 2), (5, 2)],
    8: [(3, 1)],
    9: [(1, 2), (5, 3)],
    10: [(0, 3)],
    12: [(5, 4), (2, 3), (3, 2), (1, 3), (0, 4), (4, 0), (0, 5), (4, 1), (2, 4), (5, 5), (3, 3), (1, 4)],
    13: [(4, 2)],
    14: [(1, 5), (0, 6), (3, 4), (2, 5), (4, 3), (1, 6), (0, 7), (3, 5), (5, 6)],
    15: [(2, 6), (1, 7), (3, 6)],
    16: [(4, 4), (4, 5), (2, 7), (0, 8), (3, 7), (5, 7), (1, 8), (0, 9), (4, 6), (5, 8), (4, 7), (2, 8), (3, 8), (4, 8), (5, 9), (1, 9), (4, 9), (2, 9), (3, 9)],
}


class Stream:
    def __init__(self, order, first, rows, arrays, slot):
        self.order, self.rows = order, rows
        self.acc, self.send, self.recv, self.swap, self.res, self.sems = arrays
        self.slot = slot
        self.levels = len(order)
        self.size = [rows >> (t + 1) for t in range(self.levels)]
        self.at = [rows - (rows >> t) for t in range(self.levels)]
        self.seq, self.ch = lax.axis_index("seq"), lax.axis_index("ch")
        self.low = [first]
        for t in range(self.levels):
            self.low.append(self.low[-1] + self.bit(order[t]) * self.size[t])

    def bit(self, b):
        return (self.seq // (1 << b)) % 2

    def partner(self, b):
        return {"seq": self.seq + (1 - 2 * self.bit(b)) * (1 << b)}

    def remote(self, src, dst, k, device):
        return pltpu.make_async_remote_copy(
            src_ref=src,
            dst_ref=dst,
            send_sem=self.sems[0].at[self.slot, k],
            recv_sem=self.sems[1].at[self.slot, k],
            device_id=device,
            device_id_type=pl.DeviceIdType.MESH,
        )

    def copy(self, k):
        if k < self.levels:
            window = pl.ds(self.at[k], self.size[k])
            held = self.send.at[:, pl.ds(0, self.size[k]), :]
            return self.remote(held, self.recv.at[:, window, :], k, self.partner(self.order[k]))
        if k == self.levels:
            return self.remote(self.swap.at[0], self.swap.at[1], k, {"ch": 1 - self.ch})
        t = 2 * self.levels - k
        place = spot(self.low[t + 1], 0, self.size[t])
        return self.remote(self.res.at[place, :], self.res.at[place, :], k, self.partner(self.order[t]))

    def start(self, k):
        if k < self.levels:
            away = self.low[k] + (1 - self.bit(self.order[k])) * self.size[k]
            for h in range(2):

                def pack(i, step, h=h):
                    self.send[h, spot(0, i, step), :] = self.acc[h, spot(away, i, step), :].astype(BF16)

                sliced(self.size[k], pack)
        elif k == self.levels:
            place = spot(self.low[-1], 0, self.size[-1])
            self.swap[0] = self.acc[1 - self.ch, place, :].astype(BF16)
        self.copy(k).start()

    def finish(self, k):
        self.copy(k).wait()
        if k < self.levels:
            for h in range(2):

                def add(i, step, h=h):
                    place = spot(self.low[k + 1], i, step)
                    self.acc[h, place, :] += self.recv[h, spot(self.at[k], i, step), :].astype(F32)

                sliced(self.size[k], add)
        elif k == self.levels:
            place = spot(self.low[-1], 0, self.size[-1])
            self.res[place, :] = (self.acc[self.ch, place, :] + self.swap[1].astype(F32)).astype(BF16)


def sliced(count, body):
    step = next(r for r in (96, 64, 48, 32, 16) if count % r == 0)

    def one(i, carry):
        body(pl.multiple_of(i * step, 16), step)
        return carry

    lax.fori_loop(0, count // step, one, 0)


def spot(base, i, step):
    return pl.ds(pl.multiple_of(base + i, 16), step)


HALF = INNER // 2
LEVELS = 4
EARLY_ROWS = HALF * (KERNEL + D // INNER)
ROWS = 768
SMALL_ROWS = 256


def stream_scratch():
    dma = pltpu.SemaphoreType.DMA
    out = [pltpu.VMEM((2, 4 * ROWS, INNER), F32)]
    moved = ROWS - (ROWS >> LEVELS)
    out += [pltpu.VMEM((2, ROWS // 2, INNER), BF16)] * 4
    out += [pltpu.VMEM((2, moved, INNER), BF16)] * 4
    out += [pltpu.VMEM((2, ROWS >> LEVELS, INNER), BF16)] * 4
    out += [pltpu.VMEM((4 * ROWS, INNER), BF16)]
    out += [
        pltpu.VMEM((2, SMALL_ROWS, LANES), F32),
        pltpu.VMEM((2, SMALL_ROWS // 2, LANES), BF16),
        pltpu.VMEM((2, SMALL_ROWS - (SMALL_ROWS >> LEVELS), LANES), BF16),
        pltpu.VMEM((2, SMALL_ROWS >> LEVELS, LANES), BF16),
        pltpu.VMEM((SMALL_ROWS, LANES), BF16),
    ]
    out += [dma((2 * (KERNEL + 2 * D // INNER),)), dma((5, 2 * LEVELS + 1)), dma((5, 2 * LEVELS + 1))]
    return out


def streams_of(refs):
    acc, send, recv, swap, res = refs[0], refs[1:5], refs[5:9], refs[9:13], refs[13]
    sems = refs[20:22]
    out = []
    for q, order in enumerate(ORDERS[:4]):
        out.append(Stream(order, q * ROWS, ROWS, (acc, send[q], recv[q], swap[q], res, sems), q))
    out.append(Stream(ORDERS[4], 0, SMALL_ROWS, (*refs[14:19], sems), 4))
    return out


def inner_kernel(group, pre, *refs):
    dconv_ref, before_ref, after_ref, mid_ref, hat_ref, gp_ref, scale_ref, first_ref, wc_ref, p2_ref = refs[:10]
    dn_ref, gcw_ref, gwi_ref, rows_ref = refs[10:14]
    pad_ref, cat_ref, d_ref, gg_ref, gb_ref, gbi_ref = refs[14:]
    length = mid_ref.shape[2]

    @pl.when(pl.program_id(0) == 0)
    def _():
        for ref in (gg_ref, gb_ref, gbi_ref):
            ref[...] = jnp.zeros_like(ref)

    cats = [cat_ref.at[:, j * length : (j + 1) * length] for j in range(TWO)]
    gather_windows(group, dconv_ref, before_ref, after_ref, pad_ref, cats, -1)
    d_ref[...] = jnp.dot(wc_ref[...], cat_ref[...], preferred_element_type=F32)
    mid = jnp.concatenate([mid_ref[j] for j in range(TWO)], axis=1)
    fresh = pl.program_id(0) == 0
    gcw = lax.dot_general(cat_ref[...], mid, (((1,), (1,)), ((), ())), preferred_element_type=F32)
    gcw_ref[...] = jnp.where(fresh, 0.0, gcw_ref[...]) + gcw

    def put(sl, v):
        for j in range(TWO):
            dn_ref[j, sl, :] = v[:, j * length : (j + 1) * length]

    norm_back(d_ref, gp_ref, hat_ref, across(scale_ref, 0), p2_ref, gg_ref, gb_ref, gbi_ref, put)
    dn = jnp.concatenate([dn_ref[j] for j in range(TWO)], axis=1)
    first = jnp.concatenate([first_ref[j] for j in range(TWO)], axis=1)
    gwi = lax.dot_general(dn, first, (((1,), (1,)), ((), ())), preferred_element_type=F32)
    gwi_ref[...] = jnp.where(fresh, 0.0, gwi_ref[...]) + gwi

    @pl.when(pl.program_id(0) == pl.num_programs(0) - 1)
    def _():
        for k, ref in enumerate((gbi_ref, gg_ref, gb_ref)):
            rows_ref[:, k * INNER : (k + 1) * INNER] = row_sums(ref)


def inner_call(pre, dconv, before, after, mid, hat, gp, scale, first, wc_t, p2, group):
    count, _, length = dconv.shape
    edge = pl.BlockSpec((1, INNER, group * REACH), lambda i, pre: (i // (group // TWO), 0, 0))
    own = pl.BlockSpec((TWO, INNER, length), lambda i, pre: (i, 0, 0))
    sums = [(KERNEL * INNER, INNER), (INNER, D), (8, 3 * INNER)]
    return call(
        functools.partial(inner_kernel, group),
        (count // TWO,),
        [
            own,
            edge,
            edge,
            own,
            own,
            own,
            pl.BlockSpec((TWO, 1, length), lambda i, pre: (i, 0, 0)),
            pl.BlockSpec((TWO, D, length), lambda i, pre: (i, 0, 0)),
            whole(wc_t.shape),
            whole((1, INNER, LANES), 1),
        ],
        tuple([own] + [const(v) for v in sums]),
        tuple([sds(dconv.shape, BF16)] + [sds(v, F32) for v in sums]),
        scratch=[
            pltpu.VMEM((TWO, INNER, length + 2 * LANES), BF16),
            pltpu.VMEM((KERNEL * INNER, TWO * length), BF16),
            pltpu.VMEM((INNER, TWO * length), F32),
        ]
        + [pltpu.VMEM((INNER, LANES), F32)] * 3,
        cost=cost_of(count * (2 * KERNEL * INNER + D) * INNER * length, KERNEL * INNER * INNER * 4),
    )(pre, dconv, before, after, mid, hat, gp, scale, first, wc_t, p2)


KINDS = [0, 0, 0, 0, 0, 0, 1, 0, 0, 1, 1, 1, 1, 1, 1, 1]


def turn_of(kind, step):
    steps = [k for k, v in enumerate(KINDS) if v == kind]
    return sum((jnp.asarray(step >= k).astype(jnp.int32) for k in steps[1:]), jnp.int32(0))


def is_turn(kind, step):
    return functools.reduce(jnp.logical_or, (step == k for k, v in enumerate(KINDS) if v == kind))


def tail_kernel(group, *refs):
    dn_ref, x_ref, stat_ref, mid_ref, lead_oth, trail_oth, wc_ref, wi_ref, p1_ref, p2_ref = refs[:10]
    rows_ref, rows_in_ref, gcw_ref, gwo_ref, gwi_ref = refs[10:15]
    w_in_ref, wi_ref = wi_ref, refs[-1]
    refs = refs[:-1]
    mine_ref, last_ref, total_ref, small_ref, got_ref = refs[15:20]
    stream_refs = refs[20:42]
    pad_ref, cat_ref, d_ref, give_ref, df_ref = refs[42:47]
    gg1_ref, gb1_ref, give_send, give_recv = refs[47:51]
    before_oth, after_oth, rim_send, rim_recv = refs[51:]
    rims = Rims(lead_oth, trail_oth, before_oth, after_oth, rim_send, rim_recv)
    acc, small_acc, res, small_res, load_sem = (stream_refs[k] for k in (0, 14, 13, 18, 19))
    base = 3 * ROWS
    share, length = give_ref.shape[1], give_ref.shape[2]
    seq, ch = lax.axis_index("seq"), lax.axis_index("ch")
    step, steps = pl.program_id(0), pl.num_programs(0)
    count = give_ref.shape[0]
    streams = streams_of(stream_refs)
    outer_now, conv_now = turn_of(0, step), turn_of(1, step)

    def loads():
        out = []
        for h in range(2):
            mine = pl.ds(h * HALF, HALF)
            pieces = [gcw_ref.at[k, mine, :] for k in range(KERNEL)]
            pieces += [gwo_ref.at[mine, pl.ds(j * INNER, INNER)] for j in range(D // INNER)]
            for j, piece in enumerate(pieces):
                out.append((piece, acc.at[h, pl.ds(j * HALF, HALF), :]))
            for j in range(D // INNER):
                piece = gwi_ref.at[mine, pl.ds(j * INNER, INNER)]
                out.append((piece, acc.at[h, pl.ds(base + j * HALF, HALF), :]))
        return [pltpu.make_async_copy(a, b, load_sem.at[j]) for j, (a, b) in enumerate(out)]

    def give(i):
        return pltpu.make_async_remote_copy(
            src_ref=give_ref.at[i],
            dst_ref=got_ref.at[i],
            send_sem=give_send.at[i],
            recv_sem=give_recv.at[i],
            device_id={"ch": 1 - ch},
            device_id_type=pl.DeviceIdType.MESH,
        )

    def fill_inner():
        inner = [ref[0:1, k * INNER : (k + 1) * INNER] for ref in (rows_in_ref, rows_ref) for k in range(3)]
        at = base + HALF * D // INNER
        for h in range(2):
            for k, v in enumerate(inner):
                acc[h, at + k : at + k + 1, :HALF] = v[:, h * HALF : (h + 1) * HALF]

    def fill_outer():
        small_acc[...] = jnp.zeros_like(small_acc)
        outer = [row_sums(ref)[0:1] for ref in (gg1_ref, gb1_ref)] + [rows_ref[0:1, 3 * INNER :]]
        for h in range(2):
            for k, v in enumerate(outer):
                for j in range(INNER // LANES):
                    lanes = slice(h * INNER + j * LANES, h * INNER + (j + 1) * LANES)
                    row = k * (INNER // LANES) + j
                    small_acc[h, row : row + 1, :] = v[:, lanes]

    def act(actions):
        for q, k in actions:
            if q == GIVE:
                if k > 1:
                    give(k - 2).wait()
                if k < count:
                    give(k).start()
                continue
            if k > 0:
                streams[q].finish(k - 1)
            elif q == 3:
                fill_inner()
            elif q == 4:
                fill_outer()
            if k <= 2 * LEVELS:
                streams[q].start(k)

    @pl.when(step == 0)
    def _():
        for h in range(2):
            acc[h, EARLY_ROWS:base, :] = jnp.zeros((base - EARLY_ROWS, INNER), F32)
            used = base + HALF * D // INNER
            acc[h, used:, :] = jnp.zeros((4 * ROWS - used, INNER), F32)
        for copy in loads():
            copy.start()
        before_oth[...] = jnp.zeros_like(before_oth)
        after_oth[...] = jnp.zeros_like(after_oth)
        barrier = pltpu.get_barrier_semaphore()
        for device in [streams[0].partner(b) for b in range(LEVELS)] + [{"ch": 1 - ch}]:
            pl.semaphore_signal(barrier, inc=1, device_id=device, device_id_type=pl.DeviceIdType.MESH)
        pl.semaphore_wait(barrier, LEVELS + 1 + rims.greet())
        rims.start()
        for ref in (gg1_ref, gb1_ref):
            ref[...] = jnp.zeros_like(ref)
        for j in range(D // INNER):
            block = slice(j * INNER, (j + 1) * INNER)
            wi_ref[block, :] = turned(w_in_ref[:, block])

    @pl.when(step == min(SCHEDULE))
    def _():
        for copy in loads():
            copy.wait()

    for at, actions in SCHEDULE.items():
        if at < len(KINDS):

            @pl.when(step == at)
            def _():
                act(actions)

    @pl.when(is_turn(0, step))
    def _():
        now = outer_now
        df_ref[...] = jnp.dot(wi_ref[...], dn_ref[0], preferred_element_type=F32)
        mean_in, scale_in = stat_ref[0, 0:1, :], stat_ref[0, 1:2, :]
        zero = jnp.zeros((8, length), F32)

        def inner(sl, carry):
            hat = (x_ref[0, sl, :].astype(F32) - mean_in) * scale_in
            gain = spread(p1_ref[0, sl, :], length)
            point = hat * gain + spread(p1_ref[1, sl, :], length)
            d_pre = df_ref[sl, :] * slope(point, cdf(point))
            gg1_ref[sl, :] += fold_lanes(d_pre * hat)
            gb1_ref[sl, :] += fold_lanes(d_pre)
            e = d_pre * gain
            df_ref[sl, :] = e
            return carry[0] + fold_rows(e), carry[1] + fold_rows(e * hat)

        total, dot = straight(D, length, inner, (zero, zero))
        total = total.sum(0, keepdims=True) * (scale_in / D)
        dot = dot.sum(0, keepdims=True) * (scale_in / D)
        for r in range(2):
            start = ((ch + r) % 2) * share

            def out(to, carry):
                rows = pl.ds(pl.multiple_of(start + to.start, 16), to.size)
                hat = (x_ref[0, rows, :].astype(F32) - mean_in) * scale_in
                v = (df_ref[rows, :] * scale_in - total - hat * dot).astype(BF16)
                if r == 0:
                    mine_ref[0, to, :] = v
                else:
                    give_ref[now, to, :] = v
                return carry

            straight(share, length, out, 0)

    pl.when(step == KINDS.index(1))(rims.wait)

    @pl.when(is_turn(1, step))
    def _():
        held = pl.ds(conv_now // group, 1)
        gather_windows(group, mid_ref, before_oth.at[held], after_oth.at[held], pad_ref, [cat_ref], 1, conv_now)
        conv = jnp.dot(wc_ref[...], cat_ref[...], preferred_element_type=F32)
        d_ref[...] = conv + spread(p2_ref[3], length)
        mean, scale = norm_stats(lambda sl: d_ref[sl, :], INNER, length)

        def body(sl, carry):
            hat = (d_ref[sl, :] - mean) * scale
            point = hat * spread(p2_ref[4, sl, :], length) + spread(p2_ref[5, sl, :], length)
            last_ref[0, sl, :] = (point * cdf(point)).astype(BF16)
            return carry

        straight(INNER, length, body, 0)

    @pl.when(step == steps - 1)
    def _():
        act(SCHEDULE[max(SCHEDULE)])
        done = [
            pltpu.make_async_copy(res, total_ref, load_sem.at[0]),
            pltpu.make_async_copy(small_res, small_ref, load_sem.at[1]),
        ]
        for copy in done:
            copy.start()
        for copy in done:
            copy.wait()


def tail_call(dn, tokens, stat, mid, rims_oth, wc, w_in, p1, p2, rows, rows_in, gcw, gwo, gwi, group):
    count, _, length = dn.shape
    share = D // 2
    any_spec = pl.BlockSpec(memory_space=pl.ANY)

    def fixed(shape):
        return pl.BlockSpec(shape, lambda i: (0,) * len(shape), pipeline_mode=pl.Buffered(1))

    def block(k, width):
        return pl.BlockSpec((1, width, length), lambda i: (turn_of(k, i), 0, 0))

    dma = pltpu.SemaphoreType.DMA
    return pl.pallas_call(
        functools.partial(tail_kernel, group),
        grid=(len(KINDS),),
        in_specs=[
            block(0, INNER),
            pl.BlockSpec((1, D, length), lambda i: (lax.axis_index("ch") * count + turn_of(0, i), 0, 0)),
            block(0, 2),
            block(1, INNER),
            any_spec,
            any_spec,
            fixed(wc.shape),
            fixed(w_in.shape),
            fixed(p1.shape),
            fixed(p2.shape),
            fixed(rows.shape),
            fixed(rows_in.shape),
            any_spec,
            any_spec,
            any_spec,
        ],
        out_specs=(block(0, share), block(1, INNER), any_spec, any_spec, any_spec),
        out_shape=(
            sds((count, share, length), BF16),
            sds((count, INNER, length), BF16),
            sds((4 * ROWS, INNER), BF16),
            sds((SMALL_ROWS, LANES), BF16),
            sds((count, share, length), BF16),
        ),
        scratch_shapes=stream_scratch()
        + [
            pltpu.VMEM((1, INNER, length + 2 * LANES), BF16),
            pltpu.VMEM((KERNEL * INNER, length), BF16),
            pltpu.VMEM((INNER, length), F32),
            pltpu.VMEM((count, share, length), BF16),
            pltpu.VMEM((D, length), F32),
            pltpu.VMEM((D, LANES), F32),
            pltpu.VMEM((D, LANES), F32),
            dma((count,)),
            dma((count,)),
            pltpu.VMEM(rims_oth[0].shape, BF16),
            pltpu.VMEM(rims_oth[0].shape, BF16),
            dma((2,)),
            dma((2,)),
            pltpu.VMEM((D, INNER), BF16),
        ],
        cost_estimate=cost_of(count * INNER * (KERNEL * INNER + D) * length * 4, 4 * ROWS * INNER * 12),
        compiler_params=pltpu.CompilerParams(
            vmem_limit_bytes=TAIL_BYTES, collective_id=2, has_side_effects=True
        ),
    )(dn, tokens, stat, mid, *rims_oth, wc, w_in, p1, p2, rows, rows_in, gcw, gwo, gwi)


TAIL_BYTES = 63 * 1024 * 1024


def finish_kernel(pre, mine_ref, got_ref, dy_ref, last_ref, x_ref, wo_ref, b_ref, total_ref, small_ref, _, *outs):
    gt_ref, mixed_ref, gcw_ref, gwi_ref, gwo_ref = outs[:5]
    inner_refs, outer_refs = outs[5:11], outs[11:]
    length = dy_ref.shape[2]
    step, count = pl.program_id(0), pl.num_programs(0) // 2
    part = gcw_ref.shape[1]

    @pl.when(step < count)
    def _():
        gt_ref[...] = mine_ref[...].astype(F32) + dy_ref[...].astype(F32)

    @pl.when(step >= count)
    def _():
        gt_ref[...] = got_ref[...].astype(F32) + dy_ref[...].astype(F32)

    branch = jnp.dot(wo_ref[...], last_ref[0], preferred_element_type=F32)
    mixed_ref[0] = (x_ref[0].astype(F32) + branch + spread(b_ref[...], length)).astype(BF16)
    for k in range(KERNEL):

        @pl.when(step == k)
        def _():
            gcw_ref[0] = total_ref[k * part : (k + 1) * part, :].astype(F32)

    for k, (ref, start) in enumerate(((gwo_ref, KERNEL * part), (gwi_ref, 3 * ROWS))):

        @pl.when(step == KERNEL + k)
        def _():
            for j in range(D // INNER):
                ref[:, j * INNER : (j + 1) * INNER] = total_ref[start + j * part : start + (j + 1) * part, :].astype(F32)

    @pl.when(step == 0)
    def _():
        at = 3 * ROWS + part * D // INNER
        rows = total_ref[at : at + 16, :].astype(F32)
        for k, ref in enumerate(inner_refs):
            ref[...] = rows[k, :part]
        rows = small_ref[:16, :].astype(F32)
        each = outer_refs[0].shape[0] // LANES
        for k, ref in enumerate(outer_refs):
            for j in range(each):
                ref[j * LANES : (j + 1) * LANES] = rows[k * each + j]


def finish_call(pre, mine, got, cot, last, tokens, wo_t, b_out, total, small, mixed, part):
    seqs, share, length = cot.shape
    count = got.shape[0] // TWO
    early = lambda i: jnp.minimum(i, count - 1)
    late = lambda i: jnp.maximum(i - count, 0)
    return call(
        finish_kernel,
        (2 * count,),
        [
            pl.BlockSpec((TWO, share, length), lambda i, pre: (early(i), 0, 0)),
            pl.BlockSpec((TWO, share, length), lambda i, pre: (late(i), 0, 0)),
            pl.BlockSpec((TWO, share, length), lambda i, pre: ((pre[0] // TWO + i) % (seqs // TWO), 0, 0)),
            pl.BlockSpec((1, INNER, length), lambda i, pre: (i, 0, 0)),
            pl.BlockSpec((1, share, length), lambda i, pre: (pre[2] + i, pre[1], 0)),
            whole(wo_t.shape),
            whole(b_out.shape),
            whole(total.shape),
            whole(small.shape),
            pl.BlockSpec(memory_space=pl.ANY),
        ],
        (
            pl.BlockSpec((TWO, share, length), lambda i, pre: ((pre[0] // TWO + i) % (seqs // TWO), 0, 0)),
            pl.BlockSpec((1, share, length), lambda i, pre: (pre[2] + i, 0, 0)),
            pl.BlockSpec((1, part, INNER), lambda i, pre: (jnp.minimum(i, KERNEL - 1), 0, 0)),
            const((part, D)),
            const((part, D)),
            *[const((part,))] * 6,
            *[const((share,))] * 3,
        ),
        (
            sds((seqs, share, length), F32),
            sds(mixed.shape, BF16),
            sds((KERNEL, part, INNER), F32),
            sds((part, D), F32),
            sds((part, D), F32),
            *[sds((part,), F32)] * 6,
            *[sds((share,), F32)] * 3,
        ),
        aliases={10: 1},
    )(pre, mine, got, cot, last, tokens, wo_t, b_out, total, small, mixed)


def rotate(value, axis, count, by):
    return lax.ppermute(value, axis, [(i, (i + by) % count) for i in range(count)])


def shift(value, by):
    count = lax.axis_size("seq")
    pairs = [(i, i + by) for i in range(count) if 0 <= i + by < count]
    return lax.ppermute(value, "seq", pairs)


def rims(lead, trail):
    return shift(trail, 1), shift(lead, -1)


def own_slice(value, width, dim):
    return lax.dynamic_slice_in_dim(value, lax.axis_index("ch") * width, width, dim)


def lane_copies(vectors):
    return jnp.broadcast_to(vectors[..., None], vectors.shape + (LANES,))


def body(
    tokens,
    pad_mask,
    cotangent,
    ln1_gain,
    first_norm_bias,
    w_in,
    b_in,
    ln2_gain,
    ln2_bias,
    conv_w,
    conv_b,
    ln3_gain,
    ln3_bias,
    w_out,
    b_out,
):
    chs = lax.axis_size("ch")
    ch = lax.axis_index("ch")
    seqs, _, length = tokens.shape
    share = b_out.shape[0]
    part = b_in.shape[0]
    n = seqs // chs
    group = min(4, n)
    starts = [((ch + chs - r) % chs) * n for r in range(1, chs)]
    pre = jnp.stack([ch * n, ch] + starts).astype(jnp.int32)
    pair = chs == 2 and lax.axis_size("seq") == 1 << LEVELS

    p1 = lane_copies(jnp.stack([ln1_gain, first_norm_bias]))
    bo = lane_copies(b_out)
    vectors = [b_in, ln2_gain, ln2_bias, conv_b, ln3_gain, ln3_bias]
    if pair:
        vec = jnp.pad(jnp.concatenate(vectors), (0, 2048 - 6 * part)).reshape(16, LANES)
        first, stat, w_in_full, conv_full, w_out_full, vec_full, away = first_call(
            pre, tokens, p1, (w_in, conv_w, w_out), vec, cotangent
        )
        others = [rotate(away, "ch", chs, 1)]
        vec_full = vec_full.reshape(2, 2048)[:, : 6 * part].reshape(2, 6, part)
        inner = vec_full.transpose(1, 0, 2).reshape(6, INNER)
    else:
        first, stat = first_call(pre, tokens, p1, None, None)
        w_in_full = lax.all_gather(w_in, "ch", axis=0, tiled=True)
        conv_full = lax.all_gather(conv_w, "ch", axis=1, tiled=True)
        w_out_full = lax.all_gather(w_out, "ch", axis=0, tiled=True)
        inner = lax.all_gather(jnp.stack(vectors), "ch", axis=1, tiled=True)
        others = []
        for r in range(1, chs):
            block = lax.dynamic_slice_in_dim(cotangent, ((ch + r) % chs) * n, n, 0)
            others.append(rotate(block, "ch", chs, r))

    p2 = lane_copies(inner)
    mid_own, lead, trail, hat_mid, gp_mid, scale_mid = middle_call(
        pre, first, pad_mask, w_in_full, p2, n, 0, group, True
    )
    if pair:
        wc, wc_t, before, after, wo_t = turn_call(pre, conv_full, (lead, trail), w_out_full)
    else:
        wo_t = lax.dynamic_slice_in_dim(w_out_full, ch * share, share, 1).T
        wc, wc_t = turn_call(pre, conv_full)
        before, after = rims(lead, trail)
        mid_oth, lead, trail = middle_call(pre, first, pad_mask, w_in_full, p2, seqs - n, n, group, False)
        rims_oth = rims(lead, trail)
    mixed, hat_out, gp_out, scale_out, last_own = last_call(
        pre, mid_own, before, after, tokens, wc, wo_t, p2, bo, n, 0, group, True, None
    )
    dconv, lead, trail, gg3, gb3, gcb, gwo, gbo, rows = rear_call(
        pre, cotangent, others, w_out_full, hat_out, gp_out, last_own, scale_out, p2, group
    )
    if pair:
        mid_oth, lead_oth, trail_oth, lead, trail = middle_rims_call(
            (lead, trail), first, pad_mask, w_in_full, p2, n, group
        )
        rims_oth = (lead_oth, trail_oth)
    else:
        lead, trail = rims(lead, trail)
    if pair:
        dn, gcw, gwi, rows_in = inner_call(
            pre, dconv, lead, trail, mid_own, hat_mid, gp_mid, scale_mid, first, wc_t, p2, group
        )
        mine, last_oth, total, small, got = tail_call(
            dn, tokens, stat, mid_oth, rims_oth, wc, w_in_full, p1, p2, rows, rows_in,
            gcw.reshape(KERNEL, INNER, INNER), gwo, gwi, group,
        )
        gt, mixed, gcw, gwi, gwo, *sums = finish_call(
            pre, mine, got, cotangent, last_oth, tokens, wo_t, bo, total, small, mixed, part
        )
        inner_sums, outer_sums = sums[:6], sums[6:]
    else:
        gt, *rest = front_call(
            pre, dconv, lead, trail, mid_own, hat_mid, gp_mid, scale_mid, tokens, stat, cotangent,
            wc_t, w_in_full.T, p2, p1, chs, group,
        )
        sends = [rotate(v, "ch", chs, r + 1) for r, v in enumerate(rest[: chs - 1])]
        gcw, gwi, gg2, gb2, gbi, gg1, gb1 = rest[chs - 1 :]
        gcw = gcw.reshape(KERNEL, INNER, INNER)
        inner_sums = jnp.stack([v.sum(1) for v in (gbi, gg2, gb2, gcb, gg3, gb3)])
        outer_sums = jnp.stack([v.sum(1) for v in (gg1, gb1, gbo)])
        mixed, = last_call(
            pre, mid_oth, *rims_oth, tokens, wc, wo_t, p2, bo, seqs - n, n, group, False, mixed
        )
        gcw, gwi, gwo, inner_sums, outer_sums = lax.psum((gcw, gwi, gwo, inner_sums, outer_sums), ("seq", "ch"))
        gcw = own_slice(gcw, part, 1)
        gwi = own_slice(gwi, part, 0)
        gwo = own_slice(gwo, part, 0)
        inner_sums = own_slice(inner_sums, part, 1)
        outer_sums = own_slice(outer_sums, share, 1)
        for r in range(chs - 1):
            gt = add_call(pre, sends[r], cotangent, gt, 2 + r)
    return (
        mixed,
        gt,
        outer_sums[0],
        outer_sums[1],
        gwi,
        inner_sums[0],
        inner_sums[1],
        inner_sums[2],
        gcw,
        inner_sums[3],
        inner_sums[4],
        inner_sums[5],
        gwo,
        outer_sums[2],
    )


def solution(mesh):
    in_specs = (
        P(None, None, "seq"),
        P(None, "seq"),
        P(None, "ch", "seq"),
        P(),
        P(),
        P("ch", None),
        P("ch"),
        P("ch"),
        P("ch"),
        P(None, "ch", None),
        P("ch"),
        P("ch"),
        P("ch"),
        P("ch", None),
        P("ch"),
    )
    out_specs = (
        P(None, "ch", "seq"),
        P(None, "ch", "seq"),
        P("ch"),
        P("ch"),
        P("ch", None),
        P("ch"),
        P("ch"),
        P("ch"),
        P(None, "ch", None),
        P("ch"),
        P("ch"),
        P("ch"),
        P("ch", None),
        P("ch"),
    )
    return jax.shard_map(body, mesh=mesh, in_specs=in_specs, out_specs=out_specs, check_vma=False)
```

```python
import functools
import math

import jax
import jax.numpy as jnp
from jax import lax
from jax.experimental import pallas as pl
from jax.experimental.pallas import tpu as pltpu
from jax.sharding import PartitionSpec as P

D = 1280
INNER = 640
KERNEL = 5
DILATION = 16
REACH = KERNEL // 2 * DILATION
EPS = 1e-05
HALF_ROOT = math.sqrt(0.5)
DENSITY = 1.0 / math.sqrt(2.0 * math.pi)
F32 = jnp.float32
BF16 = jnp.bfloat16
LANES = 128
VMEM_BYTES = 60 * 1024 * 1024


TWO = 2


def rows_of(width):
    return next(r for r in (64, 32, 16) if width % r == 0)


def straight(width, length, body, init):
    rows = next(r for r in (64, 32, 16) if width % r == 0 and r * length <= 64 * 256 or r == 16)
    for i in range(width // rows):
        init = body(pl.ds(i * rows, rows), init)
    return init


def fold_rows(v):
    return v.reshape(v.shape[0] // 8, 8, v.shape[1]).sum(0)


def fold_lanes(v):
    out = v[:, :LANES]
    for j in range(1, v.shape[1] // LANES):
        out = out + v[:, j * LANES : (j + 1) * LANES]
    return out


def spread(p, length):
    return jnp.concatenate([p] * (length // LANES), axis=1)


def loop(width, body, init):
    rows = rows_of(width)

    def step(i, carry):
        return body(pl.ds(pl.multiple_of(i * rows, rows), rows), carry)

    return lax.fori_loop(0, width // rows, step, init)


def norm_stats(load, width, length, rolled=False):
    def over(body, init):
        return loop(width, body, init) if rolled else straight(width, length, body, init)

    zero = jnp.zeros((8, length), F32)
    total = over(lambda sl, a: a + fold_rows(load(sl)), zero)
    mean = total.sum(0, keepdims=True) / width

    def square(sl, a):
        c = load(sl) - mean
        return a + fold_rows(c * c)

    total = over(square, zero)
    return mean, lax.rsqrt(total.sum(0, keepdims=True) / width + EPS)


def cdf(p):
    return 0.5 + 0.5 * lax.erf(p * HALF_ROOT)


def slope(p, phi):
    return phi + p * (DENSITY * jnp.exp(p * p * -0.5))


def call(kernel, grid, in_specs, out_specs, out_shape, scratch=(), prefetch=1, aliases=None, cost=None):
    return pl.pallas_call(
        kernel,
        grid_spec=pltpu.PrefetchScalarGridSpec(
            num_scalar_prefetch=prefetch,
            grid=grid,
            in_specs=in_specs,
            out_specs=out_specs,
            scratch_shapes=list(scratch),
        ),
        out_shape=out_shape,
        input_output_aliases=aliases or {},
        cost_estimate=cost,
        compiler_params=pltpu.CompilerParams(vmem_limit_bytes=VMEM_BYTES),
    )


def cost_of(macs, bytes_accessed):
    return pl.CostEstimate(flops=int(2 * macs), bytes_accessed=int(bytes_accessed), transcendentals=0)


def whole(shape, at=0):
    return pl.BlockSpec(shape, lambda i, pre: (at,) + (0,) * (len(shape) - 1), pipeline_mode=pl.Buffered(1))


def sds(shape, dtype):
    return jax.ShapeDtypeStruct(shape, dtype)


def weight_copies(own_refs, full_refs, sems):
    seq, ch = lax.axis_index("seq"), lax.axis_index("ch")
    core, row = seq % 2, (seq // 2) % 2
    send_sem, recv_sem = sems
    across, along, beside = {"ch": 1 - ch}, {"seq": seq + 2 - 4 * row}, {"seq": seq + 1 - 2 * core}

    def part(ref, at, size):
        at = pl.multiple_of(at, 16)
        return ref.at[:, pl.ds(at, size), :] if len(ref.shape) == 3 else ref.at[pl.ds(at, size), :]

    (w_in, conv, w_out), (w_in_full, conv_full, w_out_full) = own_refs, full_refs
    items = [
        (w_in, w_in_full),
        (conv.at[pl.ds(0, 2)], conv_full.at[pl.ds(0, 2)]),
        (conv.at[pl.ds(2, 3)], conv_full.at[pl.ds(2, 3)]),
        (w_out, w_out_full),
    ]
    local, first_hop, second_hop, third_hop = [], [], [], []
    for k, (own, full) in enumerate(items):
        half = own.shape[-2]
        size = half // 4

        def remote(src, dst, slot, device):
            return pltpu.make_async_remote_copy(
                src_ref=src,
                dst_ref=dst,
                send_sem=send_sem.at[k, slot],
                recv_sem=recv_sem.at[k, slot],
                device_id=device,
                device_id_type=pl.DeviceIdType.MESH,
            )

        quarter = (row * 2 + core) * size
        local.append(remote(own, part(full, ch * half, half), 4, beside))
        first_hop.append(remote(part(own, quarter, size), part(full, ch * half + quarter, size), 0, across))
        landed = (1 - ch) * half
        mine = part(full, landed + quarter, size)
        second_hop.append(remote(mine, mine, 1, along))
        both = []
        for j, r in enumerate((row, 1 - row)):
            piece = part(full, landed + (r * 2 + core) * size, size)
            both.append(remote(piece, piece, 2 + j, beside))
        third_hop.append(both)
    return local, first_hop, second_hop, third_hop


def first_kernel(comm, pre, x_ref, p_ref, *rest):
    if comm:
        own_refs, own_vec, cot_ref, first_ref, stat_ref = rest[:3], rest[3], rest[4], rest[5], rest[6]
        full_refs, full_vec, away_ref = rest[7:10], rest[10], rest[11]
        exchange(own_refs, own_vec, full_refs, full_vec, rest[12:14], rest[14:])

        @pl.when(pl.program_id(0) < pl.num_programs(0) // 2)
        def _():
            away_ref[...] = cot_ref[...]

    else:
        first_ref, stat_ref = rest
    length = x_ref.shape[2]
    mean, scale = norm_stats(lambda sl: x_ref[0, sl, :].astype(F32), D, length, True)
    stat_ref[0, 0:1, :] = mean
    stat_ref[0, 1:2, :] = scale

    def body(sl, carry):
        hat = (x_ref[0, sl, :].astype(F32) - mean) * scale
        point = hat * spread(p_ref[0, sl, :], length) + spread(p_ref[1, sl, :], length)
        first_ref[0, sl, :] = (point * cdf(point)).astype(BF16)
        return carry

    loop(D, body, 0)


def exchange(own_refs, own_vec, full_refs, full_vec, sems, vec_sems):
    step, steps = pl.program_id(0), pl.num_programs(0)
    seq, ch = lax.axis_index("seq"), lax.axis_index("ch")
    core, row = seq % 2, (seq // 2) % 2
    local, first_hop, second_hop, third_hop = weight_copies(own_refs, full_refs, sems)
    vec_local = pltpu.make_async_copy(own_vec, full_vec.at[ch], vec_sems[0])
    vec_remote = pltpu.make_async_remote_copy(
        src_ref=own_vec,
        dst_ref=full_vec.at[ch],
        send_sem=vec_sems[1],
        recv_sem=vec_sems[2],
        device_id={"ch": 1 - ch},
        device_id_type=pl.DeviceIdType.MESH,
    )

    @pl.when(step == 0)
    def _():
        barrier = pltpu.get_barrier_semaphore()
        for device in ({"ch": 1 - ch}, {"seq": seq + 2 - 4 * row}, {"seq": seq + 1 - 2 * core}):
            pl.semaphore_signal(barrier, inc=1, device_id=device, device_id_type=pl.DeviceIdType.MESH)
        pl.semaphore_wait(barrier, 3)
        vec_remote.start()
        first_hop[0].start()
        vec_local.start()
        for copy in local:
            copy.start()

    for k in range(4):

        if k > 0:

            @pl.when(step == (0, 1, 3, 5)[k])
            def _():
                first_hop[k].start()

        @pl.when(step == (4, 7, 10, 12)[k])
        def _():
            first_hop[k].wait()
            second_hop[k].start()
            third_hop[k][0].start()

        @pl.when(step == (7, 10, 14, 15)[k])
        def _():
            second_hop[k].wait()
            third_hop[k][1].start()

    @pl.when(step == steps - 1)
    def _():
        vec_remote.wait()
        vec_local.wait()
        for k in range(4):
            local[k].wait()
            third_hop[k][0].wait()
            third_hop[k][1].wait()


def first_call(pre, tokens, p1, weights, vec, cot=None):
    seqs, _, length = tokens.shape
    comm = weights is not None
    any_spec = pl.BlockSpec(memory_space=pl.ANY)
    in_specs = [pl.BlockSpec((1, D, length), lambda i, pre: ((pre[0] + i) % seqs, 0, 0)), whole((2, D, LANES))]
    out_specs = [
        pl.BlockSpec((1, D, length), lambda i, pre: (i, 0, 0)),
        pl.BlockSpec((1, 2, length), lambda i, pre: (i, 0, 0)),
    ]
    shapes = [sds((seqs, D, length), BF16), sds((seqs, 2, length), F32)]
    args, scratch = [pre, tokens, p1], []
    if comm:
        in_specs += [any_spec] * 4
        out_specs += [any_spec] * 4
        shapes += [sds(w.shape[:-2] + (2 * w.shape[-2], w.shape[-1]), BF16) for w in weights]
        shapes.append(sds((2,) + vec.shape, F32))
        args += list(weights) + [vec]
        dma = pltpu.SemaphoreType.DMA
        scratch = [dma((4, 5)), dma((4, 5)), dma, dma, dma]

    def kernel(*refs):
        first_kernel(comm, *refs)

    if comm:

        def at(i):
            return ((lax.axis_index("ch") * (seqs // 2) + i) % seqs, 0, 0)

        n, share = seqs // 2, cot.shape[1]

        def away(i):
            return ((1 - lax.axis_index("ch")) * n + jnp.minimum(i, n - 1), 0, 0)

        shapes.append(sds((n, share, length), BF16))
        args.append(cot)

        return pl.pallas_call(
            lambda *refs: first_kernel(True, None, *refs),
            grid=(seqs,),
            in_specs=[
                pl.BlockSpec((1, D, length), at),
                pl.BlockSpec((2, D, LANES), lambda i: (0, 0, 0), pipeline_mode=pl.Buffered(1)),
            ]
            + [any_spec] * 4
            + [pl.BlockSpec((1, share, length), away)],
            out_specs=tuple(
                [pl.BlockSpec((1, D, length), lambda i: (i, 0, 0)), pl.BlockSpec((1, 2, length), lambda i: (i, 0, 0))]
                + [any_spec] * 4
                + [pl.BlockSpec((1, share, length), lambda i: (jnp.minimum(i, n - 1), 0, 0))]
            ),
            out_shape=tuple(shapes),
            scratch_shapes=scratch,
            cost_estimate=cost_of(seqs * D * length * 40, seqs * D * length * 4),
            compiler_params=pltpu.CompilerParams(
                vmem_limit_bytes=VMEM_BYTES, collective_id=1, has_side_effects=True
            ),
        )(*args[1:])
    return call(kernel, (seqs,), in_specs, tuple(out_specs), tuple(shapes))(*args)


class Rims:
    def __init__(self, lead, trail, before, after, send_sem, recv_sem):
        self.seq, self.count = lax.axis_index("seq"), lax.axis_size("seq")
        self.before, self.after = before, after

        def remote(src, dst, k, by):
            return pltpu.make_async_remote_copy(
                src_ref=src,
                dst_ref=dst,
                send_sem=send_sem.at[k],
                recv_sem=recv_sem.at[k],
                device_id={"seq": self.seq + by},
                device_id_type=pl.DeviceIdType.MESH,
            )

        self.up = lambda: remote(trail, before, 0, 1)
        self.down = lambda: remote(lead, after, 1, -1)
        self.has_up, self.has_down = self.seq < self.count - 1, self.seq > 0

    def greet(self):
        barrier = pltpu.get_barrier_semaphore()
        for there, by in ((self.has_up, 1), (self.has_down, -1)):

            @pl.when(there)
            def _():
                pl.semaphore_signal(
                    barrier, inc=1, device_id={"seq": self.seq + by}, device_id_type=pl.DeviceIdType.MESH
                )
        return self.has_up.astype(jnp.int32) + self.has_down.astype(jnp.int32)

    def start(self):
        pl.when(self.has_up)(lambda: self.up().start())
        pl.when(self.has_down)(lambda: self.down().start())

    def wait(self):
        @pl.when(self.has_up)
        def _():
            self.up().wait_send()
            self.down().wait_recv()

        @pl.when(self.has_down)
        def _():
            self.down().wait_send()
            self.up().wait_recv()


def rim_steps(lead, trail, before, after, zeros, send_sem, recv_sem, local_sem):
    rims = Rims(lead, trail, before, after, send_sem, recv_sem)
    step, steps = pl.program_id(0), pl.num_programs(0)
    ends = (
        (jnp.logical_not(rims.has_down), lambda: pltpu.make_async_copy(zeros, before, local_sem.at[0])),
        (jnp.logical_not(rims.has_up), lambda: pltpu.make_async_copy(zeros, after, local_sem.at[1])),
    )

    @pl.when(step == 0)
    def _():
        zeros[...] = jnp.zeros_like(zeros)
        pl.semaphore_wait(pltpu.get_barrier_semaphore(), rims.greet())
        rims.start()
        for there, copy in ends:
            pl.when(there)(lambda: copy().start())

    def last():
        rims.wait()
        for there, copy in ends:
            pl.when(there)(lambda: copy().wait())

    pl.when(step == steps - 1)(last)


def rim_scratch(shape):
    dma = pltpu.SemaphoreType.DMA
    return [pltpu.VMEM(shape, BF16), dma((2,)), dma((2,)), dma((2,))]


def put_edges(group, ref, lead_ref, trail_ref):
    length = ref.shape[2]
    place = pl.program_id(0) % (group // TWO)
    for k in range(group // TWO):

        @pl.when(place == k)
        def _():
            for j in range(TWO):
                lanes = slice((k * TWO + j) * REACH, (k * TWO + j + 1) * REACH)
                lead_ref[0, :, lanes] = ref[j, :, :REACH]
                trail_ref[0, :, lanes] = ref[j, :, length - REACH :]


def middle_rims_kernel(group, lead_in, trail_in, first_ref, mask_ref, w_ref, p_ref, *rest):
    rim_steps(lead_in, trail_in, *rest[3:5], *rest[5:9])
    middle_kernel(group, False, None, first_ref, mask_ref, w_ref, p_ref, *rest[:3], *rest[9:])


def middle_rims_call(edges, first, mask, w_in, p2, count, group):
    _, _, length = first.shape
    seqs = mask.shape[0]
    edge = pl.BlockSpec((1, INNER, group * REACH), lambda i: (i // (group // TWO), 0, 0))
    edge_shape = sds((count // group, INNER, group * REACH), BF16)
    any_spec = pl.BlockSpec(memory_space=pl.ANY)

    def fixed(shape):
        return pl.BlockSpec(shape, lambda i: (0,) * len(shape), pipeline_mode=pl.Buffered(1))

    def mask_at(i):
        return (((lax.axis_index("ch") + 1) * (count // TWO) + i) % (seqs // TWO), 0, 0)

    return pl.pallas_call(
        functools.partial(middle_rims_kernel, group),
        grid=(count // TWO,),
        in_specs=[
            any_spec,
            any_spec,
            pl.BlockSpec((TWO, D, length), lambda i: (count // TWO + i, 0, 0)),
            pl.BlockSpec((TWO, 1, length), mask_at),
            fixed((INNER, D)),
            fixed((3, INNER, LANES)),
        ],
        out_specs=(pl.BlockSpec((TWO, INNER, length), lambda i: (i, 0, 0)), edge, edge, any_spec, any_spec),
        out_shape=(sds((count, INNER, length), BF16), *[edge_shape] * 4),
        scratch_shapes=rim_scratch(edge_shape.shape) + [pltpu.VMEM((INNER, length), F32)] * TWO,
        cost_estimate=cost_of(count * INNER * D * length * 1.5, count * (D + INNER * 3) * length * 2),
        compiler_params=pltpu.CompilerParams(vmem_limit_bytes=VMEM_BYTES, collective_id=4, has_side_effects=True),
    )(*edges, first, mask.reshape(seqs, 1, length), w_in, p2)


def middle_kernel(group, keep, pre, first_ref, mask_ref, w_ref, p_ref, mid_ref, lead_ref, trail_ref, *rest):
    nar_refs = rest[-TWO:]
    length = first_ref.shape[2]
    for j in range(TWO):
        nar = jnp.dot(w_ref[...], first_ref[j], preferred_element_type=F32)
        nar_refs[j][...] = nar + spread(p_ref[0], length)
    for j in range(TWO):
        nar_ref = nar_refs[j]
        mean, scale = norm_stats(lambda sl: nar_ref[sl, :], INNER, length)
        mask = mask_ref[j].astype(F32)

        def body(sl, carry):
            hat = (nar_ref[sl, :] - mean) * scale
            point = hat * spread(p_ref[1, sl, :], length) + spread(p_ref[2, sl, :], length)
            phi = cdf(point)
            mid_ref[j, sl, :] = (point * phi * mask).astype(BF16)
            if keep:
                rest[0][j, sl, :] = hat.astype(BF16)
                rest[1][j, sl, :] = slope(point, phi) * mask
            return carry

        straight(INNER, length, body, 0)
        if keep:
            rest[2][j] = scale
    put_edges(group, mid_ref, lead_ref, trail_ref)


def middle_call(pre, first, mask, w_in, p2, count, offset, group, keep):
    _, _, length = first.shape
    seqs = mask.shape[0]
    edge = pl.BlockSpec((1, INNER, group * REACH), lambda i, pre: (i // (group // TWO), 0, 0))
    edge_shape = sds((count // group, INNER, group * REACH), BF16)
    own = pl.BlockSpec((TWO, INNER, length), lambda i, pre: (i, 0, 0))
    outs = [own, edge, edge]
    shapes = [sds((count, INNER, length), BF16), edge_shape, edge_shape]
    if keep:
        outs += [own, own, pl.BlockSpec((TWO, 1, length), lambda i, pre: (i, 0, 0))]
        shapes += [
            sds((count, INNER, length), BF16),
            sds((count, INNER, length), F32),
            sds((count, 1, length), F32),
        ]
    return call(
        functools.partial(middle_kernel, group, keep),
        (count // TWO,),
        [
            pl.BlockSpec((TWO, D, length), lambda i, pre: (offset // TWO + i, 0, 0)),
            pl.BlockSpec((TWO, 1, length), lambda i, pre: (((pre[0] + offset) // TWO + i) % (seqs // TWO), 0, 0)),
            whole((INNER, D)),
            whole((3, INNER, LANES)),
        ],
        tuple(outs),
        tuple(shapes),
        scratch=[pltpu.VMEM((INNER, length), F32)] * TWO,
        cost=cost_of(count * INNER * D * length * 1.5, count * (D + INNER * 3) * length * 2),
    )(pre, first, mask.reshape(seqs, 1, length), w_in, p2)


def gather_windows(group, body_ref, before_ref, after_ref, pad_ref, cat_refs, order, step=None):
    width, length, count = body_ref.shape[1], body_ref.shape[2], len(cat_refs)
    place = (pl.program_id(0) if step is None else step) % (group // count)
    for k in range(group // count):

        @pl.when(place == k)
        def _():
            for j in range(count):
                lanes = slice((k * count + j) * REACH, (k * count + j + 1) * REACH)
                pad_ref[j, :, LANES - REACH : LANES] = before_ref[0, :, lanes]
                pad_ref[j, :, LANES + length : LANES + length + REACH] = after_ref[0, :, lanes]

    for j in range(count):
        pad_ref[j, :, LANES : LANES + length] = body_ref[j]
        for tap in range(KERNEL):
            start = LANES + order * (tap - KERNEL // 2) * DILATION
            cat_refs[j][tap * width : (tap + 1) * width, :] = pad_ref[j, :, start : start + length]


def last_kernel(
    group, keep, pre, mid_ref, before_ref, after_ref, x_ref, wc_ref, wo_ref, p_ref, b_ref, *rest
):
    if keep:
        mixed_ref, hat_ref, gp_ref, scale_ref, last_out = rest[:5]
        last_refs = [last_out.at[j] for j in range(TWO)]
    else:
        mixed_ref = rest[1]
        last_refs = rest[-TWO:]
        rest = rest[:-TWO]
    pad_ref, cat_refs, conv_refs = rest[-1 - 2 * TWO], rest[-2 * TWO : -TWO], rest[-TWO:]
    length = mid_ref.shape[2]
    gather_windows(group, mid_ref, before_ref, after_ref, pad_ref, cat_refs, 1)
    for j in range(TWO):
        conv = jnp.dot(wc_ref[...], cat_refs[j][...], preferred_element_type=F32)
        conv_refs[j][...] = conv + spread(p_ref[0], length)
    for j in range(TWO):
        conv_ref, last_ref = conv_refs[j], last_refs[j]
        mean, scale = norm_stats(lambda sl: conv_ref[sl, :], INNER, length)

        def body(sl, carry):
            hat = (conv_ref[sl, :] - mean) * scale
            point = hat * spread(p_ref[1, sl, :], length) + spread(p_ref[2, sl, :], length)
            phi = cdf(point)
            last_ref[sl, :] = (point * phi).astype(BF16)
            if keep:
                hat_ref[j, sl, :] = hat.astype(BF16)
                gp_ref[j, sl, :] = slope(point, phi)
            return carry

        straight(INNER, length, body, 0)
        if keep:
            scale_ref[j] = scale
        branch = jnp.dot(wo_ref[...], last_ref[...], preferred_element_type=F32)
        mixed_ref[j] = (x_ref[j].astype(F32) + branch + spread(b_ref[...], length)).astype(BF16)


def last_call(pre, mid, before, after, tokens, wc, wo_t, p2, b_out, count, offset, group, keep, mixed):
    _, _, length = mid.shape
    seqs, share = tokens.shape[0], wo_t.shape[0]
    edge = pl.BlockSpec((1, INNER, group * REACH), lambda i, pre: (i // (group // TWO), 0, 0))
    own = pl.BlockSpec((TWO, INNER, length), lambda i, pre: (i, 0, 0))

    def pair_at(i, pre):
        return ((pre[0] + offset) // TWO + i) % (seqs // TWO)

    outs = [pl.BlockSpec((TWO, share, length), lambda i, pre: (pair_at(i, pre), 0, 0))]
    shapes = [sds((seqs, share, length), BF16)]
    in_specs = [
        own,
        edge,
        edge,
        pl.BlockSpec((TWO, share, length), lambda i, pre: (pair_at(i, pre), pre[1], 0)),
        whole((INNER, KERNEL * INNER)),
        whole((share, INNER)),
        whole((3, INNER, LANES), 1),
        whole((share, LANES)),
    ]
    args = [pre, mid, before, after, tokens, wc, wo_t, p2, b_out]
    aliases = None
    scratch = [pltpu.VMEM((TWO, INNER, length + 2 * LANES), BF16)]
    scratch += [pltpu.VMEM((KERNEL * INNER, length), BF16)] * TWO
    scratch += [pltpu.VMEM((INNER, length), F32)] * TWO
    if keep:
        outs += [own, own, pl.BlockSpec((TWO, 1, length), lambda i, pre: (i, 0, 0)), own]
        saved = sds((count, INNER, length), BF16)
        shapes += [saved, sds((count, INNER, length), F32), sds((count, 1, length), F32), saved]
    else:
        scratch += [pltpu.VMEM((INNER, length), BF16)] * TWO
        in_specs.append(pl.BlockSpec(memory_space=pl.ANY))
        args.append(mixed)
        aliases = {len(args) - 1: 0}
    return call(
        functools.partial(last_kernel, group, keep),
        (count // TWO,),
        in_specs,
        tuple(outs),
        tuple(shapes),
        scratch=scratch,
        aliases=aliases,
        cost=cost_of(count * INNER * (KERNEL * INNER + share) * length * 1.3, count * share * 6 * length * 2),
    )(*args)


def side(ref, sl):
    return jnp.concatenate([ref[j, sl, :].astype(F32) for j in range(ref.shape[0])], axis=1)


def across(ref, row):
    return jnp.concatenate([ref[j, row : row + 1, :] for j in range(ref.shape[0])], axis=1)


def row_sums(ref):
    ones = jnp.ones((8, LANES), F32)
    return lax.dot_general(
        ones, ref[...], (((1,), (1,)), ((), ())), precision=lax.Precision.HIGHEST, preferred_element_type=F32
    )


def norm_back(d_ref, gp_ref, hat_ref, scale, gain_ref, gg_ref, gb_ref, sum_ref, put):
    wide = d_ref.shape[1]
    zero = jnp.zeros((8, wide), F32)

    def body(sl, carry):
        d_pre = d_ref[sl, :] * side(gp_ref, sl)
        hat = side(hat_ref, sl)
        gg_ref[sl, :] += fold_lanes(d_pre * hat)
        gb_ref[sl, :] += fold_lanes(d_pre)
        e = d_pre * spread(gain_ref[0, sl, :], wide)
        d_ref[sl, :] = e
        return carry[0] + fold_rows(e), carry[1] + fold_rows(e * hat)

    total, dot = straight(INNER, wide, body, (zero, zero))
    total = total.sum(0, keepdims=True) * (scale / INNER)
    dot = dot.sum(0, keepdims=True) * (scale / INNER)

    def finish(sl, carry):
        v = (d_ref[sl, :] * scale - total - side(hat_ref, sl) * dot).astype(BF16)
        put(sl, v)
        sum_ref[sl, :] += fold_lanes(v.astype(F32))
        return carry

    straight(INNER, wide, finish, 0)


def rear_kernel(group, chs, pre, *refs):
    dy_refs = refs[:chs]
    w_ref, hat_ref, gp_ref, last_ref, scale_ref, p_ref = refs[chs : chs + 6]
    dconv_ref, lead_ref, trail_ref, gg_ref, gb_ref, gc_ref, gw_ref, go_ref = refs[chs + 6 : chs + 14]
    rows_ref, dy_ref, d_ref = refs[chs + 14 :]
    share, length = dy_refs[0].shape[1], dy_refs[0].shape[2]

    @pl.when(pl.program_id(0) == 0)
    def _():
        for ref in (gg_ref, gb_ref, gc_ref, gw_ref, go_ref):
            ref[...] = jnp.zeros_like(ref)

    for r in range(chs):
        at = pl.multiple_of(((pre[1] + chs - r) % chs) * share, share)
        for j in range(TWO):
            dy_ref[pl.ds(at, share), j * length : (j + 1) * length] = dy_refs[r][j]
    d_ref[...] = jnp.dot(w_ref[...], dy_ref[...], preferred_element_type=F32)
    last = jnp.concatenate([last_ref[j] for j in range(TWO)], axis=1)
    gw_ref[...] += lax.dot_general(last, dy_ref[...], (((1,), (1,)), ((), ())), preferred_element_type=F32)
    go_ref[...] += fold_lanes(dy_ref[...].astype(F32))

    def put(sl, v):
        for j in range(TWO):
            dconv_ref[j, sl, :] = v[:, j * length : (j + 1) * length]

    norm_back(d_ref, gp_ref, hat_ref, across(scale_ref, 0), p_ref, gg_ref, gb_ref, gc_ref, put)
    put_edges(group, dconv_ref, lead_ref, trail_ref)

    @pl.when(pl.program_id(0) == pl.num_programs(0) - 1)
    def _():
        for k, ref in enumerate((gc_ref, gg_ref, gb_ref)):
            rows_ref[:, k * INNER : (k + 1) * INNER] = row_sums(ref)
        rows_ref[:, 3 * INNER :] = row_sums(go_ref)


def const(shape):
    return pl.BlockSpec(shape, lambda i, pre: (0,) * len(shape), pipeline_mode=pl.Buffered(1))


def rear_call(pre, cot, others, w_out, hat, gp, last, scale, p2, group):
    seqs, share, length = cot.shape
    count = hat.shape[0]
    chs = 1 + len(others)
    edge = pl.BlockSpec((1, INNER, group * REACH), lambda i, pre: (i // (group // TWO), 0, 0))
    edge_shape = sds((count // group, INNER, group * REACH), BF16)
    own = pl.BlockSpec((TWO, INNER, length), lambda i, pre: (i, 0, 0))
    sums = [(INNER, LANES)] * 3 + [(INNER, D), (D, LANES), (8, 3 * INNER + D)]
    return call(
        functools.partial(rear_kernel, group, chs),
        (count // TWO,),
        [pl.BlockSpec((TWO, share, length), lambda i, pre: (pre[0] // TWO + i, 0, 0))]
        + [pl.BlockSpec((TWO, share, length), lambda i, pre: (i, 0, 0))] * (chs - 1)
        + [
            whole((INNER, D)),
            own,
            own,
            own,
            pl.BlockSpec((TWO, 1, length), lambda i, pre: (i, 0, 0)),
            whole((1, INNER, LANES), 4),
        ],
        tuple([own, edge, edge] + [const(v) for v in sums]),
        tuple([sds((count, INNER, length), BF16), edge_shape, edge_shape] + [sds(v, F32) for v in sums]),
        scratch=[pltpu.VMEM((D, TWO * length), BF16), pltpu.VMEM((INNER, TWO * length), F32)],
        cost=cost_of(count * INNER * D * length * 2.5, count * INNER * 5 * length * 2),
    )(pre, cot, *others, w_out, hat, gp, last, scale, p2)


def front_kernel(group, chs, pre, *refs):
    dconv_ref, before_ref, after_ref, mid_ref, hat_ref, gp_ref, scale_ref = refs[:7]
    x_ref, stat_ref, dy_ref, wc_ref, wi_ref, p2_ref, p1_ref = refs[7:14]
    refs = refs[14:]
    gt_ref = refs[0]
    send_refs = refs[1:chs]
    gcw_ref, gwi_ref, gg2_ref, gb2_ref, gbi_ref, gg1_ref, gb1_ref = refs[chs : chs + 7]
    pad_ref, cat_ref, d_ref, dn_ref, df_ref, first_ref = refs[chs + 7 :]
    share, length = dy_ref.shape[1], dy_ref.shape[2]
    wide = TWO * length

    @pl.when(pl.program_id(0) == 0)
    def _():
        for ref in (gcw_ref, gwi_ref, gg2_ref, gb2_ref, gbi_ref, gg1_ref, gb1_ref):
            ref[...] = jnp.zeros_like(ref)

    cats = [cat_ref.at[:, j * length : (j + 1) * length] for j in range(TWO)]
    gather_windows(group, dconv_ref, before_ref, after_ref, pad_ref, cats, -1)
    d_ref[...] = jnp.dot(wc_ref[...], cat_ref[...], preferred_element_type=F32)
    mid = jnp.concatenate([mid_ref[j] for j in range(TWO)], axis=1)
    gcw_ref[...] += lax.dot_general(cat_ref[...], mid, (((1,), (1,)), ((), ())), preferred_element_type=F32)

    def put(sl, v):
        dn_ref[sl, :] = v

    norm_back(d_ref, gp_ref, hat_ref, across(scale_ref, 0), p2_ref, gg2_ref, gb2_ref, gbi_ref, put)
    df_ref[...] = jnp.dot(wi_ref[...], dn_ref[...], preferred_element_type=F32)
    mean_in, scale_in = across(stat_ref, 0), across(stat_ref, 1)
    zero = jnp.zeros((8, wide), F32)

    def inner(sl, carry):
        hat = (side(x_ref, sl) - mean_in) * scale_in
        gain = spread(p1_ref[0, sl, :], wide)
        point = hat * gain + spread(p1_ref[1, sl, :], wide)
        phi = cdf(point)
        first_ref[sl, :] = (point * phi).astype(BF16)
        d_pre = df_ref[sl, :] * slope(point, phi)
        gg1_ref[sl, :] += fold_lanes(d_pre * hat)
        gb1_ref[sl, :] += fold_lanes(d_pre)
        e = d_pre * gain
        df_ref[sl, :] = e
        return carry[0] + fold_rows(e), carry[1] + fold_rows(e * hat)

    total, dot = straight(D, wide, inner, (zero, zero))
    total = total.sum(0, keepdims=True) * (scale_in / D)
    dot = dot.sum(0, keepdims=True) * (scale_in / D)
    gwi_ref[...] += lax.dot_general(
        dn_ref[...], first_ref[...], (((1,), (1,)), ((), ())), preferred_element_type=F32
    )
    for r in range(chs):
        base = ((pre[1] + r) % chs) * share

        def out(to, carry):
            rows = pl.ds(pl.multiple_of(base + to.start, 16), to.size)
            hat = (side(x_ref, rows) - mean_in) * scale_in
            v = df_ref[rows, :] * scale_in - total - hat * dot
            for j in range(TWO):
                half = v[:, j * length : (j + 1) * length]
                if r == 0:
                    gt_ref[j, to, :] = half + dy_ref[j, to, :].astype(F32)
                else:
                    send_refs[r - 1][j, to, :] = half.astype(BF16)
            return carry

        straight(share, wide, out, 0)


def front_call(pre, dconv, before, after, mid, hat, gp, scale, tokens, stat, cot, wc_t, wi_t, p2, p1, chs, group):
    seqs, share, length = cot.shape
    count = dconv.shape[0]
    edge = pl.BlockSpec((1, INNER, group * REACH), lambda i, pre: (i // (group // TWO), 0, 0))
    own = pl.BlockSpec((TWO, INNER, length), lambda i, pre: (i, 0, 0))

    def seq_block(rows):
        return pl.BlockSpec((TWO, rows, length), lambda i, pre: (pre[0] // TWO + i, 0, 0))

    inner_part, outer_part = (INNER, LANES), (D, LANES)
    sums = [(KERNEL * INNER, INNER), (INNER, D), inner_part, inner_part, inner_part, outer_part, outer_part]
    wide = TWO * length
    return call(
        functools.partial(front_kernel, group, chs),
        (count // TWO,),
        [
            own,
            edge,
            edge,
            own,
            own,
            own,
            pl.BlockSpec((TWO, 1, length), lambda i, pre: (i, 0, 0)),
            seq_block(D),
            pl.BlockSpec((TWO, 2, length), lambda i, pre: (i, 0, 0)),
            seq_block(share),
            whole((INNER, KERNEL * INNER)),
            whole((D, INNER)),
            whole((1, INNER, LANES), 1),
            whole((2, D, LANES)),
        ],
        tuple(
            [seq_block(share)]
            + [pl.BlockSpec((TWO, share, length), lambda i, pre: (i, 0, 0))] * (chs - 1)
            + [const(v) for v in sums]
        ),
        tuple(
            [sds((seqs, share, length), F32)]
            + [sds((count, share, length), BF16)] * (chs - 1)
            + [sds(v, F32) for v in sums]
        ),
        scratch=[
            pltpu.VMEM((TWO, INNER, length + 2 * LANES), BF16),
            pltpu.VMEM((KERNEL * INNER, wide), BF16),
            pltpu.VMEM((INNER, wide), F32),
            pltpu.VMEM((INNER, wide), BF16),
            pltpu.VMEM((D, wide), F32),
            pltpu.VMEM((D, wide), BF16),
        ],
        cost=cost_of(count * INNER * (2 * KERNEL * INNER + 2 * D) * length * 1.3, count * D * 8 * length * 2),
    )(pre, dconv, before, after, mid, hat, gp, scale, tokens, stat, cot, wc_t, wi_t, p2, p1)


def add_kernel(pre, part_ref, dy_ref, _, gt_ref):
    gt_ref[...] = part_ref[...].astype(F32) + dy_ref[...].astype(F32)


def add_call(pre, part, cot, gt, start):
    seqs, share, length = cot.shape
    count = part.shape[0]
    at = lambda i, pre: (pre[start] + i, 0, 0)
    return call(
        add_kernel,
        (count,),
        [
            pl.BlockSpec((1, share, length), lambda i, pre: (i, 0, 0)),
            pl.BlockSpec((1, share, length), at),
            pl.BlockSpec(memory_space=pl.ANY),
        ],
        pl.BlockSpec((1, share, length), at),
        sds((seqs, share, length), F32),
        aliases={3: 0},
        cost=cost_of(count * share * length, count * share * length * 8),
    )(pre, part, cot, gt)


def turned(square):
    unit = (
        lax.broadcasted_iota(jnp.int32, (INNER, INNER), 0) == lax.broadcasted_iota(jnp.int32, (INNER, INNER), 1)
    ).astype(F32).astype(BF16)
    return lax.dot_general(unit, square, (((1,), (1,)), ((), ())), preferred_element_type=F32).astype(BF16)


def turn_kernel(pre, w_ref, flat_ref, turned_ref):
    flat_ref[...] = w_ref[0]
    turned_ref[...] = turned(w_ref[0])


def turn_rims_kernel(lead, trail, w_ref, wo_ref, flat_ref, turned_ref, before, after, wo_t_ref, *rest):
    rim_steps(lead, trail, before, after, *rest)
    turn_kernel(None, w_ref, flat_ref, turned_ref)

    @pl.when(pl.program_id(0) == 0)
    def _():
        wo_t_ref[...] = turned(wo_ref[...])


def turn_call(pre, conv, edges=None, w_out=None):
    shape = sds((INNER, KERNEL * INNER), BF16)
    if edges is not None:
        any_spec = pl.BlockSpec(memory_space=pl.ANY)
        column = pl.BlockSpec((INNER, INNER), lambda k: (0, k))
        return pl.pallas_call(
            turn_rims_kernel,
            grid=(KERNEL,),
            in_specs=[
                any_spec,
                any_spec,
                pl.BlockSpec((1, INNER, INNER), lambda k: (k, 0, 0)),
                pl.BlockSpec((INNER, INNER), lambda k: (0, lax.axis_index("ch"))),
            ],
            out_specs=(column, column, any_spec, any_spec, pl.BlockSpec((INNER, INNER), lambda k: (0, 0))),
            out_shape=(shape, shape, *[sds(e.shape, BF16) for e in edges], sds((INNER, INNER), BF16)),
            scratch_shapes=rim_scratch(edges[0].shape),
            cost_estimate=cost_of(KERNEL * INNER**3, KERNEL * INNER * INNER * 6),
            compiler_params=pltpu.CompilerParams(
                vmem_limit_bytes=VMEM_BYTES, collective_id=3, has_side_effects=True
            ),
        )(*edges, conv, w_out)
    block = pl.BlockSpec((INNER, INNER), lambda k, pre: (0, k))
    return call(
        turn_kernel,
        (KERNEL,),
        [pl.BlockSpec((1, INNER, INNER), lambda k, pre: (k, 0, 0))],
        (block, block),
        (shape, shape),
        cost=cost_of(KERNEL * INNER**3, KERNEL * INNER * INNER * 6),
    )(pre, conv)


ORDERS = ((0, 1, 2, 3), (0, 1, 2, 3), (0, 2, 3, 1), (0, 1, 2, 3), (0, 1, 2, 3))
GIVE = 5
SCHEDULE = {
    1: [(5, 0), (0, 0)],
    2: [(2, 0), (0, 1), (1, 0)],
    3: [(5, 1), (2, 1)],
    5: [(1, 1), (3, 0)],
    7: [(0, 2), (2, 2), (5, 2)],
    8: [(3, 1)],
    9: [(1, 2), (5, 3)],
    10: [(0, 3)],
    12: [(5, 4), (2, 3), (3, 2), (1, 3), (0, 4), (4, 0), (0, 5), (4, 1), (2, 4), (5, 5), (3, 3), (1, 4)],
    13: [(4, 2)],
    14: [(1, 5), (0, 6), (3, 4), (2, 5), (4, 3), (1, 6), (0, 7), (3, 5), (5, 6)],
    15: [(2, 6), (1, 7), (3, 6)],
    16: [(4, 4), (4, 5), (2, 7), (0, 8), (3, 7), (5, 7), (1, 8), (0, 9), (4, 6), (5, 8), (4, 7), (2, 8), (3, 8), (4, 8), (5, 9), (1, 9), (4, 9), (2, 9), (3, 9)],
}


class Stream:
    def __init__(self, order, first, rows, arrays, slot):
        self.order, self.rows = order, rows
        self.acc, self.send, self.recv, self.swap, self.res, self.sems = arrays
        self.slot = slot
        self.levels = len(order)
        self.size = [rows >> (t + 1) for t in range(self.levels)]
        self.at = [rows - (rows >> t) for t in range(self.levels)]
        self.seq, self.ch = lax.axis_index("seq"), lax.axis_index("ch")
        self.low = [first]
        for t in range(self.levels):
            self.low.append(self.low[-1] + self.bit(order[t]) * self.size[t])

    def bit(self, b):
        return (self.seq // (1 << b)) % 2

    def partner(self, b):
        return {"seq": self.seq + (1 - 2 * self.bit(b)) * (1 << b)}

    def remote(self, src, dst, k, device):
        return pltpu.make_async_remote_copy(
            src_ref=src,
            dst_ref=dst,
            send_sem=self.sems[0].at[self.slot, k],
            recv_sem=self.sems[1].at[self.slot, k],
            device_id=device,
            device_id_type=pl.DeviceIdType.MESH,
        )

    def copy(self, k):
        if k < self.levels:
            window = pl.ds(self.at[k], self.size[k])
            held = self.send.at[:, pl.ds(0, self.size[k]), :]
            return self.remote(held, self.recv.at[:, window, :], k, self.partner(self.order[k]))
        if k == self.levels:
            return self.remote(self.swap.at[0], self.swap.at[1], k, {"ch": 1 - self.ch})
        t = 2 * self.levels - k
        place = spot(self.low[t + 1], 0, self.size[t])
        return self.remote(self.res.at[place, :], self.res.at[place, :], k, self.partner(self.order[t]))

    def start(self, k):
        if k < self.levels:
            away = self.low[k] + (1 - self.bit(self.order[k])) * self.size[k]
            for h in range(2):

                def pack(i, step, h=h):
                    self.send[h, spot(0, i, step), :] = self.acc[h, spot(away, i, step), :].astype(BF16)

                sliced(self.size[k], pack)
        elif k == self.levels:
            place = spot(self.low[-1], 0, self.size[-1])
            self.swap[0] = self.acc[1 - self.ch, place, :].astype(BF16)
        self.copy(k).start()

    def finish(self, k):
        self.copy(k).wait()
        if k < self.levels:
            for h in range(2):

                def add(i, step, h=h):
                    place = spot(self.low[k + 1], i, step)
                    self.acc[h, place, :] += self.recv[h, spot(self.at[k], i, step), :].astype(F32)

                sliced(self.size[k], add)
        elif k == self.levels:
            place = spot(self.low[-1], 0, self.size[-1])
            self.res[place, :] = (self.acc[self.ch, place, :] + self.swap[1].astype(F32)).astype(BF16)


def sliced(count, body):
    step = next(r for r in (96, 64, 48, 32, 16) if count % r == 0)

    def one(i, carry):
        body(pl.multiple_of(i * step, 16), step)
        return carry

    lax.fori_loop(0, count // step, one, 0)


def spot(base, i, step):
    return pl.ds(pl.multiple_of(base + i, 16), step)


HALF = INNER // 2
LEVELS = 4
EARLY_ROWS = HALF * (KERNEL + D // INNER)
ROWS = 768
SMALL_ROWS = 256


def stream_scratch():
    dma = pltpu.SemaphoreType.DMA
    out = [pltpu.VMEM((2, 4 * ROWS, INNER), F32)]
    moved = ROWS - (ROWS >> LEVELS)
    out += [pltpu.VMEM((2, ROWS // 2, INNER), BF16)] * 4
    out += [pltpu.VMEM((2, moved, INNER), BF16)] * 4
    out += [pltpu.VMEM((2, ROWS >> LEVELS, INNER), BF16)] * 4
    out += [pltpu.VMEM((4 * ROWS, INNER), BF16)]
    out += [
        pltpu.VMEM((2, SMALL_ROWS, LANES), F32),
        pltpu.VMEM((2, SMALL_ROWS // 2, LANES), BF16),
        pltpu.VMEM((2, SMALL_ROWS - (SMALL_ROWS >> LEVELS), LANES), BF16),
        pltpu.VMEM((2, SMALL_ROWS >> LEVELS, LANES), BF16),
        pltpu.VMEM((SMALL_ROWS, LANES), BF16),
    ]
    out += [dma((2 * (KERNEL + 2 * D // INNER),)), dma((5, 2 * LEVELS + 1)), dma((5, 2 * LEVELS + 1))]
    return out


def streams_of(refs):
    acc, send, recv, swap, res = refs[0], refs[1:5], refs[5:9], refs[9:13], refs[13]
    sems = refs[20:22]
    out = []
    for q, order in enumerate(ORDERS[:4]):
        out.append(Stream(order, q * ROWS, ROWS, (acc, send[q], recv[q], swap[q], res, sems), q))
    out.append(Stream(ORDERS[4], 0, SMALL_ROWS, (*refs[14:19], sems), 4))
    return out


def inner_kernel(group, pre, *refs):
    dconv_ref, before_ref, after_ref, mid_ref, hat_ref, gp_ref, scale_ref, first_ref, wc_ref, p2_ref = refs[:10]
    dn_ref, gcw_ref, gwi_ref, rows_ref = refs[10:14]
    pad_ref, cat_ref, d_ref, gg_ref, gb_ref, gbi_ref = refs[14:]
    length = mid_ref.shape[2]

    @pl.when(pl.program_id(0) == 0)
    def _():
        for ref in (gg_ref, gb_ref, gbi_ref):
            ref[...] = jnp.zeros_like(ref)

    cats = [cat_ref.at[:, j * length : (j + 1) * length] for j in range(TWO)]
    gather_windows(group, dconv_ref, before_ref, after_ref, pad_ref, cats, -1)
    d_ref[...] = jnp.dot(wc_ref[...], cat_ref[...], preferred_element_type=F32)
    mid = jnp.concatenate([mid_ref[j] for j in range(TWO)], axis=1)
    fresh = pl.program_id(0) == 0
    gcw = lax.dot_general(cat_ref[...], mid, (((1,), (1,)), ((), ())), preferred_element_type=F32)
    gcw_ref[...] = jnp.where(fresh, 0.0, gcw_ref[...]) + gcw

    def put(sl, v):
        for j in range(TWO):
            dn_ref[j, sl, :] = v[:, j * length : (j + 1) * length]

    norm_back(d_ref, gp_ref, hat_ref, across(scale_ref, 0), p2_ref, gg_ref, gb_ref, gbi_ref, put)
    dn = jnp.concatenate([dn_ref[j] for j in range(TWO)], axis=1)
    first = jnp.concatenate([first_ref[j] for j in range(TWO)], axis=1)
    gwi = lax.dot_general(dn, first, (((1,), (1,)), ((), ())), preferred_element_type=F32)
    gwi_ref[...] = jnp.where(fresh, 0.0, gwi_ref[...]) + gwi

    @pl.when(pl.program_id(0) == pl.num_programs(0) - 1)
    def _():
        for k, ref in enumerate((gbi_ref, gg_ref, gb_ref)):
            rows_ref[:, k * INNER : (k + 1) * INNER] = row_sums(ref)


def inner_call(pre, dconv, before, after, mid, hat, gp, scale, first, wc_t, p2, group):
    count, _, length = dconv.shape
    edge = pl.BlockSpec((1, INNER, group * REACH), lambda i, pre: (i // (group // TWO), 0, 0))
    own = pl.BlockSpec((TWO, INNER, length), lambda i, pre: (i, 0, 0))
    sums = [(KERNEL * INNER, INNER), (INNER, D), (8, 3 * INNER)]
    return call(
        functools.partial(inner_kernel, group),
        (count // TWO,),
        [
            own,
            edge,
            edge,
            own,
            own,
            own,
            pl.BlockSpec((TWO, 1, length), lambda i, pre: (i, 0, 0)),
            pl.BlockSpec((TWO, D, length), lambda i, pre: (i, 0, 0)),
            whole(wc_t.shape),
            whole((1, INNER, LANES), 1),
        ],
        tuple([own] + [const(v) for v in sums]),
        tuple([sds(dconv.shape, BF16)] + [sds(v, F32) for v in sums]),
        scratch=[
            pltpu.VMEM((TWO, INNER, length + 2 * LANES), BF16),
            pltpu.VMEM((KERNEL * INNER, TWO * length), BF16),
            pltpu.VMEM((INNER, TWO * length), F32),
        ]
        + [pltpu.VMEM((INNER, LANES), F32)] * 3,
        cost=cost_of(count * (2 * KERNEL * INNER + D) * INNER * length, KERNEL * INNER * INNER * 4),
    )(pre, dconv, before, after, mid, hat, gp, scale, first, wc_t, p2)


KINDS = [0, 0, 0, 0, 0, 0, 1, 0, 0, 1, 1, 1, 1, 1, 1, 1]


def turn_of(kind, step):
    steps = [k for k, v in enumerate(KINDS) if v == kind]
    return sum((jnp.asarray(step >= k).astype(jnp.int32) for k in steps[1:]), jnp.int32(0))


def is_turn(kind, step):
    return functools.reduce(jnp.logical_or, (step == k for k, v in enumerate(KINDS) if v == kind))


def tail_kernel(group, *refs):
    dn_ref, x_ref, stat_ref, mid_ref, lead_oth, trail_oth, wc_ref, wi_ref, p1_ref, p2_ref = refs[:10]
    rows_ref, rows_in_ref, gcw_ref, gwo_ref, gwi_ref = refs[10:15]
    w_in_ref, wi_ref = wi_ref, refs[-1]
    refs = refs[:-1]
    mine_ref, last_ref, total_ref, small_ref, got_ref = refs[15:20]
    stream_refs = refs[20:42]
    pad_ref, cat_ref, d_ref, give_ref, df_ref = refs[42:47]
    gg1_ref, gb1_ref, give_send, give_recv = refs[47:51]
    before_oth, after_oth, rim_send, rim_recv = refs[51:]
    rims = Rims(lead_oth, trail_oth, before_oth, after_oth, rim_send, rim_recv)
    acc, small_acc, res, small_res, load_sem = (stream_refs[k] for k in (0, 14, 13, 18, 19))
    base = 3 * ROWS
    share, length = give_ref.shape[1], give_ref.shape[2]
    seq, ch = lax.axis_index("seq"), lax.axis_index("ch")
    step, steps = pl.program_id(0), pl.num_programs(0)
    count = give_ref.shape[0]
    streams = streams_of(stream_refs)
    outer_now, conv_now = turn_of(0, step), turn_of(1, step)

    def loads():
        out = []
        for h in range(2):
            mine = pl.ds(h * HALF, HALF)
            pieces = [gcw_ref.at[k, mine, :] for k in range(KERNEL)]
            pieces += [gwo_ref.at[mine, pl.ds(j * INNER, INNER)] for j in range(D // INNER)]
            for j, piece in enumerate(pieces):
                out.append((piece, acc.at[h, pl.ds(j * HALF, HALF), :]))
            for j in range(D // INNER):
                piece = gwi_ref.at[mine, pl.ds(j * INNER, INNER)]
                out.append((piece, acc.at[h, pl.ds(base + j * HALF, HALF), :]))
        return [pltpu.make_async_copy(a, b, load_sem.at[j]) for j, (a, b) in enumerate(out)]

    def give(i):
        return pltpu.make_async_remote_copy(
            src_ref=give_ref.at[i],
            dst_ref=got_ref.at[i],
            send_sem=give_send.at[i],
            recv_sem=give_recv.at[i],
            device_id={"ch": 1 - ch},
            device_id_type=pl.DeviceIdType.MESH,
        )

    def fill_inner():
        inner = [ref[0:1, k * INNER : (k + 1) * INNER] for ref in (rows_in_ref, rows_ref) for k in range(3)]
        at = base + HALF * D // INNER
        for h in range(2):
            for k, v in enumerate(inner):
                acc[h, at + k : at + k + 1, :HALF] = v[:, h * HALF : (h + 1) * HALF]

    def fill_outer():
        small_acc[...] = jnp.zeros_like(small_acc)
        outer = [row_sums(ref)[0:1] for ref in (gg1_ref, gb1_ref)] + [rows_ref[0:1, 3 * INNER :]]
        for h in range(2):
            for k, v in enumerate(outer):
                for j in range(INNER // LANES):
                    lanes = slice(h * INNER + j * LANES, h * INNER + (j + 1) * LANES)
                    row = k * (INNER // LANES) + j
                    small_acc[h, row : row + 1, :] = v[:, lanes]

    def act(actions):
        for q, k in actions:
            if q == GIVE:
                if k > 1:
                    give(k - 2).wait()
                if k < count:
                    give(k).start()
                continue
            if k > 0:
                streams[q].finish(k - 1)
            elif q == 3:
                fill_inner()
            elif q == 4:
                fill_outer()
            if k <= 2 * LEVELS:
                streams[q].start(k)

    @pl.when(step == 0)
    def _():
        for h in range(2):
            acc[h, EARLY_ROWS:base, :] = jnp.zeros((base - EARLY_ROWS, INNER), F32)
            used = base + HALF * D // INNER
            acc[h, used:, :] = jnp.zeros((4 * ROWS - used, INNER), F32)
        for copy in loads():
            copy.start()
        before_oth[...] = jnp.zeros_like(before_oth)
        after_oth[...] = jnp.zeros_like(after_oth)
        barrier = pltpu.get_barrier_semaphore()
        for device in [streams[0].partner(b) for b in range(LEVELS)] + [{"ch": 1 - ch}]:
            pl.semaphore_signal(barrier, inc=1, device_id=device, device_id_type=pl.DeviceIdType.MESH)
        pl.semaphore_wait(barrier, LEVELS + 1 + rims.greet())
        rims.start()
        for ref in (gg1_ref, gb1_ref):
            ref[...] = jnp.zeros_like(ref)
        for j in range(D // INNER):
            block = slice(j * INNER, (j + 1) * INNER)
            wi_ref[block, :] = turned(w_in_ref[:, block])

    @pl.when(step == min(SCHEDULE))
    def _():
        for copy in loads():
            copy.wait()

    for at, actions in SCHEDULE.items():
        if at < len(KINDS):

            @pl.when(step == at)
            def _():
                act(actions)

    @pl.when(is_turn(0, step))
    def _():
        now = outer_now
        df_ref[...] = jnp.dot(wi_ref[...], dn_ref[0], preferred_element_type=F32)
        mean_in, scale_in = stat_ref[0, 0:1, :], stat_ref[0, 1:2, :]
        zero = jnp.zeros((8, length), F32)

        def inner(sl, carry):
            hat = (x_ref[0, sl, :].astype(F32) - mean_in) * scale_in
            gain = spread(p1_ref[0, sl, :], length)
            point = hat * gain + spread(p1_ref[1, sl, :], length)
            d_pre = df_ref[sl, :] * slope(point, cdf(point))
            gg1_ref[sl, :] += fold_lanes(d_pre * hat)
            gb1_ref[sl, :] += fold_lanes(d_pre)
            e = d_pre * gain
            df_ref[sl, :] = e
            return carry[0] + fold_rows(e), carry[1] + fold_rows(e * hat)

        total, dot = straight(D, length, inner, (zero, zero))
        total = total.sum(0, keepdims=True) * (scale_in / D)
        dot = dot.sum(0, keepdims=True) * (scale_in / D)
        for r in range(2):
            start = ((ch + r) % 2) * share

            def out(to, carry):
                rows = pl.ds(pl.multiple_of(start + to.start, 16), to.size)
                hat = (x_ref[0, rows, :].astype(F32) - mean_in) * scale_in
                v = (df_ref[rows, :] * scale_in - total - hat * dot).astype(BF16)
                if r == 0:
                    mine_ref[0, to, :] = v
                else:
                    give_ref[now, to, :] = v
                return carry

            straight(share, length, out, 0)

    pl.when(step == KINDS.index(1))(rims.wait)

    @pl.when(is_turn(1, step))
    def _():
        held = pl.ds(conv_now // group, 1)
        gather_windows(group, mid_ref, before_oth.at[held], after_oth.at[held], pad_ref, [cat_ref], 1, conv_now)
        conv = jnp.dot(wc_ref[...], cat_ref[...], preferred_element_type=F32)
        d_ref[...] = conv + spread(p2_ref[3], length)
        mean, scale = norm_stats(lambda sl: d_ref[sl, :], INNER, length)

        def body(sl, carry):
            hat = (d_ref[sl, :] - mean) * scale
            point = hat * spread(p2_ref[4, sl, :], length) + spread(p2_ref[5, sl, :], length)
            last_ref[0, sl, :] = (point * cdf(point)).astype(BF16)
            return carry

        straight(INNER, length, body, 0)

    @pl.when(step == steps - 1)
    def _():
        act(SCHEDULE[max(SCHEDULE)])
        done = [
            pltpu.make_async_copy(res, total_ref, load_sem.at[0]),
            pltpu.make_async_copy(small_res, small_ref, load_sem.at[1]),
        ]
        for copy in done:
            copy.start()
        for copy in done:
            copy.wait()


def tail_call(dn, tokens, stat, mid, rims_oth, wc, w_in, p1, p2, rows, rows_in, gcw, gwo, gwi, group):
    count, _, length = dn.shape
    share = D // 2
    any_spec = pl.BlockSpec(memory_space=pl.ANY)

    def fixed(shape):
        return pl.BlockSpec(shape, lambda i: (0,) * len(shape), pipeline_mode=pl.Buffered(1))

    def block(k, width):
        return pl.BlockSpec((1, width, length), lambda i: (turn_of(k, i), 0, 0))

    dma = pltpu.SemaphoreType.DMA
    return pl.pallas_call(
        functools.partial(tail_kernel, group),
        grid=(len(KINDS),),
        in_specs=[
            block(0, INNER),
            pl.BlockSpec((1, D, length), lambda i: (lax.axis_index("ch") * count + turn_of(0, i), 0, 0)),
            block(0, 2),
            block(1, INNER),
            any_spec,
            any_spec,
            fixed(wc.shape),
            fixed(w_in.shape),
            fixed(p1.shape),
            fixed(p2.shape),
            fixed(rows.shape),
            fixed(rows_in.shape),
            any_spec,
            any_spec,
            any_spec,
        ],
        out_specs=(block(0, share), block(1, INNER), any_spec, any_spec, any_spec),
        out_shape=(
            sds((count, share, length), BF16),
            sds((count, INNER, length), BF16),
            sds((4 * ROWS, INNER), BF16),
            sds((SMALL_ROWS, LANES), BF16),
            sds((count, share, length), BF16),
        ),
        scratch_shapes=stream_scratch()
        + [
            pltpu.VMEM((1, INNER, length + 2 * LANES), BF16),
            pltpu.VMEM((KERNEL * INNER, length), BF16),
            pltpu.VMEM((INNER, length), F32),
            pltpu.VMEM((count, share, length), BF16),
            pltpu.VMEM((D, length), F32),
            pltpu.VMEM((D, LANES), F32),
            pltpu.VMEM((D, LANES), F32),
            dma((count,)),
            dma((count,)),
            pltpu.VMEM(rims_oth[0].shape, BF16),
            pltpu.VMEM(rims_oth[0].shape, BF16),
            dma((2,)),
            dma((2,)),
            pltpu.VMEM((D, INNER), BF16),
        ],
        cost_estimate=cost_of(count * INNER * (KERNEL * INNER + D) * length * 4, 4 * ROWS * INNER * 12),
        compiler_params=pltpu.CompilerParams(
            vmem_limit_bytes=TAIL_BYTES, collective_id=2, has_side_effects=True
        ),
    )(dn, tokens, stat, mid, *rims_oth, wc, w_in, p1, p2, rows, rows_in, gcw, gwo, gwi)


TAIL_BYTES = 63 * 1024 * 1024


def finish_kernel(pre, mine_ref, got_ref, dy_ref, last_ref, x_ref, wo_ref, b_ref, total_ref, small_ref, _, *outs):
    gt_ref, mixed_ref, gcw_ref, gwi_ref, gwo_ref = outs[:5]
    inner_refs, outer_refs = outs[5:11], outs[11:]
    length = dy_ref.shape[2]
    step, count = pl.program_id(0), pl.num_programs(0) // 2
    part = gcw_ref.shape[1]

    @pl.when(step < count)
    def _():
        gt_ref[...] = mine_ref[...].astype(F32) + dy_ref[...].astype(F32)

    @pl.when(step >= count)
    def _():
        gt_ref[...] = got_ref[...].astype(F32) + dy_ref[...].astype(F32)

    branch = jnp.dot(wo_ref[...], last_ref[0], preferred_element_type=F32)
    mixed_ref[0] = (x_ref[0].astype(F32) + branch + spread(b_ref[...], length)).astype(BF16)
    for k in range(KERNEL):

        @pl.when(step == k)
        def _():
            gcw_ref[0] = total_ref[k * part : (k + 1) * part, :].astype(F32)

    for k, (ref, start) in enumerate(((gwo_ref, KERNEL * part), (gwi_ref, 3 * ROWS))):

        @pl.when(step == KERNEL + k)
        def _():
            for j in range(D // INNER):
                ref[:, j * INNER : (j + 1) * INNER] = total_ref[start + j * part : start + (j + 1) * part, :].astype(F32)

    @pl.when(step == 0)
    def _():
        at = 3 * ROWS + part * D // INNER
        rows = total_ref[at : at + 16, :].astype(F32)
        for k, ref in enumerate(inner_refs):
            ref[...] = rows[k, :part]
        rows = small_ref[:16, :].astype(F32)
        each = outer_refs[0].shape[0] // LANES
        for k, ref in enumerate(outer_refs):
            for j in range(each):
                ref[j * LANES : (j + 1) * LANES] = rows[k * each + j]


def finish_call(pre, mine, got, cot, last, tokens, wo_t, b_out, total, small, mixed, part):
    seqs, share, length = cot.shape
    count = got.shape[0] // TWO
    early = lambda i: jnp.minimum(i, count - 1)
    late = lambda i: jnp.maximum(i - count, 0)
    return call(
        finish_kernel,
        (2 * count,),
        [
            pl.BlockSpec((TWO, share, length), lambda i, pre: (early(i), 0, 0)),
            pl.BlockSpec((TWO, share, length), lambda i, pre: (late(i), 0, 0)),
            pl.BlockSpec((TWO, share, length), lambda i, pre: ((pre[0] // TWO + i) % (seqs // TWO), 0, 0)),
            pl.BlockSpec((1, INNER, length), lambda i, pre: (i, 0, 0)),
            pl.BlockSpec((1, share, length), lambda i, pre: (pre[2] + i, pre[1], 0)),
            whole(wo_t.shape),
            whole(b_out.shape),
            whole(total.shape),
            whole(small.shape),
            pl.BlockSpec(memory_space=pl.ANY),
        ],
        (
            pl.BlockSpec((TWO, share, length), lambda i, pre: ((pre[0] // TWO + i) % (seqs // TWO), 0, 0)),
            pl.BlockSpec((1, share, length), lambda i, pre: (pre[2] + i, 0, 0)),
            pl.BlockSpec((1, part, INNER), lambda i, pre: (jnp.minimum(i, KERNEL - 1), 0, 0)),
            const((part, D)),
            const((part, D)),
            *[const((part,))] * 6,
            *[const((share,))] * 3,
        ),
        (
            sds((seqs, share, length), F32),
            sds(mixed.shape, BF16),
            sds((KERNEL, part, INNER), F32),
            sds((part, D), F32),
            sds((part, D), F32),
            *[sds((part,), F32)] * 6,
            *[sds((share,), F32)] * 3,
        ),
        aliases={10: 1},
    )(pre, mine, got, cot, last, tokens, wo_t, b_out, total, small, mixed)


def rotate(value, axis, count, by):
    return lax.ppermute(value, axis, [(i, (i + by) % count) for i in range(count)])


def shift(value, by):
    count = lax.axis_size("seq")
    pairs = [(i, i + by) for i in range(count) if 0 <= i + by < count]
    return lax.ppermute(value, "seq", pairs)


def rims(lead, trail):
    return shift(trail, 1), shift(lead, -1)


def own_slice(value, width, dim):
    return lax.dynamic_slice_in_dim(value, lax.axis_index("ch") * width, width, dim)


def lane_copies(vectors):
    return jnp.broadcast_to(vectors[..., None], vectors.shape + (LANES,))


def body(
    tokens,
    pad_mask,
    cotangent,
    ln1_gain,
    first_norm_bias,
    w_in,
    b_in,
    ln2_gain,
    ln2_bias,
    conv_w,
    conv_b,
    ln3_gain,
    ln3_bias,
    w_out,
    b_out,
):
    chs = lax.axis_size("ch")
    ch = lax.axis_index("ch")
    seqs, _, length = tokens.shape
    share = b_out.shape[0]
    part = b_in.shape[0]
    n = seqs // chs
    group = min(4, n)
    starts = [((ch + chs - r) % chs) * n for r in range(1, chs)]
    pre = jnp.stack([ch * n, ch] + starts).astype(jnp.int32)
    pair = chs == 2 and lax.axis_size("seq") == 1 << LEVELS

    p1 = lane_copies(jnp.stack([ln1_gain, first_norm_bias]))
    bo = lane_copies(b_out)
    vectors = [b_in, ln2_gain, ln2_bias, conv_b, ln3_gain, ln3_bias]
    if pair:
        vec = jnp.pad(jnp.concatenate(vectors), (0, 2048 - 6 * part)).reshape(16, LANES)
        first, stat, w_in_full, conv_full, w_out_full, vec_full, away = first_call(
            pre, tokens, p1, (w_in, conv_w, w_out), vec, cotangent
        )
        others = [rotate(away, "ch", chs, 1)]
        vec_full = vec_full.reshape(2, 2048)[:, : 6 * part].reshape(2, 6, part)
        inner = vec_full.transpose(1, 0, 2).reshape(6, INNER)
    else:
        first, stat = first_call(pre, tokens, p1, None, None)
        w_in_full = lax.all_gather(w_in, "ch", axis=0, tiled=True)
        conv_full = lax.all_gather(conv_w, "ch", axis=1, tiled=True)
        w_out_full = lax.all_gather(w_out, "ch", axis=0, tiled=True)
        inner = lax.all_gather(jnp.stack(vectors), "ch", axis=1, tiled=True)
        others = []
        for r in range(1, chs):
            block = lax.dynamic_slice_in_dim(cotangent, ((ch + r) % chs) * n, n, 0)
            others.append(rotate(block, "ch", chs, r))

    p2 = lane_copies(inner)
    mid_own, lead, trail, hat_mid, gp_mid, scale_mid = middle_call(
        pre, first, pad_mask, w_in_full, p2, n, 0, group, True
    )
    if pair:
        wc, wc_t, before, after, wo_t = turn_call(pre, conv_full, (lead, trail), w_out_full)
    else:
        wo_t = lax.dynamic_slice_in_dim(w_out_full, ch * share, share, 1).T
        wc, wc_t = turn_call(pre, conv_full)
        before, after = rims(lead, trail)
        mid_oth, lead, trail = middle_call(pre, first, pad_mask, w_in_full, p2, seqs - n, n, group, False)
        rims_oth = rims(lead, trail)
    mixed, hat_out, gp_out, scale_out, last_own = last_call(
        pre, mid_own, before, after, tokens, wc, wo_t, p2, bo, n, 0, group, True, None
    )
    dconv, lead, trail, gg3, gb3, gcb, gwo, gbo, rows = rear_call(
        pre, cotangent, others, w_out_full, hat_out, gp_out, last_own, scale_out, p2, group
    )
    if pair:
        mid_oth, lead_oth, trail_oth, lead, trail = middle_rims_call(
            (lead, trail), first, pad_mask, w_in_full, p2, n, group
        )
        rims_oth = (lead_oth, trail_oth)
    else:
        lead, trail = rims(lead, trail)
    if pair:
        dn, gcw, gwi, rows_in = inner_call(
            pre, dconv, lead, trail, mid_own, hat_mid, gp_mid, scale_mid, first, wc_t, p2, group
        )
        mine, last_oth, total, small, got = tail_call(
            dn, tokens, stat, mid_oth, rims_oth, wc, w_in_full, p1, p2, rows, rows_in,
            gcw.reshape(KERNEL, INNER, INNER), gwo, gwi, group,
        )
        gt, mixed, gcw, gwi, gwo, *sums = finish_call(
            pre, mine, got, cotangent, last_oth, tokens, wo_t, bo, total, small, mixed, part
        )
        inner_sums, outer_sums = sums[:6], sums[6:]
    else:
        gt, *rest = front_call(
            pre, dconv, lead, trail, mid_own, hat_mid, gp_mid, scale_mid, tokens, stat, cotangent,
            wc_t, w_in_full.T, p2, p1, chs, group,
        )
        sends = [rotate(v, "ch", chs, r + 1) for r, v in enumerate(rest[: chs - 1])]
        gcw, gwi, gg2, gb2, gbi, gg1, gb1 = rest[chs - 1 :]
        gcw = gcw.reshape(KERNEL, INNER, INNER)
        inner_sums = jnp.stack([v.sum(1) for v in (gbi, gg2, gb2, gcb, gg3, gb3)])
        outer_sums = jnp.stack([v.sum(1) for v in (gg1, gb1, gbo)])
        mixed, = last_call(
            pre, mid_oth, *rims_oth, tokens, wc, wo_t, p2, bo, seqs - n, n, group, False, mixed
        )
        gcw, gwi, gwo, inner_sums, outer_sums = lax.psum((gcw, gwi, gwo, inner_sums, outer_sums), ("seq", "ch"))
        gcw = own_slice(gcw, part, 1)
        gwi = own_slice(gwi, part, 0)
        gwo = own_slice(gwo, part, 0)
        inner_sums = own_slice(inner_sums, part, 1)
        outer_sums = own_slice(outer_sums, share, 1)
        for r in range(chs - 1):
            gt = add_call(pre, sends[r], cotangent, gt, 2 + r)
    return (
        mixed,
        gt,
        outer_sums[0],
        outer_sums[1],
        gwi,
        inner_sums[0],
        inner_sums[1],
        inner_sums[2],
        gcw,
        inner_sums[3],
        inner_sums[4],
        inner_sums[5],
        gwo,
        outer_sums[2],
    )


def solution(mesh):
    in_specs = (
        P(None, None, "seq"),
        P(None, "seq"),
        P(None, "ch", "seq"),
        P(),
        P(),
        P("ch", None),
        P("ch"),
        P("ch"),
        P("ch"),
        P(None, "ch", None),
        P("ch"),
        P("ch"),
        P("ch"),
        P("ch", None),
        P("ch"),
    )
    out_specs = (
        P(None, "ch", "seq"),
        P(None, "ch", "seq"),
        P("ch"),
        P("ch"),
        P("ch", None),
        P("ch"),
        P("ch"),
        P("ch"),
        P(None, "ch", None),
        P("ch"),
        P("ch"),
        P("ch"),
        P("ch", None),
        P("ch"),
    )
    return jax.shard_map(body, mesh=mesh, in_specs=in_specs, out_specs=out_specs, check_vma=False)
```
